128 devices in a mesh: wide: 16 (over y, z), grp: 8 (over x, core).
Axes of the slice: x: 4, y: 4, z: 4, core: 2. Of those that a mesh axis runs over, the one named last changes fastest.
Arguments:
- eta_hat: bfloat16 [2, 2048, 2048], P(None, ('wide', 'grp')), may hold values from -0.0008544922 to 0.0008544922
- phi_hat: bfloat16 [2, 2048, 2048], P(None, ('wide', 'grp')), may hold values from -0.00061035156 to 0.00061035156
- patch_tiles: int32 [256], replicated, may hold values from 0 to 1023, as said below
- fraction: bfloat16 [2, 128, 64, 128, 128], P(None, ('wide', 'grp')), may hold values from 0 to 1
Outputs:
- surface: float32 [2048, 2048], P(('wide', 'grp'))
- fraction_next: bfloat16 [2, 128, 64, 128, 128], P(None, ('wide', 'grp'))
- tendency: float32 [2, 2048, 2048], P(None, ('wide', 'grp'))
The draws below stay inside these ranges and needn't reach their ends.
Inputs may be any that keep to these rules, and one draw needn't show every extreme that they name: `patch_tiles`: for each g below 8, entries g * 32 to (g + 1) * 32 - 1 are distinct tiles, in ascending order, whose column t % 32 lies in [g * 4, (g + 1) * 4). Of these, the tiles of one band (rows (t // 32) // 2 equal) are at most 8, and in every group one band holds exactly 8.
All inputs are finite; a program needn't handle non-finite values.
Results may differ from the reference program's by a relative error of at most 0.019.
Values may be sent and summed in bfloat16 or wider, within the bound.
A program may use at most 192 MiB of HBM per device.

```python
import math
import jax
import jax.numpy as jnp
from jax import lax

NM = 2048
RADIX = 32
TS = 64
LV = 64
SIDE = 128
N_WIDE = 16
N_GRP = 8
DEVICES = 128


def draw_patch_tiles(key, part):
    tiles_side = NM // TS
    band_tiles = NM // N_WIDE // TS
    col_tiles = NM // N_GRP // TS
    per_owner = band_tiles * col_tiles
    owner_cap = min(per_owner, N_WIDE)
    per_group = 2 * N_WIDE
    candidates = N_WIDE * per_owner

    def one_group(group_index, group_sort_key):
        key_reward, key_complete, key_noise = jax.random.split(group_sort_key, 3)
        owner_reward = jax.random.randint(key_reward, (N_WIDE,), 0, 4)
        complete_owner = jax.random.randint(key_complete, (), 0, N_WIDE)
        owner_reward = jnp.where(jnp.arange(N_WIDE) == complete_owner, 8, owner_reward)
        random_noise = jax.random.randint(key_noise, (candidates,), 0, 1024)
        member_index = jnp.arange(candidates, dtype=jnp.int32)
        holder_index = member_index // per_owner
        pinned_choice = (group_index == 0) & (member_index == 0) | (group_index == N_GRP - 1) & (member_index == candidates - 1)
        rating_values = owner_reward[holder_index] * 2097152 + random_noise * 1024 + member_index + jnp.where(pinned_choice, 18 * 2097152, 0)
        same_owner = holder_index[:, None] == holder_index[None, :]
        higher = same_owner & (rating_values[None, :] > rating_values[:, None])
        position = jnp.sum(higher.astype(jnp.int32), axis=1)
        rating_values = jnp.where(position < owner_cap, rating_values, -1 - member_index)
        chosen = lax.top_k(rating_values, per_group)[1]
        owner_sel = chosen // per_owner
        within = chosen % per_owner
        tile_row = owner_sel * band_tiles + within // col_tiles
        tile_col = group_index * col_tiles + within % col_tiles
        return jnp.sort(tile_row * tiles_side + tile_col)
    group_keys = jax.random.split(key, N_GRP)
    lists = jax.vmap(one_group)(jnp.arange(N_GRP, dtype=jnp.int32), group_keys)
    return lists.reshape(N_GRP * per_group).astype(jnp.int32)


def shard_levels(rng, dims, cuts, least, top_value):
    loudness = 1.0
    for axis_at, blocks in cuts:
        draws = jax.random.uniform(jax.random.fold_in(jax.random.fold_in(rng, 6), axis_at), (blocks,), jnp.float32, least / len(cuts), top_value / len(cuts))
        loudness = loudness * jnp.repeat(jnp.exp(draws), dims[axis_at] // blocks).reshape((-1,) + (1,) * (len(dims) - 1 - axis_at))
    return loudness


def scatter_about(rng, shape, width, limit, cuts=(), kind=jnp.bfloat16):
    drawn = width * jax.random.normal(rng, shape, jnp.float32)
    if cuts:
        drawn = drawn * shard_levels(rng, shape, cuts, -0.22, 0.18)
    return jnp.clip(drawn, -limit, limit).astype(kind)


def setup_inputs(seed: int = 0) -> dict:
    splits = jax.random.split(jax.random.key(seed), 5)
    eta_hat = scatter_about(splits[0], (2, NM, NM), (11 * NM * NM) ** -0.5, 0.0008544922, ((1, 128),))
    phi_hat = scatter_about(splits[1], (2, NM, NM), (25 * NM * NM) ** -0.5, 0.00061035156, ((1, 128),))
    patch_tiles = draw_patch_tiles(jax.random.fold_in(splits[4], 71), 0)
    fraction = jnp.clip(1.0 * jax.random.uniform(splits[3], (2, DEVICES, LV, SIDE, SIDE), jnp.float32) ** shard_levels(splits[3], (2, DEVICES, LV, SIDE, SIDE), ((1, 128),), -0.2, 0.2), 0.0, 1.0).astype(jnp.bfloat16)
    return {"eta_hat": eta_hat, "phi_hat": phi_hat, "patch_tiles": patch_tiles, "fraction": fraction}


Z_BOTTOM = -2.0
Z_TOP = 2.0
DECAY_RATE = 0.5
COURANT = 0.3


def refine(field):
    return jnp.repeat(jnp.repeat(field, 2, axis=0), 2, axis=1)


def upwind_flux(values, speeds, axis):
    widths = tuple((1, 1) if dim_index == axis else (0, 0) for dim_index in range(3))
    padded = jnp.pad(values, widths, mode="edge")
    speed_pad = jnp.pad(speeds, widths, mode="edge")
    count_faces = padded.shape[axis] - 1
    left_vals = lax.slice_in_dim(padded, 0, count_faces, axis=axis)
    right_vals = lax.slice_in_dim(padded, 1, count_faces + 1, axis=axis)
    face_speed = 0.5 * (lax.slice_in_dim(speed_pad, 0, count_faces, axis=axis) + lax.slice_in_dim(speed_pad, 1, count_faces + 1, axis=axis))
    face_flux = jnp.maximum(face_speed, 0.0) * left_vals + jnp.minimum(face_speed, 0.0) * right_vals
    return lax.slice_in_dim(face_flux, 1, count_faces, axis=axis) - lax.slice_in_dim(face_flux, 0, count_faces - 1, axis=axis)


def patch_step(state, height, along_x, along_y):
    levels = state.shape[0]
    side = state.shape[1]
    spacing = (Z_TOP - Z_BOTTOM) / levels
    level_z = (Z_BOTTOM + (jnp.arange(levels, dtype=jnp.float32) + 0.5) * spacing)[:, None, None]
    fine_h = refine(height)[None]
    from_sea = jnp.clip((fine_h - level_z) / spacing + 0.5, 0.0, 1.0)
    position = jnp.arange(side, dtype=jnp.float32)
    edge_dist = jnp.minimum(position, side - 1.0 - position)
    distance = jnp.minimum(edge_dist[:, None], edge_dist[None, :])
    weight = 0.3 + 0.7 * jnp.exp(-8.0 * distance / side)
    blended = weight * from_sea + (1.0 - weight) * state.astype(jnp.float32)
    profile = jnp.exp(DECAY_RATE * (level_z - Z_TOP))
    speed_x = refine(along_x)[None] * profile
    speed_y = refine(along_y)[None] * profile
    moved = blended - COURANT * (upwind_flux(blended, speed_x, 2) + upwind_flux(blended, speed_y, 1))
    updated = jnp.clip(moved, 0.0, 1.0)
    column = Z_BOTTOM + spacing * jnp.sum(updated, axis=0)
    coarse = column.reshape(side // 2, 2, side // 2, 2).mean(axis=(1, 3))
    return updated.astype(jnp.bfloat16), coarse


def wave_numbers(length):
    signed = (jnp.arange(length, dtype=jnp.int32) + length // 2) % length - length // 2
    return signed.astype(jnp.float32) * (2.0 * math.pi / length)


def small_tables(length):
    index_row = jnp.arange(length, dtype=jnp.int32)
    phase = (index_row[:, None] * index_row[None, :]) % length
    angle = phase.astype(jnp.float32) * (2.0 * math.pi / length)
    return jnp.cos(angle).astype(jnp.bfloat16), jnp.sin(angle).astype(jnp.bfloat16)


def contract(data, table, pattern):
    return jnp.einsum(pattern, data.astype(jnp.float32), table.astype(jnp.float32))


def factored_transform(real_in, imag_in, direction_sign, real_only):
    length = real_in.shape[-1]
    leading = real_in.shape[:-1]
    inner_size = length // RADIX
    cos_p, sin_p = small_tables(RADIX)
    cos_q, sin_q = small_tables(inner_size)
    split_re = real_in.reshape(leading + (RADIX, inner_size))
    segment_re = contract(split_re, cos_p, "...pq,pk->...kq")
    segment_im = direction_sign * contract(split_re, sin_p, "...pq,pk->...kq")
    if imag_in is not None:
        split_im = imag_in.reshape(leading + (RADIX, inner_size))
        segment_re = segment_re - direction_sign * contract(split_im, sin_p, "...pq,pk->...kq")
        segment_im = segment_im + contract(split_im, cos_p, "...pq,pk->...kq")
    first_idx = jnp.arange(RADIX, dtype=jnp.int32)[:, None]
    second_idx = jnp.arange(inner_size, dtype=jnp.int32)[None, :]
    angle = ((first_idx * second_idx) % length).astype(jnp.float32) * (2.0 * math.pi / length)
    twist_cos = jnp.cos(angle)
    twist_sin = jnp.sin(angle)
    turned_re = (segment_re * twist_cos - direction_sign * segment_im * twist_sin).astype(jnp.bfloat16)
    turned_im = (segment_im * twist_cos + direction_sign * segment_re * twist_sin).astype(jnp.bfloat16)
    out_re = contract(turned_re, cos_q, "...kq,qm->...km") - direction_sign * contract(turned_im, sin_q, "...kq,qm->...km")
    out_re = jnp.swapaxes(out_re, -1, -2).reshape(leading + (length,))
    if real_only:
        return out_re
    out_im = contract(turned_im, cos_q, "...kq,qm->...km") + direction_sign * contract(turned_re, sin_q, "...kq,qm->...km")
    out_im = jnp.swapaxes(out_im, -1, -2).reshape(leading + (length,))
    return out_re, out_im


def reference(eta_hat, phi_hat, patch_tiles, fraction):
    wavenum = wave_numbers(NM)
    phi_re = phi_hat[0].astype(jnp.float32)
    phi_im = phi_hat[1].astype(jnp.float32)
    coef_re = jnp.stack([eta_hat[0], (-wavenum[:, None] * phi_im).astype(jnp.bfloat16), (-wavenum[None, :] * phi_im).astype(jnp.bfloat16)])
    coef_im = jnp.stack([eta_hat[1], (wavenum[:, None] * phi_re).astype(jnp.bfloat16), (wavenum[None, :] * phi_re).astype(jnp.bfloat16)])
    half_re, half_im = factored_transform(coef_re, coef_im, 1.0, False)
    half_re = jnp.swapaxes(half_re.astype(jnp.bfloat16), 1, 2)
    half_im = jnp.swapaxes(half_im.astype(jnp.bfloat16), 1, 2)
    physical = factored_transform(half_re, half_im, 1.0, True)
    elevation = physical[0]
    velocity_x = physical[1]
    velocity_y = physical[2]
    devices = N_WIDE * N_GRP
    per_group = 2 * N_WIDE
    tiles_side = NM // TS

    def one_patch(flat_index):
        slot_index = flat_index // devices
        column_index = flat_index % devices
        wide_pos = column_index // N_GRP
        grp_pos = column_index % N_GRP
        tile_id = patch_tiles[grp_pos * per_group + slot_index * N_WIDE + wide_pos]
        row_start = ((tile_id // tiles_side) * TS).astype(jnp.int32)
        col_start = ((tile_id % tiles_side) * TS).astype(jnp.int32)
        height = lax.dynamic_slice(elevation, (row_start, col_start), (TS, TS))
        along_x = lax.dynamic_slice(velocity_x, (row_start, col_start), (TS, TS))
        along_y = lax.dynamic_slice(velocity_y, (row_start, col_start), (TS, TS))
        new_state, coarse = patch_step(fraction[slot_index, column_index], height, along_x, along_y)
        return new_state, coarse, tile_id

    states, coarse_all, tile_ids = lax.map(one_patch, jnp.arange(2 * devices, dtype=jnp.int32))
    fraction_next = states.reshape(fraction.shape)
    tile_stack = elevation.reshape(tiles_side, TS, tiles_side, TS).transpose(0, 2, 1, 3).reshape(tiles_side * tiles_side, TS, TS)
    tile_stack = tile_stack.at[tile_ids].set(coarse_all)
    surface = tile_stack.reshape(tiles_side, tiles_side, TS, TS).transpose(0, 2, 1, 3).reshape(NM, NM)
    drive = (-(surface + 0.5 * (velocity_x * velocity_x + velocity_y * velocity_y))).astype(jnp.bfloat16)
    row_re, row_im = factored_transform(drive, None, -1.0, False)
    row_re = row_re.astype(jnp.bfloat16).T
    row_im = row_im.astype(jnp.bfloat16).T
    spec_re, spec_im = factored_transform(row_re, row_im, -1.0, False)
    tendency = jnp.stack([spec_re, spec_im]) * (1.0 / NM)
    return surface, fraction_next, tendency
```

```python
import functools
import math

import jax
import jax.numpy as jnp
import numpy as np
from jax import lax
from jax.experimental import pallas as pl
from jax.experimental.pallas import tpu as pltpu
from jax.sharding import PartitionSpec as P

F32 = jnp.float32
BF16 = jnp.bfloat16
MESH = pl.DeviceIdType.MESH

N = 2048
D = 128
NW = 16
NG = 8
L = 128
R = 16
LV = 64
SIDE = 128
TS = 64
Z_BOTTOM = -2.0
Z_TOP = 2.0
DECAY_RATE = 0.5
COURANT = 0.3
VMEM_LIMIT = 56 << 20


def unit(phase, length):
    angle = (phase % length) * (2.0 * math.pi / length)
    return np.cos(angle), np.sin(angle)


def lane_tables(sign):
    k1 = np.arange(R)[:, None]
    n2 = np.arange(L)[None, :]
    tc, ts = unit(k1 * n2, N)
    k2 = np.arange(D)[:, None]
    c, s = unit(k2 * n2, D)
    spread = np.concatenate([c, sign * s], axis=1)
    return (
        jnp.asarray(tc, F32),
        jnp.asarray(sign * ts, F32),
        jnp.asarray(spread, F32).astype(BF16),
    )


def block_tables(sign, blocks, full):
    k1 = np.arange(D)[:, None]
    src = np.arange(D)[None, :]
    c, s = unit(k1 * src, D)
    gather = np.concatenate([c, sign * s], axis=0)
    j = np.tile(np.arange(R), 8)[None, :]
    tc, ts = unit(k1 * j, N)
    k2 = np.arange(R)[:, None]
    jj = np.arange(R)[None, :]
    cc, ss = unit(k2 * jj, R)
    ss = sign * ss
    rows = []
    for part in range(2 if full else 1):
        for e in range(blocks):
            out = np.zeros((R, 2, 4, R))
            out[:, 0, e, :] = cc if part == 0 else ss
            out[:, 1, e, :] = -ss if part == 0 else cc
            rows.append(out.reshape(R, L))
    finish = np.concatenate(rows, axis=0)
    return (
        jnp.asarray(gather, F32).astype(BF16),
        jnp.asarray(tc, F32),
        jnp.asarray(sign * ts, F32),
        jnp.asarray(finish, F32).astype(BF16),
    )


def fourth(x, sign):
    (ar, ai), (br, bi), (cr, ci), (dr, di) = x
    t0r, t0i, t1r, t1i = ar + cr, ai + ci, ar - cr, ai - ci
    t2r, t2i, t3r, t3i = br + dr, bi + di, br - dr, bi - di
    if sign < 0:
        t3r, t3i = -t3r, -t3i
    return (
        (t0r + t2r, t0i + t2i),
        (t1r - t3i, t1i + t3r),
        (t0r - t2r, t0i - t2i),
        (t1r + t3i, t1i - t3r),
    )


def times(x, re, im):
    if abs(im) < 1e-12 and abs(re - 1.0) < 1e-12:
        return x
    a, b = x
    return (a * re - b * im, a * im + b * re)


def sixteenth(x, sign):
    inner = []
    for b in range(4):
        y = fourth([x[4 * a + b] for a in range(4)], sign)
        turned = []
        for c in range(4):
            angle = sign * 2.0 * math.pi * b * c / 16
            turned.append(times(y[c], math.cos(angle), math.sin(angle)))
        inner.append(turned)
    out = [None] * 16
    for c in range(4):
        z = fourth([inner[b][c] for b in range(4)], sign)
        for d in range(4):
            out[c + 4 * d] = z[d]
    return out


def nt_dot(a, b):
    return lax.dot_general(a, b, (((1,), (1,)), ((), ())), preferred_element_type=F32)


def blocks_in(x, gather, tc, ts, flip):
    both = jnp.dot(gather, x, preferred_element_type=F32)
    parts = []
    for h in range(2):
        a = both[:D, h * L:(h + 1) * L]
        b = both[D:, h * L:(h + 1) * L]
        u = a * tc - b * ts
        v = b * tc + a * ts
        parts.append((u + flip * pltpu.roll(v, 64, 1)).astype(BF16))
    return jnp.concatenate(parts, axis=0)


def coords(flat):
    return (flat // NG, flat % NG)


def lane_iota(rows):
    return lax.broadcasted_iota(jnp.int32, (rows, L), 1)


def greet_all(me):
    barrier = pltpu.get_barrier_semaphore()

    def greet(k, carry):
        pl.semaphore_signal(
            barrier, inc=1, device_id=coords(lax.rem(me + k, D)), device_id_type=MESH
        )
        return carry

    lax.fori_loop(1, D, greet, 0)
    return barrier


def rise_kernel(
    tiles, eta, phi, tw_c, tw_s, spread, gather, bt_c, bt_s, finish,
    phys, foot,
    tb, wide32, send, recv, send1, recv1, send2, recv2,
    ssem, rsem, ssem1, rsem1, ssem2, rsem2,
):
    w = lax.axis_index("wide")
    g = lax.axis_index("grp")
    me = w * NG + g
    barrier = greet_all(me)

    row = lax.broadcasted_iota(jnp.int32, (R, L), 0)
    lane = lane_iota(R)
    kx = me * R + row
    kx = jnp.where(kx >= N // 2, kx - N, kx).astype(F32) * (2.0 * math.pi / N)

    for f in range(3):
        x = []
        for n1 in range(16):
            cols = slice(n1 * L, (n1 + 1) * L)
            if f == 0:
                x.append((eta[0, :, cols].astype(F32), eta[1, :, cols].astype(F32)))
            else:
                if f == 1:
                    k = kx
                else:
                    base = n1 * L if n1 < 8 else n1 * L - N
                    k = (lane + base).astype(F32) * (2.0 * math.pi / N)
                x.append((-k * phi[1, :, cols].astype(F32), k * phi[0, :, cols].astype(F32)))
        y = sixteenth(x, 1)
        for k1 in range(16):
            c, s = tw_c[k1:k1 + 1, :], tw_s[k1:k1 + 1, :]
            a, b = y[k1]
            re = (a * c - b * s).astype(BF16)
            im = (a * s + b * c).astype(BF16)
            up = slice(f * R, (f + 1) * R)
            dn = slice(64 + f * R, 64 + (f + 1) * R)
            tb[k1, up, 0:L] = re
            tb[k1, up, L:2 * L] = -im
            tb[k1, dn, 0:L] = im
            tb[k1, dn, L:2 * L] = re

    zero = jnp.zeros((R, 2 * L), BF16)

    def rows_out(kk, carry):
        for h in range(2):
            tb[2 * kk + h, 48:64, :] = zero
            tb[2 * kk + h, 112:128, :] = zero
        rhs = tb[pl.ds(2 * kk, 2)].reshape(2 * L, 2 * L)
        z = nt_dot(spread[...], rhs)
        wide32[pl.ds(2 * kk, D, stride=R), :] = z[:, :L]
        wide32[pl.ds(2 * kk + 1, D, stride=R), :] = z[:, L:]
        return carry

    lax.fori_loop(0, 8, rows_out, 0)

    def narrow(i, carry):
        part = wide32[pl.ds(pl.multiple_of(i * 128, 128), 128), :]
        send[pl.ds(i * 8, 8)] = part.reshape(8, R, L).astype(BF16)
        return carry

    lax.fori_loop(0, 16, narrow, 0)

    pl.semaphore_wait(barrier, D - 1)
    pltpu.make_async_copy(send.at[me], recv.at[me], rsem).start()

    def post(k, carry):
        d = lax.rem(me + k, D)
        pltpu.make_async_remote_copy(
            send.at[d], recv.at[me], ssem, rsem, device_id=coords(d), device_id_type=MESH
        ).start()
        return carry

    lax.fori_loop(1, D, post, 0)
    pltpu.make_async_copy(recv, recv, rsem).wait()

    def widen(i, carry):
        part = recv[pl.ds(i * 8, 8)].astype(F32)
        wide32[pl.ds(pl.multiple_of(i * 128, 128), 128), :] = part.reshape(128, L)
        return carry

    lax.fori_loop(0, 16, widen, 0)

    flip = jnp.where(lane_iota(D) < 64, -1.0, 1.0).astype(F32)

    def columns(yy, carry):
        x = jnp.concatenate(
            [
                wide32[pl.ds(2 * yy, D, stride=R), :].astype(BF16),
                wide32[pl.ds(2 * yy + 1, D, stride=R), :].astype(BF16),
            ],
            axis=1,
        )
        t = blocks_in(x, gather[...], bt_c[...], bt_s[...], flip)
        out = nt_dot(finish[...], t)
        phys[pl.ds(2 * yy, 48, stride=R), :] = out[:, :L]
        phys[pl.ds(2 * yy + 1, 48, stride=R), :] = out[:, L:]
        return carry

    lax.fori_loop(0, 8, columns, 0)

    low = lane < 64

    def by_group(q, carry):
        for h in range(2):
            at = [pl.multiple_of((f * 16 + 2 * q + h) * R, R) for f in range(3)]
            ht = phys[pl.ds(at[0], R), :]
            vx = phys[pl.ds(at[1], R), :]
            vy = phys[pl.ds(at[2], R), :]
            send1[q, h] = ht.astype(BF16)
            send1[q, 2 + 2 * h] = jnp.where(low, vx, pltpu.roll(vy, 64, 1)).astype(BF16)
            send1[q, 3 + 2 * h] = jnp.where(low, pltpu.roll(vx, 64, 1), vy).astype(BF16)
        return carry

    lax.fori_loop(0, NG, by_group, 0)

    pltpu.make_async_copy(send1.at[g], recv1.at[g], rsem1).start()
    for k in range(1, NG):
        d = lax.rem(g + k, NG)
        pltpu.make_async_remote_copy(
            send1.at[d], recv1.at[g], ssem1, rsem1, device_id=(w, d), device_id_type=MESH
        ).start()
    pltpu.make_async_copy(recv1, recv1, rsem1).wait()

    def choose(d, carry):
        t0 = tiles[g * 32 + d]
        t1 = tiles[g * 32 + 16 + d]
        t = jnp.where(lax.shift_right_logical(t0, 6) == w, t0, t1)
        upper = jnp.bitwise_and(lax.shift_right_logical(t, 5), 1) * 4
        col = jnp.bitwise_and(t, 3)
        odd = jnp.bitwise_and(t, 1)
        pair = lax.shift_right_logical(col, 1)
        right = (lane * 0 + odd) == 1
        for q in range(4):
            send2[d, q] = recv1[upper + q, 2 + col]
        for q in range(2):
            a = recv1[upper + 2 * q, pair].astype(F32)
            b = recv1[upper + 2 * q + 1, pair].astype(F32)
            lo = jnp.where(right, pltpu.roll(a, 64, 1), a)
            hi = jnp.where(right, b, pltpu.roll(b, 64, 1))
            send2[d, 4 + q] = jnp.where(low, lo, hi).astype(BF16)
        return carry

    lax.fori_loop(0, NW, choose, 0)

    pltpu.make_async_copy(send2.at[w], recv2.at[w], rsem2).start()
    for k in range(1, NW):
        d = lax.rem(w + k, NW)
        pltpu.make_async_remote_copy(
            send2.at[d], recv2.at[w], ssem2, rsem2, device_id=(d, g), device_id_type=MESH
        ).start()
    pltpu.make_async_copy(recv2, recv2, rsem2).wait()

    for s in range(2):
        t = tiles[g * 32 + s * 16 + w]
        band = jnp.bitwise_and(lax.shift_right_logical(t, 6), NW - 1)
        for q in range(6):
            foot[s, q] = recv2[band, q]

    pltpu.make_async_copy(send.at[pl.ds(0, D - 1)], send.at[pl.ds(0, D - 1)], ssem).wait()
    pltpu.make_async_copy(send1.at[pl.ds(0, NG - 1)], send1.at[pl.ds(0, NG - 1)], ssem1).wait()
    pltpu.make_async_copy(send2.at[pl.ds(0, NW - 1)], send2.at[pl.ds(0, NW - 1)], ssem2).wait()


def patch_tables():
    pos = np.arange(SIDE)
    edge = np.minimum(pos, SIDE - 1 - pos)
    dist = np.minimum(edge[:, None], edge[None, :])
    weight = 0.3 + 0.7 * np.exp(-8.0 * dist / SIDE)
    x = np.arange(SIDE)
    pick = np.zeros((2, L, SIDE))
    for h in range(2):
        pick[h, 64 * h + x // 2, x] = 1.0
    rows = np.zeros((SIDE, TS))
    rows[x, x // 2] = 1.0
    halves = np.zeros((2, SIDE, 32))
    for i in range(SIDE):
        r = i // 2
        blk, within = r // 16, r % 16
        halves[blk % 2, i, (blk // 2) * 16 + within] = 1.0
    z = Z_BOTTOM + (np.arange(LV) + 0.5) * ((Z_TOP - Z_BOTTOM) / LV)
    prof = np.exp(DECAY_RATE * (z - Z_TOP))
    return (
        jnp.asarray(prof, F32),
        jnp.asarray(weight, F32),
        jnp.asarray(pick, F32).astype(BF16),
        jnp.asarray(rows, F32).astype(BF16),
        jnp.asarray(halves, F32).astype(BF16),
        jnp.asarray(np.swapaxes(pick, 1, 2), F32),
        jnp.asarray(rows.T, F32),
    )


RB = 16
PAD = 8


def patch_kernel(
    prof, foot, state, weight, pick, rows, halves, down_l, down_r,
    state_out, coarse,
    hh, cf, bl, total, gathered,
):
    s = pl.program_id(0)

    vel = foot[0, 0:4].reshape(64, L)
    hgt = foot[0, 4:6].reshape(32, L)

    def up(m, sel, spread_rows):
        wide = jnp.dot(m, sel, preferred_element_type=F32).astype(BF16)
        return jnp.dot(spread_rows, wide, preferred_element_type=F32)

    height = up(hgt, pick[0], halves[0]) + up(hgt, pick[1], halves[1])
    ax = up(vel, pick[0], rows[...])
    ay = up(vel, pick[1], rows[...])
    scale = LV / (Z_TOP - Z_BOTTOM)
    hh[...] = height * scale - Z_BOTTOM * scale

    lane = lax.broadcasted_iota(jnp.int32, (SIDE, SIDE), 1)
    sub = lax.broadcasted_iota(jnp.int32, (SIDE, SIDE), 0)

    def faces(a, axis, index):
        after = jnp.where(index == SIDE - 1, a, pltpu.roll(a, SIDE - 1, axis))
        before = jnp.where(index == 0, a, pltpu.roll(a, 1, axis))
        return (0.5 * COURANT) * (a + after), (0.5 * COURANT) * (before + a)

    center = jnp.zeros((SIDE, SIDE), F32)
    for n, (a, axis, index) in enumerate(((ax, 1, lane), (ay, 0, sub))):
        upper, lower = faces(a, axis, index)
        center += jnp.maximum(upper, 0.0) - jnp.minimum(lower, 0.0)
        from_up = jnp.minimum(upper, 0.0)
        from_low = -jnp.maximum(lower, 0.0)
        last, first = index == SIDE - 1, index == 0
        center += jnp.where(last, from_up, 0.0) + jnp.where(first, from_low, 0.0)
        cf[1 + 2 * n] = jnp.where(last, 0.0, from_up)
        cf[2 + 2 * n] = jnp.where(first, 0.0, from_low)
    cf[0] = center

    edge = jnp.zeros((PAD, SIDE), F32)
    for b in range(SIDE // RB):
        rs = slice(b * RB, (b + 1) * RB)
        h = hh[rs, :]
        wt = weight[rs, :]
        keep = 1.0 - wt

        def blend(k, carry, b=b, rs=rs, h=h, wt=wt, keep=keep):
            sea = jnp.clip(h - k.astype(F32), 0.0, 1.0)
            bl[k, PAD + b * RB:PAD + (b + 1) * RB, :] = (
                wt * sea + keep * state[0, k, rs, :].astype(F32)
            )
            if b == 0:
                bl[k, 0:PAD, :] = edge
            if b == SIDE // RB - 1:
                bl[k, PAD + SIDE:, :] = edge
            return carry

        lax.fori_loop(0, LV, blend, 0, unroll=4)

    for b in range(SIDE // RB):
        rs = slice(b * RB, (b + 1) * RB)
        at = PAD + b * RB
        c0, c1, c2, c3, c4 = (cf[n, rs, :] for n in range(5))

        def move(k, acc, at=at, rs=rs, c0=c0, c1=c1, c2=c2, c3=c3, c4=c4):
            mid = bl[k, at:at + RB, :]
            nxt = bl[k, at + 1:at + 1 + RB, :]
            prv = bl[k, at - 1:at - 1 + RB, :]
            out = c0 * mid + c1 * pltpu.roll(mid, SIDE - 1, 1) + c2 * pltpu.roll(mid, 1, 1)
            out = out + c3 * nxt + c4 * prv
            new = jnp.clip(mid - prof[k] * out, 0.0, 1.0)
            state_out[0, k, rs, :] = new.astype(BF16)
            return acc + new

        total[rs, :] = lax.fori_loop(0, LV, move, jnp.zeros((RB, SIDE), F32), unroll=4)

    column = total[...] * (1.0 / scale) + Z_BOTTOM
    high = lax.Precision.HIGHEST
    packed = jnp.dot(column, down_l[0], preferred_element_type=F32, precision=high)
    packed = 0.25 * jnp.dot(down_r[...], packed, preferred_element_type=F32, precision=high)

    @pl.when(s == 0)
    def _():
        gathered[...] = packed

    @pl.when(s == 1)
    def _():
        coarse[...] = (gathered[...] + packed).astype(BF16).reshape(4, R, L)


def patches(foot, fraction):
    prof, weight, pick, rows, halves, down_l, down_r = patch_tables()
    full = lambda shape: pl.BlockSpec(shape, lambda s: (0,) * len(shape))
    return pl.pallas_call(
        patch_kernel,
        grid=(2,),
        out_shape=(
            jax.ShapeDtypeStruct((2, LV, SIDE, SIDE), BF16),
            jax.ShapeDtypeStruct((4, R, L), BF16),
        ),
        in_specs=[
            pl.BlockSpec(memory_space=pltpu.SMEM),
            pl.BlockSpec((1, 6, R, L), lambda s: (s, 0, 0, 0)),
            pl.BlockSpec((1, LV, SIDE, SIDE), lambda s: (s, 0, 0, 0)),
            full((SIDE, SIDE)),
            full((2, L, SIDE)),
            full((SIDE, TS)),
            full((2, SIDE, 32)),
            pl.BlockSpec((1, SIDE, L), lambda s: (s, 0, 0)),
            full((TS, SIDE)),
        ],
        out_specs=(
            pl.BlockSpec((1, LV, SIDE, SIDE), lambda s: (s, 0, 0, 0)),
            full((4, R, L)),
        ),
        scratch_shapes=[
            pltpu.VMEM((SIDE, SIDE), F32),
            pltpu.VMEM((5, SIDE, SIDE), F32),
            pltpu.VMEM((LV, SIDE + 2 * PAD, SIDE), F32),
            pltpu.VMEM((SIDE, SIDE), F32),
            pltpu.VMEM((TS, L), F32),
        ],
        compiler_params=pltpu.CompilerParams(
            dimension_semantics=("arbitrary",), vmem_limit_bytes=VMEM_LIMIT
        ),
        name="patches",
    )(prof, foot, fraction, weight, pick, rows, halves, down_l, down_r)


def fall_kernel(
    tiles, phys, coarse, tw_c, tw_s, spread, gather, bt_c, bt_s, finish,
    surface, tendency,
    source, tb, got, send, recv, out32,
    ssem, rsem, ssem2, rsem2,
):
    w = lax.axis_index("wide")
    g = lax.axis_index("grp")
    me = w * NG + g
    barrier = greet_all(me)

    row_of = 2 * w + g // 4
    for q in range(NG):
        want = row_of * 32 + 4 * q
        at = jnp.int32(0)
        for step in (16, 8, 4, 2, 1):
            at = at + jnp.where(tiles[q * 32 + at + step - 1] < want, step, 0)
        for c in range(4):
            found = tiles[q * 32 + at]
            cc = 4 * q + c
            source[0, cc] = jnp.bitwise_and(at, NW - 1) * NG + q
            source[1, cc] = lax.shift_right_logical(at, 4)
            source[2, cc] = jnp.where(found == want + c, 1, 0)
            at = jnp.minimum(at + jnp.where(found <= want + c, 1, 0), 31)

    pl.semaphore_wait(barrier, D - 1)
    pltpu.make_async_copy(coarse.at[g % 4], got.at[me], rsem).start()

    def post(k, carry):
        d = lax.rem(me + k, D)
        pltpu.make_async_remote_copy(
            coarse.at[d % 4], got.at[me], ssem, rsem, device_id=coords(d), device_id_type=MESH
        ).start()
        return carry

    lax.fori_loop(1, D, post, 0)
    pltpu.make_async_copy(got, got, rsem).wait()

    lane = lane_iota(R)
    low = lane < 64
    x = []
    for k2 in range(16):
        halves = []
        for h in range(2):
            cc = 2 * k2 + h
            tile = got[source[0, cc]].astype(F32)
            same = (lane * 0 + source[1, cc]) == h
            halves.append(jnp.where(same, tile, pltpu.roll(tile, 64, 1)))
        there = jnp.where(low, source[2, 2 * k2], source[2, 2 * k2 + 1]) == 1
        ht = phys[k2 * R:(k2 + 1) * R, :]
        vx = phys[256 + k2 * R:256 + (k2 + 1) * R, :]
        vy = phys[512 + k2 * R:512 + (k2 + 1) * R, :]
        sea = jnp.where(there, jnp.where(low, halves[0], halves[1]), ht)
        surface[:, k2 * L:(k2 + 1) * L] = sea
        x.append((-(sea + 0.5 * (vx * vx + vy * vy)), jnp.zeros((R, L), F32)))
    y = sixteenth(x, -1)
    for k1 in range(16):
        c, s = tw_c[k1:k1 + 1, :], tw_s[k1:k1 + 1, :]
        a, b = y[k1]
        re = (a * c - b * s).astype(BF16)
        im = (a * s + b * c).astype(BF16)
        q, e = k1 // 4, k1 % 4
        up = slice(e * R, (e + 1) * R)
        dn = slice(64 + e * R, 64 + (e + 1) * R)
        tb[q, up, 0:L] = re
        tb[q, up, L:2 * L] = -im
        tb[q, dn, 0:L] = im
        tb[q, dn, L:2 * L] = re

    for q in range(2):
        rhs = tb[2 * q:2 * q + 2].reshape(2 * L, 2 * L)
        z = nt_dot(spread[...], rhs)
        send[:, 2 * q, :] = z[:, :L]
        send[:, 2 * q + 1, :] = z[:, L:]

    pltpu.make_async_copy(send.at[me], recv.at[me], rsem2).start()

    def post2(k, carry):
        d = lax.rem(me + k, D)
        pltpu.make_async_remote_copy(
            send.at[d], recv.at[me], ssem2, rsem2, device_id=coords(d), device_id_type=MESH
        ).start()
        return carry

    lax.fori_loop(1, D, post2, 0)
    pltpu.make_async_copy(recv, recv, rsem2).wait()

    flip = jnp.where(lane_iota(D) < 64, -1.0, 1.0).astype(F32)
    for q in range(2):
        xx = jnp.concatenate(
            [recv[:, 2 * q, :].astype(BF16), recv[:, 2 * q + 1, :].astype(BF16)], axis=1
        )
        t = blocks_in(xx, gather[...], bt_c[...], bt_s[...], flip)
        out = nt_dot(finish[...], t) * (1.0 / N)
        for h in range(2):
            for c in range(2):
                for e in range(4):
                    r0 = (c * 4 + e) * R
                    out32[pl.ds(c * 256 + 8 * q + 4 * h + e, R, stride=R), :] = out[
                        r0:r0 + R, h * L:(h + 1) * L
                    ]
    for c in range(2):
        for k2 in range(16):
            at = c * 256 + k2 * R
            tendency[c, :, k2 * L:(k2 + 1) * L] = out32[at:at + R, :]

    pltpu.make_async_copy(got.at[pl.ds(0, D - 1)], got.at[pl.ds(0, D - 1)], ssem).wait()
    pltpu.make_async_copy(send.at[pl.ds(0, D - 1)], send.at[pl.ds(0, D - 1)], ssem2).wait()


def vmem(n):
    return [pl.BlockSpec(memory_space=pltpu.VMEM)] * n


def shards(eta_hat, phi_hat, patch_tiles, fraction):
    smem = pl.BlockSpec(memory_space=pltpu.SMEM)
    dma = pltpu.SemaphoreType.DMA
    phys, foot = pl.pallas_call(
        rise_kernel,
        out_shape=(
            jax.ShapeDtypeStruct((48 * R, L), F32),
            jax.ShapeDtypeStruct((2, 6, R, L), BF16),
        ),
        in_specs=[smem] + vmem(9),
        out_specs=tuple(vmem(2)),
        scratch_shapes=[
            pltpu.VMEM((16, L, 2 * L), BF16),
            pltpu.VMEM((D * R, L), F32),
            pltpu.VMEM((D, R, L), BF16),
            pltpu.VMEM((D, R, L), BF16),
            pltpu.VMEM((NG, 6, R, L), BF16),
            pltpu.VMEM((NG, 6, R, L), BF16),
            pltpu.VMEM((NW, 6, R, L), BF16),
            pltpu.VMEM((NW, 6, R, L), BF16),
        ] + [dma] * 6,
        compiler_params=pltpu.CompilerParams(
            collective_id=1, has_side_effects=True, vmem_limit_bytes=VMEM_LIMIT
        ),
        name="rise",
    )(patch_tiles, eta_hat, phi_hat, *lane_tables(1), *block_tables(1, 3, False))

    new_state, coarse = patches(foot, fraction[:, 0])

    surface, tendency = pl.pallas_call(
        fall_kernel,
        out_shape=(
            jax.ShapeDtypeStruct((R, N), F32),
            jax.ShapeDtypeStruct((2, R, N), F32),
        ),
        in_specs=[smem] + vmem(9),
        out_specs=tuple(vmem(2)),
        scratch_shapes=[
            pltpu.SMEM((3, 32), jnp.int32),
            pltpu.VMEM((4, L, 2 * L), BF16),
            pltpu.VMEM((D, R, L), BF16),
            pltpu.VMEM((D, 4, L), F32),
            pltpu.VMEM((D, 4, L), F32),
            pltpu.VMEM((512, L), F32),
        ] + [dma] * 4,
        compiler_params=pltpu.CompilerParams(
            collective_id=2, has_side_effects=True, vmem_limit_bytes=VMEM_LIMIT
        ),
        name="fall",
    )(patch_tiles, phys, coarse, *lane_tables(-1), *block_tables(-1, 4, True))
    return (surface, new_state[:, None], tendency)


def solution(mesh):
    placed = (
        P(None, ("wide", "grp"), None),
        P(None, ("wide", "grp"), None),
        P(),
        P(None, ("wide", "grp"), None, None, None),
    )
    return jax.shard_map(
        shards,
        mesh=mesh,
        in_specs=placed,
        out_specs=(
            P(("wide", "grp"), None),
            P(None, ("wide", "grp"), None, None, None),
            P(None, ("wide", "grp"), None),
        ),
        check_vma=False,
    )
```

```python
import functools
import math

import jax
import jax.numpy as jnp
import numpy as np
from jax import lax
from jax.experimental import pallas as pl
from jax.experimental.pallas import tpu as pltpu
from jax.sharding import PartitionSpec as P

F32 = jnp.float32
BF16 = jnp.bfloat16
MESH = pl.DeviceIdType.MESH

N = 2048
D = 128
NW = 16
NG = 8
L = 128
R = 16
LV = 64
SIDE = 128
TS = 64
Z_BOTTOM = -2.0
Z_TOP = 2.0
DECAY_RATE = 0.5
COURANT = 0.3
VMEM_LIMIT = 56 << 20


def unit(phase, length):
    angle = (phase % length) * (2.0 * math.pi / length)
    return np.cos(angle), np.sin(angle)


def lane_tables(sign, by_group):
    k1 = np.arange(R)[:, None]
    n2 = np.arange(L)[None, :]
    tc, ts = unit(k1 * n2, N)
    k2 = np.arange(D)
    if by_group:
        k2 = k2.reshape(NW, NG).T.reshape(-1)
    c, s = unit(k2[:, None] * n2, D)
    spread = np.concatenate([c, sign * s], axis=1)
    return (
        jnp.asarray(tc, F32),
        jnp.asarray(sign * ts, F32),
        jnp.asarray(spread, F32).astype(BF16),
    )


def block_tables(sign, blocks, full):
    k1 = np.arange(D)[:, None]
    src = np.arange(D)[None, :]
    c, s = unit(k1 * src, D)
    gather = np.concatenate([c, sign * s], axis=0)
    j = np.tile(np.arange(R), 8)[None, :]
    tc, ts = unit(k1 * j, N)
    k2 = np.arange(R)[:, None]
    jj = np.arange(R)[None, :]
    cc, ss = unit(k2 * jj, R)
    ss = sign * ss
    rows = []
    for part in range(2 if full else 1):
        for e in range(blocks):
            out = np.zeros((R, 2, 4, R))
            out[:, 0, e, :] = cc if part == 0 else ss
            out[:, 1, e, :] = -ss if part == 0 else cc
            rows.append(out.reshape(R, L))
    finish = np.concatenate(rows, axis=0)
    return (
        jnp.asarray(gather, F32).astype(BF16),
        jnp.asarray(tc, F32),
        jnp.asarray(sign * ts, F32),
        jnp.asarray(finish, F32).astype(BF16),
    )


def fourth(x, sign):
    (ar, ai), (br, bi), (cr, ci), (dr, di) = x
    t0r, t0i, t1r, t1i = ar + cr, ai + ci, ar - cr, ai - ci
    t2r, t2i, t3r, t3i = br + dr, bi + di, br - dr, bi - di
    if sign < 0:
        t3r, t3i = -t3r, -t3i
    return (
        (t0r + t2r, t0i + t2i),
        (t1r - t3i, t1i + t3r),
        (t0r - t2r, t0i - t2i),
        (t1r + t3i, t1i - t3r),
    )


def times(x, re, im):
    if abs(im) < 1e-12 and abs(re - 1.0) < 1e-12:
        return x
    a, b = x
    return (a * re - b * im, a * im + b * re)


def sixteenth(x, sign):
    inner = []
    for b in range(4):
        y = fourth([x[4 * a + b] for a in range(4)], sign)
        turned = []
        for c in range(4):
            angle = sign * 2.0 * math.pi * b * c / 16
            turned.append(times(y[c], math.cos(angle), math.sin(angle)))
        inner.append(turned)
    out = [None] * 16
    for c in range(4):
        z = fourth([inner[b][c] for b in range(4)], sign)
        for d in range(4):
            out[c + 4 * d] = z[d]
    return out


def nt_dot(a, b):
    return lax.dot_general(a, b, (((1,), (1,)), ((), ())), preferred_element_type=F32)


def blocks_in(x, gather, tc, ts, flip):
    both = jnp.dot(gather, x, preferred_element_type=F32)
    parts = []
    for h in range(2):
        a = both[:D, h * L:(h + 1) * L]
        b = both[D:, h * L:(h + 1) * L]
        u = a * tc - b * ts
        v = b * tc + a * ts
        parts.append((u + flip * pltpu.roll(v, 64, 1)).astype(BF16))
    return jnp.concatenate(parts, axis=0)


def coords(flat):
    return (flat // NG, flat % NG)


def lane_iota(rows):
    return lax.broadcasted_iota(jnp.int32, (rows, L), 1)


def greet_all(me):
    barrier = pltpu.get_barrier_semaphore()

    def greet(k, carry):
        pl.semaphore_signal(
            barrier, inc=1, device_id=coords(lax.rem(me + k, D)), device_id_type=MESH
        )
        return carry

    lax.fori_loop(1, D, greet, 0)
    return barrier


def rise_kernel(
    tiles, eta, phi, tw_c, tw_s, spread, gather, bt_c, bt_s, finish,
    phys, foot,
    tb, wide32, send, recv, send1, recv1, send2, recv2,
    ssem, rsem, ssem1, rsem1, ssem2, rsem2,
):
    w = lax.axis_index("wide")
    g = lax.axis_index("grp")
    me = w * NG + g
    barrier = greet_all(me)

    row = lax.broadcasted_iota(jnp.int32, (R, L), 0)
    lane = lane_iota(R)
    kx = me * R + row
    kx = jnp.where(kx >= N // 2, kx - N, kx).astype(F32) * (2.0 * math.pi / N)

    for f in range(3):
        x = []
        for n1 in range(16):
            cols = slice(n1 * L, (n1 + 1) * L)
            if f == 0:
                x.append((eta[0, :, cols].astype(F32), eta[1, :, cols].astype(F32)))
            else:
                if f == 1:
                    k = kx
                else:
                    base = n1 * L if n1 < 8 else n1 * L - N
                    k = (lane + base).astype(F32) * (2.0 * math.pi / N)
                x.append((-k * phi[1, :, cols].astype(F32), k * phi[0, :, cols].astype(F32)))
        y = sixteenth(x, 1)
        for k1 in range(16):
            c, s = tw_c[k1:k1 + 1, :], tw_s[k1:k1 + 1, :]
            a, b = y[k1]
            re = (a * c - b * s).astype(BF16)
            im = (a * s + b * c).astype(BF16)
            up = slice(f * R, (f + 1) * R)
            dn = slice(64 + f * R, 64 + (f + 1) * R)
            tb[k1, up, 0:L] = re
            tb[k1, up, L:2 * L] = -im
            tb[k1, dn, 0:L] = im
            tb[k1, dn, L:2 * L] = re

    zero = jnp.zeros((R, 2 * L), BF16)

    def rows_out(kk, carry):
        for h in range(2):
            tb[2 * kk + h, 48:64, :] = zero
            tb[2 * kk + h, 112:128, :] = zero
        rhs = tb[pl.ds(2 * kk, 2)].reshape(2 * L, 2 * L)
        z = nt_dot(spread[...], rhs)
        wide32[pl.ds(2 * kk, D, stride=R), :] = z[:, :L]
        wide32[pl.ds(2 * kk + 1, D, stride=R), :] = z[:, L:]
        return carry

    lax.fori_loop(0, 8, rows_out, 0, unroll=2)

    def narrow(i, carry):
        part = wide32[pl.ds(pl.multiple_of(i * 128, 128), 128), :]
        send[pl.ds(i * 8, 8)] = part.reshape(8, R, L).astype(BF16)
        return carry

    lax.fori_loop(0, 16, narrow, 0)

    pl.semaphore_wait(barrier, D - 1)
    pltpu.make_async_copy(send.at[me], recv.at[me], rsem).start()

    def post(k, carry):
        d = lax.rem(me + k, D)
        pltpu.make_async_remote_copy(
            send.at[d], recv.at[me], ssem, rsem, device_id=coords(d), device_id_type=MESH
        ).start()
        return carry

    lax.fori_loop(1, D, post, 0)
    pltpu.make_async_copy(recv, recv, rsem).wait()

    def widen(i, carry):
        part = recv[pl.ds(i * 8, 8)].astype(F32)
        wide32[pl.ds(pl.multiple_of(i * 128, 128), 128), :] = part.reshape(128, L)
        return carry

    lax.fori_loop(0, 16, widen, 0)

    flip = jnp.where(lane_iota(D) < 64, -1.0, 1.0).astype(F32)

    def columns(yy, carry):
        x = jnp.concatenate(
            [
                wide32[pl.ds(2 * yy, D, stride=R), :].astype(BF16),
                wide32[pl.ds(2 * yy + 1, D, stride=R), :].astype(BF16),
            ],
            axis=1,
        )
        t = blocks_in(x, gather[...], bt_c[...], bt_s[...], flip)
        out = nt_dot(finish[...], t)
        phys[pl.ds(2 * yy, 48, stride=R), :] = out[:, :L]
        phys[pl.ds(2 * yy + 1, 48, stride=R), :] = out[:, L:]
        return carry

    lax.fori_loop(0, 8, columns, 0, unroll=4)

    low = lane < 64

    def by_group(q, carry):
        for h in range(2):
            at = [pl.multiple_of((f * 16 + 2 * q + h) * R, R) for f in range(3)]
            ht = phys[pl.ds(at[0], R), :]
            vx = phys[pl.ds(at[1], R), :]
            vy = phys[pl.ds(at[2], R), :]
            send1[q, h] = ht.astype(BF16)
            send1[q, 2 + 2 * h] = jnp.where(low, vx, pltpu.roll(vy, 64, 1)).astype(BF16)
            send1[q, 3 + 2 * h] = jnp.where(low, pltpu.roll(vx, 64, 1), vy).astype(BF16)
        return carry

    lax.fori_loop(0, NG, by_group, 0, unroll=2)

    pltpu.make_async_copy(send1.at[g], recv1.at[g], rsem1).start()
    for k in range(1, NG):
        d = lax.rem(g + k, NG)
        pltpu.make_async_remote_copy(
            send1.at[d], recv1.at[g], ssem1, rsem1, device_id=(w, d), device_id_type=MESH
        ).start()
    pltpu.make_async_copy(recv1, recv1, rsem1).wait()

    def choose(d, carry):
        t0 = tiles[g * 32 + d]
        t1 = tiles[g * 32 + 16 + d]
        t = jnp.where(lax.shift_right_logical(t0, 6) == w, t0, t1)
        upper = jnp.bitwise_and(lax.shift_right_logical(t, 5), 1) * 4
        col = jnp.bitwise_and(t, 3)
        odd = jnp.bitwise_and(t, 1)
        pair = lax.shift_right_logical(col, 1)
        right = (lane * 0 + odd) == 1
        for q in range(4):
            send2[d, q] = recv1[upper + q, 2 + col]
        for q in range(2):
            a = recv1[upper + 2 * q, pair].astype(F32)
            b = recv1[upper + 2 * q + 1, pair].astype(F32)
            lo = jnp.where(right, pltpu.roll(a, 64, 1), a)
            hi = jnp.where(right, b, pltpu.roll(b, 64, 1))
            send2[d, 4 + q] = jnp.where(low, lo, hi).astype(BF16)
        return carry

    lax.fori_loop(0, NW, choose, 0)

    pltpu.make_async_copy(send2.at[w], recv2.at[w], rsem2).start()
    for k in range(1, NW):
        d = lax.rem(w + k, NW)
        pltpu.make_async_remote_copy(
            send2.at[d], recv2.at[w], ssem2, rsem2, device_id=(d, g), device_id_type=MESH
        ).start()
    pltpu.make_async_copy(recv2, recv2, rsem2).wait()

    for s in range(2):
        t = tiles[g * 32 + s * 16 + w]
        band = jnp.bitwise_and(lax.shift_right_logical(t, 6), NW - 1)
        for q in range(6):
            foot[s, q] = recv2[band, q]

    pltpu.make_async_copy(send.at[pl.ds(0, D - 1)], send.at[pl.ds(0, D - 1)], ssem).wait()
    pltpu.make_async_copy(send1.at[pl.ds(0, NG - 1)], send1.at[pl.ds(0, NG - 1)], ssem1).wait()
    pltpu.make_async_copy(send2.at[pl.ds(0, NW - 1)], send2.at[pl.ds(0, NW - 1)], ssem2).wait()


def patch_tables():
    pos = np.arange(SIDE)
    edge = np.minimum(pos, SIDE - 1 - pos)
    dist = np.minimum(edge[:, None], edge[None, :])
    weight = 0.3 + 0.7 * np.exp(-8.0 * dist / SIDE)
    x = np.arange(SIDE)
    pick = np.zeros((2, L, SIDE))
    for h in range(2):
        pick[h, 64 * h + x // 2, x] = 1.0
    rows = np.zeros((SIDE, TS))
    rows[x, x // 2] = 1.0
    halves = np.zeros((2, SIDE, 32))
    for i in range(SIDE):
        r = i // 2
        blk, within = r // 16, r % 16
        halves[blk % 2, i, (blk // 2) * 16 + within] = 1.0
    z = Z_BOTTOM + (np.arange(LV) + 0.5) * ((Z_TOP - Z_BOTTOM) / LV)
    prof = np.exp(DECAY_RATE * (z - Z_TOP))
    return (
        jnp.asarray(prof, F32),
        jnp.asarray(weight, F32),
        jnp.asarray(pick, F32).astype(BF16),
        jnp.asarray(rows, F32).astype(BF16),
        jnp.asarray(halves, F32).astype(BF16),
    )


RB = 16
PAD = 8
STEP = 16
TOGETHER = 8


def patch_kernel(
    prof, foot, state, weight, pick, rows, halves, down_rows, down_cols,
    state_out, coarse,
    hh, cf, bl, total,
):
    j = pl.program_id(1)
    scale = LV / (Z_TOP - Z_BOTTOM)

    @pl.when(j == 0)
    def _():
        vel = foot[0, 0:4].reshape(64, L)
        hgt = foot[0, 4:6].reshape(32, L)

        def up(m, sel, spread_rows):
            wide = jnp.dot(m, sel, preferred_element_type=F32).astype(BF16)
            return jnp.dot(spread_rows, wide, preferred_element_type=F32)

        height = up(hgt, pick[0], halves[0]) + up(hgt, pick[1], halves[1])
        ax = up(vel, pick[0], rows[...])
        ay = up(vel, pick[1], rows[...])
        hh[...] = height * scale - Z_BOTTOM * scale

        lane = lax.broadcasted_iota(jnp.int32, (SIDE, SIDE), 1)
        sub = lax.broadcasted_iota(jnp.int32, (SIDE, SIDE), 0)

        def faces(a, axis, index):
            after = jnp.where(index == SIDE - 1, a, pltpu.roll(a, SIDE - 1, axis))
            before = jnp.where(index == 0, a, pltpu.roll(a, 1, axis))
            return (0.5 * COURANT) * (a + after), (0.5 * COURANT) * (before + a)

        center = jnp.zeros((SIDE, SIDE), F32)
        for n, (a, axis, index) in enumerate(((ax, 1, lane), (ay, 0, sub))):
            upper, lower = faces(a, axis, index)
            center += jnp.maximum(upper, 0.0) - jnp.minimum(lower, 0.0)
            from_up = jnp.minimum(upper, 0.0)
            from_low = -jnp.maximum(lower, 0.0)
            last, first = index == SIDE - 1, index == 0
            center += jnp.where(last, from_up, 0.0) + jnp.where(first, from_low, 0.0)
            cf[1 + 2 * n] = jnp.where(last, 0.0, from_up)
            cf[2 + 2 * n] = jnp.where(first, 0.0, from_low)
        cf[0] = center
        total[...] = jnp.zeros((SIDE, SIDE), F32)
        edge = jnp.zeros((TOGETHER, PAD, SIDE), F32)
        bl[:, 0:PAD, :] = edge
        bl[:, PAD + SIDE:, :] = edge

    def group(i, carry):
        for b in range(SIDE // RB):
            rs = slice(b * RB, (b + 1) * RB)
            h, wt = hh[rs, :], weight[rs, :]
            keep = 1.0 - wt
            for l in range(TOGETHER):
                here = i * TOGETHER + l
                sea = jnp.clip(h - (j * STEP + here).astype(F32), 0.0, 1.0)
                bl[l, PAD + b * RB:PAD + (b + 1) * RB, :] = (
                    wt * sea + keep * state[0, here, rs, :].astype(F32)
                )
        for b in range(SIDE // RB):
            rs = slice(b * RB, (b + 1) * RB)
            at = PAD + b * RB
            c0, c1, c2, c3, c4 = (cf[n, rs, :] for n in range(5))
            acc = total[rs, :]
            for l in range(TOGETHER):
                here = i * TOGETHER + l
                mid = bl[l, at:at + RB, :]
                nxt = bl[l, at + 1:at + 1 + RB, :]
                prv = bl[l, at - 1:at - 1 + RB, :]
                out = c0 * mid + c1 * pltpu.roll(mid, SIDE - 1, 1) + c2 * pltpu.roll(mid, 1, 1)
                out = out + c3 * nxt + c4 * prv
                new = jnp.clip(mid - prof[j * STEP + here] * out, 0.0, 1.0)
                state_out[0, here, rs, :] = new.astype(BF16)
                acc = acc + new
            total[rs, :] = acc
        return carry

    lax.fori_loop(0, STEP // TOGETHER, group, 0)

    @pl.when(j == LV // STEP - 1)
    def _():
        column = total[...] * (1.0 / scale) + Z_BOTTOM
        high = lax.Precision.HIGHEST

        def down(h):
            part = jnp.dot(down_rows[h], column, preferred_element_type=F32, precision=high)
            return jnp.dot(part, down_cols[h], preferred_element_type=F32, precision=high)

        coarse[0] = (0.25 * (down(0) + down(1))).astype(BF16).reshape(2, R, L)


def patches(foot, fraction):
    prof, weight, pick, rows, halves = patch_tables()
    down_rows = jnp.swapaxes(halves, 1, 2).astype(F32)
    down_cols = jnp.swapaxes(pick, 1, 2).astype(F32)
    full = lambda shape: pl.BlockSpec(shape, lambda s, j: (0,) * len(shape))
    levels = pl.BlockSpec((1, STEP, SIDE, SIDE), lambda s, j: (s, j, 0, 0))
    return pl.pallas_call(
        patch_kernel,
        grid=(2, LV // STEP),
        out_shape=(
            jax.ShapeDtypeStruct((2, LV, SIDE, SIDE), BF16),
            jax.ShapeDtypeStruct((2, 2, R, L), BF16),
        ),
        in_specs=[
            pl.BlockSpec(memory_space=pltpu.SMEM),
            pl.BlockSpec((1, 6, R, L), lambda s, j: (s, 0, 0, 0)),
            levels,
            full((SIDE, SIDE)),
            full((2, L, SIDE)),
            full((SIDE, TS)),
            full((2, SIDE, 32)),
            full((2, 32, SIDE)),
            full((2, SIDE, L)),
        ],
        out_specs=(levels, pl.BlockSpec((1, 2, R, L), lambda s, j: (s, 0, 0, 0))),
        scratch_shapes=[
            pltpu.VMEM((SIDE, SIDE), F32),
            pltpu.VMEM((5, SIDE, SIDE), F32),
            pltpu.VMEM((TOGETHER, SIDE + 2 * PAD, SIDE), F32),
            pltpu.VMEM((SIDE, SIDE), F32),
        ],
        compiler_params=pltpu.CompilerParams(
            dimension_semantics=("arbitrary", "arbitrary"), vmem_limit_bytes=VMEM_LIMIT
        ),
        name="patches",
    )(prof, foot, fraction, weight, pick, rows, halves, down_rows, down_cols)


def rank_of(tiles, q, want):
    at = jnp.int32(0)
    for step in (16, 8, 4, 2, 1):
        at = at + jnp.where(tiles[q * 32 + at + step - 1] < want, step, 0)
    return at


def fall_kernel(
    tiles, phys, coarse, tw_c, tw_s, spread, gather, bt_c, bt_s, finish,
    out,
    source, tb, block, got1, strip, got2, send1, recv1, rows32, send2, recv2, cols32, out32,
    bsem, bsem2, csem1, dsem1, csem2, dsem2, csem3, dsem3,
):
    w = lax.axis_index("wide")
    g = lax.axis_index("grp")
    barrier = pltpu.get_barrier_semaphore()
    for k in range(1, NG):
        pl.semaphore_signal(
            barrier, inc=1, device_id=(w, lax.rem(g + k, NG)), device_id_type=MESH
        )
    for k in range(1, NW):
        pl.semaphore_signal(
            barrier, inc=1, device_id=(lax.rem(w + k, NW), g), device_id_type=MESH
        )

    first = lax.shift_right_logical(tiles[g * 32 + w], 6)
    for d in range(NW):
        slot = jnp.where(first == d, 0, 1)
        for p in range(2):
            block[d, p] = coarse[slot, p]

    pl.semaphore_wait(barrier, NG + NW - 2)

    pltpu.make_async_copy(block.at[w], got1.at[w], csem1).start()
    for k in range(1, NW):
        d = lax.rem(w + k, NW)
        pltpu.make_async_remote_copy(
            block.at[d], got1.at[w], bsem, csem1, device_id=(d, g), device_id_type=MESH
        ).start()

    for upper in range(2):
        want = (2 * w + upper) * 32 + 4 * g
        at = rank_of(tiles, g, want)
        for c in range(4):
            source[0, 4 * upper + c] = jnp.bitwise_and(at, NW - 1)
            at = jnp.minimum(at + jnp.where(tiles[g * 32 + at] <= want + c, 1, 0), 31)
    for q in range(NG):
        want = (2 * w + g // 4) * 32 + 4 * q
        at = rank_of(tiles, q, want)
        for c in range(4):
            found = tiles[q * 32 + at]
            source[1, 4 * q + c] = jnp.where(found == want + c, 1, 0)
            at = jnp.minimum(at + jnp.where(found <= want + c, 1, 0), 31)

    lane = lane_iota(R)
    low = lane < 64
    pltpu.make_async_copy(got1, got1, csem1).wait()

    for q in range(NG):
        upper, rb = q // 4, q % 4
        for p in range(2):
            sides = []
            for h in range(2):
                tile = got1[source[0, 4 * upper + 2 * p + h], rb // 2].astype(F32)
                sides.append(tile if rb % 2 == h else pltpu.roll(tile, 64, 1))
            strip[q, p] = jnp.where(low, sides[0], sides[1]).astype(BF16)

    pltpu.make_async_copy(strip.at[g], got2.at[g], csem2).start()
    for k in range(1, NG):
        d = lax.rem(g + k, NG)
        pltpu.make_async_remote_copy(
            strip.at[d], got2.at[g], dsem1, csem2, device_id=(w, d), device_id_type=MESH
        ).start()
    pltpu.make_async_copy(got2, got2, csem2).wait()

    x = []
    for k2 in range(16):
        there = jnp.where(low, source[1, 2 * k2], source[1, 2 * k2 + 1]) == 1
        ht = phys[k2 * R:(k2 + 1) * R, :]
        vx = phys[256 + k2 * R:256 + (k2 + 1) * R, :]
        vy = phys[512 + k2 * R:512 + (k2 + 1) * R, :]
        sea = -jnp.where(there, got2[k2 // 2, k2 % 2].astype(F32), ht)
        out[0, :, k2 * L:(k2 + 1) * L] = sea
        x.append((sea - 0.5 * (vx * vx + vy * vy), jnp.zeros((R, L), F32)))
    y = sixteenth(x, -1)
    for k1 in range(16):
        c, s = tw_c[k1:k1 + 1, :], tw_s[k1:k1 + 1, :]
        a, b = y[k1]
        re = (a * c - b * s).astype(BF16)
        im = (a * s + b * c).astype(BF16)
        q, e = k1 // 4, k1 % 4
        up = slice(e * R, (e + 1) * R)
        dn = slice(64 + e * R, 64 + (e + 1) * R)
        tb[q, up, 0:L] = re
        tb[q, up, L:2 * L] = -im
        tb[q, dn, 0:L] = im
        tb[q, dn, L:2 * L] = re

    for q in range(2):
        rhs = tb[2 * q:2 * q + 2].reshape(2 * L, 2 * L)
        z = nt_dot(spread[...], rhs).astype(BF16)
        for h in range(2):
            for d in range(NG):
                send1[d, 2 * q + h] = z[d * NW:(d + 1) * NW, h * L:(h + 1) * L]

    pltpu.make_async_copy(send1.at[g], recv1.at[g], csem3).start()
    for k in range(1, NG):
        d = lax.rem(g + k, NG)
        pltpu.make_async_remote_copy(
            send1.at[d], recv1.at[g], dsem2, csem3, device_id=(w, d), device_id_type=MESH
        ).start()
    pltpu.make_async_copy(recv1, recv1, csem3).wait()

    rows32[...] = recv1[...].astype(F32).reshape(4 * NG * NW, L)
    for d in range(NW):
        send2[d] = rows32[pl.ds(d, 4 * NG, stride=NW), :].astype(BF16).reshape(2, R, L)

    pltpu.make_async_copy(send2.at[w], recv2.at[w], dsem3).start()
    for k in range(1, NW):
        d = lax.rem(w + k, NW)
        pltpu.make_async_remote_copy(
            send2.at[d], recv2.at[w], bsem2, dsem3, device_id=(d, g), device_id_type=MESH
        ).start()
    pltpu.make_async_copy(recv2, recv2, dsem3).wait()

    cols32[...] = recv2[...].astype(F32).reshape(4 * D, L)
    flip = jnp.where(lane_iota(D) < 64, -1.0, 1.0).astype(F32)
    for q in range(2):
        xx = jnp.concatenate(
            [
                cols32[pl.ds(2 * q, D, stride=4), :].astype(BF16),
                cols32[pl.ds(2 * q + 1, D, stride=4), :].astype(BF16),
            ],
            axis=1,
        )
        t = blocks_in(xx, gather[...], bt_c[...], bt_s[...], flip)
        done = nt_dot(finish[...], t)
        for h in range(2):
            for c in range(2):
                for e in range(4):
                    r0 = (c * 4 + e) * R
                    out32[pl.ds(c * 256 + 8 * q + 4 * h + e, R, stride=R), :] = done[
                        r0:r0 + R, h * L:(h + 1) * L
                    ]
    for c in range(2):
        for k2 in range(16):
            at = c * 256 + k2 * R
            out[1 + c, :, k2 * L:(k2 + 1) * L] = out32[at:at + R, :]

    def sent(buf, n, sem):
        pltpu.make_async_copy(buf.at[pl.ds(0, n)], buf.at[pl.ds(0, n)], sem).wait()

    sent(block, NW - 1, bsem)
    sent(send2, NW - 1, bsem2)
    sent(strip, NG - 1, dsem1)
    sent(send1, NG - 1, dsem2)


def vmem(n):
    return [pl.BlockSpec(memory_space=pltpu.VMEM)] * n


def shards(eta_hat, phi_hat, patch_tiles, fraction):
    smem = pl.BlockSpec(memory_space=pltpu.SMEM)
    dma = pltpu.SemaphoreType.DMA
    phys, foot = pl.pallas_call(
        rise_kernel,
        out_shape=(
            jax.ShapeDtypeStruct((48 * R, L), F32),
            jax.ShapeDtypeStruct((2, 6, R, L), BF16),
        ),
        in_specs=[smem] + vmem(9),
        out_specs=tuple(vmem(2)),
        scratch_shapes=[
            pltpu.VMEM((16, L, 2 * L), BF16),
            pltpu.VMEM((D * R, L), F32),
            pltpu.VMEM((D, R, L), BF16),
            pltpu.VMEM((D, R, L), BF16),
            pltpu.VMEM((NG, 6, R, L), BF16),
            pltpu.VMEM((NG, 6, R, L), BF16),
            pltpu.VMEM((NW, 6, R, L), BF16),
            pltpu.VMEM((NW, 6, R, L), BF16),
        ] + [dma] * 6,
        compiler_params=pltpu.CompilerParams(
            collective_id=1, has_side_effects=True, vmem_limit_bytes=VMEM_LIMIT
        ),
        name="rise",
    )(patch_tiles, eta_hat, phi_hat, *lane_tables(1, False), *block_tables(1, 3, False))

    new_state, coarse = patches(foot, fraction[:, 0])

    fallen = pl.pallas_call(
        fall_kernel,
        out_shape=jax.ShapeDtypeStruct((3, R, N), F32),
        in_specs=[smem] + vmem(9),
        out_specs=vmem(1)[0],
        scratch_shapes=[
            pltpu.SMEM((2, 32), jnp.int32),
            pltpu.VMEM((4, L, 2 * L), BF16),
            pltpu.VMEM((NW, 2, R, L), BF16),
            pltpu.VMEM((NW, 2, R, L), BF16),
            pltpu.VMEM((NG, 2, R, L), BF16),
            pltpu.VMEM((NG, 2, R, L), BF16),
            pltpu.VMEM((NG, 4, NW, L), BF16),
            pltpu.VMEM((NG, 4, NW, L), BF16),
            pltpu.VMEM((4 * NG * NW, L), F32),
            pltpu.VMEM((NW, 2, R, L), BF16),
            pltpu.VMEM((NW, 2, R, L), BF16),
            pltpu.VMEM((4 * D, L), F32),
            pltpu.VMEM((512, L), F32),
        ] + [dma] * 8,
        compiler_params=pltpu.CompilerParams(
            collective_id=2, has_side_effects=True, vmem_limit_bytes=VMEM_LIMIT
        ),
        name="fall",
    )(patch_tiles, phys, coarse, *lane_tables(-1, True), *block_tables(-1, 4, True))
    return (-fallen[0], new_state[:, None], fallen[1:] * (1.0 / N))


def solution(mesh):
    placed = (
        P(None, ("wide", "grp"), None),
        P(None, ("wide", "grp"), None),
        P(),
        P(None, ("wide", "grp"), None, None, None),
    )
    return jax.shard_map(
        shards,
        mesh=mesh,
        in_specs=placed,
        out_specs=(
            P(("wide", "grp"), None),
            P(None, ("wide", "grp"), None, None, None),
            P(None, ("wide", "grp"), None),
        ),
        check_vma=False,
    )
```

```python
import functools
import math

import jax
import jax.numpy as jnp
import numpy as np
from jax import lax
from jax.experimental import pallas as pl
from jax.experimental.pallas import tpu as pltpu
from jax.sharding import PartitionSpec as P

F32 = jnp.float32
BF16 = jnp.bfloat16
MESH = pl.DeviceIdType.MESH

N = 2048
D = 128
NW = 16
NG = 8
L = 128
R = 16
LV = 64
SIDE = 128
TS = 64
Z_BOTTOM = -2.0
Z_TOP = 2.0
DECAY_RATE = 0.5
COURANT = 0.3
VMEM_LIMIT = 56 << 20


def unit(phase, length):
    angle = (phase % length) * (2.0 * math.pi / length)
    return np.cos(angle), np.sin(angle)


def lane_tables(sign):
    k1 = np.arange(R)[:, None]
    n2 = np.arange(L)[None, :]
    tc, ts = unit(k1 * n2, N)
    k2 = np.arange(D)[:, None]
    c, s = unit(k2 * n2, D)
    spread = np.concatenate([c, sign * s], axis=1)
    return (
        jnp.asarray(tc, F32),
        jnp.asarray(sign * ts, F32),
        jnp.asarray(spread, F32).astype(BF16),
    )


def block_tables(sign, blocks, full):
    k1 = np.arange(D)[:, None]
    src = np.arange(D)[None, :]
    c, s = unit(k1 * src, D)
    gather = np.concatenate([c, sign * s], axis=0)
    j = np.tile(np.arange(R), 8)[None, :]
    tc, ts = unit(k1 * j, N)
    k2 = np.arange(R)[:, None]
    jj = np.arange(R)[None, :]
    cc, ss = unit(k2 * jj, R)
    ss = sign * ss
    rows = []
    for part in range(2 if full else 1):
        for e in range(blocks):
            out = np.zeros((R, 2, 4, R))
            out[:, 0, e, :] = cc if part == 0 else ss
            out[:, 1, e, :] = -ss if part == 0 else cc
            rows.append(out.reshape(R, L))
    finish = np.concatenate(rows, axis=0)
    return (
        jnp.asarray(gather, F32).astype(BF16),
        jnp.asarray(tc, F32),
        jnp.asarray(sign * ts, F32),
        jnp.asarray(finish, F32).astype(BF16),
    )


def fourth(x, sign):
    (ar, ai), (br, bi), (cr, ci), (dr, di) = x
    t0r, t0i, t1r, t1i = ar + cr, ai + ci, ar - cr, ai - ci
    t2r, t2i, t3r, t3i = br + dr, bi + di, br - dr, bi - di
    if sign < 0:
        t3r, t3i = -t3r, -t3i
    return (
        (t0r + t2r, t0i + t2i),
        (t1r - t3i, t1i + t3r),
        (t0r - t2r, t0i - t2i),
        (t1r + t3i, t1i - t3r),
    )


def times(x, re, im):
    if abs(im) < 1e-12 and abs(re - 1.0) < 1e-12:
        return x
    a, b = x
    return (a * re - b * im, a * im + b * re)


def sixteenth(x, sign):
    inner = []
    for b in range(4):
        y = fourth([x[4 * a + b] for a in range(4)], sign)
        turned = []
        for c in range(4):
            angle = sign * 2.0 * math.pi * b * c / 16
            turned.append(times(y[c], math.cos(angle), math.sin(angle)))
        inner.append(turned)
    out = [None] * 16
    for c in range(4):
        z = fourth([inner[b][c] for b in range(4)], sign)
        for d in range(4):
            out[c + 4 * d] = z[d]
    return out


def nt_dot(a, b):
    return lax.dot_general(a, b, (((1,), (1,)), ((), ())), preferred_element_type=F32)


def blocks_in(x, gather, tc, ts, flip):
    both = jnp.dot(gather, x, preferred_element_type=F32)
    parts = []
    for h in range(2):
        a = both[:D, h * L:(h + 1) * L]
        b = both[D:, h * L:(h + 1) * L]
        u = a * tc - b * ts
        v = b * tc + a * ts
        parts.append((u + flip * pltpu.roll(v, 64, 1)).astype(BF16))
    return jnp.concatenate(parts, axis=0)


def lane_iota(rows):
    return lax.broadcasted_iota(jnp.int32, (rows, L), 1)


def hops(step):
    return min(step, 4 - step)


def far(kw, kg):
    return hops(kw // 4) + hops(kw % 4) + hops(kg // 2) + 0.5 * (kg % 2)


WIDE_STEPS = sorted(range(1, NW), key=lambda k: -far(k, 0))
GRP_STEPS = sorted(range(1, NG), key=lambda k: -far(0, k))
ALL_STEPS = sorted(
    [(kw, kg) for kw in range(NW) for kg in range(NG) if kw or kg], key=lambda k: -far(*k)
)


def around():
    w = lax.axis_index("wide")
    g = lax.axis_index("grp")
    y = [lax.rem(w // 4 + k, 4) for k in range(4)]
    z = [lax.rem(w % 4 + k, 4) for k in range(4)]
    x = [lax.rem(g // 2 + k, 4) for k in range(4)]
    c = [g % 2, 1 - g % 2]
    ws = [y[k // 4] * 4 + z[k % 4] for k in range(NW)]
    gs = [x[k // 2] * 2 + c[k % 2] for k in range(NG)]
    return w, g, ws, gs


def greet_all(ws, gs):
    barrier = pltpu.get_barrier_semaphore()
    for kw, kg in ALL_STEPS:
        pl.semaphore_signal(
            barrier, inc=1, device_id=(ws[kw], gs[kg]), device_id_type=MESH
        )
    return barrier


def spread_all(send, recv, ssem, rsem, ws, gs):
    me = ws[0] * NG + gs[0]
    pltpu.make_async_copy(send.at[me], recv.at[me], rsem).start()
    for kw, kg in ALL_STEPS:
        pltpu.make_async_remote_copy(
            send.at[ws[kw] * NG + gs[kg]], recv.at[me], ssem, rsem,
            device_id=(ws[kw], gs[kg]), device_id_type=MESH,
        ).start()
    pltpu.make_async_copy(recv, recv, rsem).wait()


def sent(buf, n, sem):
    pltpu.make_async_copy(buf.at[pl.ds(0, n)], buf.at[pl.ds(0, n)], sem).wait()


def rise_kernel(
    tiles, eta, phi, tw_c, tw_s, spread, gather, bt_c, bt_s, finish,
    phys, foot,
    tb, wide32, send, recv, send1, recv1, send2, recv2,
    ssem, rsem, ssem1, rsem1, ssem2, rsem2,
):
    w, g, ws, gs = around()
    me = w * NG + g
    barrier = greet_all(ws, gs)

    row = lax.broadcasted_iota(jnp.int32, (R, L), 0)
    lane = lane_iota(R)
    kx = me * R + row
    kx = jnp.where(kx >= N // 2, kx - N, kx).astype(F32) * (2.0 * math.pi / N)

    for f in range(3):
        x = []
        for n1 in range(16):
            cols = slice(n1 * L, (n1 + 1) * L)
            if f == 0:
                x.append((eta[0, :, cols].astype(F32), eta[1, :, cols].astype(F32)))
            else:
                if f == 1:
                    k = kx
                else:
                    base = n1 * L if n1 < 8 else n1 * L - N
                    k = (lane + base).astype(F32) * (2.0 * math.pi / N)
                x.append((-k * phi[1, :, cols].astype(F32), k * phi[0, :, cols].astype(F32)))
        y = sixteenth(x, 1)
        for k1 in range(16):
            c, s = tw_c[k1:k1 + 1, :], tw_s[k1:k1 + 1, :]
            a, b = y[k1]
            re = (a * c - b * s).astype(BF16)
            im = (a * s + b * c).astype(BF16)
            up = slice(f * R, (f + 1) * R)
            dn = slice(64 + f * R, 64 + (f + 1) * R)
            tb[k1, up, 0:L] = re
            tb[k1, up, L:2 * L] = -im
            tb[k1, dn, 0:L] = im
            tb[k1, dn, L:2 * L] = re

    zero = jnp.zeros((R, 2 * L), BF16)

    def rows_out(kk, carry):
        for h in range(2):
            tb[2 * kk + h, 48:64, :] = zero
            tb[2 * kk + h, 112:128, :] = zero
        rhs = tb[pl.ds(2 * kk, 2)].reshape(2 * L, 2 * L)
        z = nt_dot(spread[...], rhs)
        wide32[pl.ds(2 * kk, D, stride=R), :] = z[:, :L]
        wide32[pl.ds(2 * kk + 1, D, stride=R), :] = z[:, L:]
        return carry

    lax.fori_loop(0, 8, rows_out, 0, unroll=2)

    def narrow(i, carry):
        part = wide32[pl.ds(pl.multiple_of(i * 128, 128), 128), :]
        send[pl.ds(i * 8, 8)] = part.reshape(8, R, L).astype(BF16)
        return carry

    lax.fori_loop(0, 16, narrow, 0)

    pl.semaphore_wait(barrier, D - 1)
    spread_all(send, recv, ssem, rsem, ws, gs)

    def widen(i, carry):
        part = recv[pl.ds(i * 8, 8)].astype(F32)
        wide32[pl.ds(pl.multiple_of(i * 128, 128), 128), :] = part.reshape(128, L)
        return carry

    lax.fori_loop(0, 16, widen, 0)

    flip = jnp.where(lane_iota(D) < 64, -1.0, 1.0).astype(F32)

    def columns(yy, carry):
        x = jnp.concatenate(
            [
                wide32[pl.ds(2 * yy, D, stride=R), :].astype(BF16),
                wide32[pl.ds(2 * yy + 1, D, stride=R), :].astype(BF16),
            ],
            axis=1,
        )
        t = blocks_in(x, gather[...], bt_c[...], bt_s[...], flip)
        out = nt_dot(finish[...], t)
        phys[pl.ds(2 * yy, 48, stride=R), :] = out[:, :L]
        phys[pl.ds(2 * yy + 1, 48, stride=R), :] = out[:, L:]
        return carry

    lax.fori_loop(0, 8, columns, 0, unroll=4)

    low = lane < 64

    def by_group(q, carry):
        for h in range(2):
            at = [pl.multiple_of((f * 16 + 2 * q + h) * R, R) for f in range(3)]
            ht = phys[pl.ds(at[0], R), :]
            vx = phys[pl.ds(at[1], R), :]
            vy = phys[pl.ds(at[2], R), :]
            send1[q, h] = ht.astype(BF16)
            send1[q, 2 + 2 * h] = jnp.where(low, vx, pltpu.roll(vy, 64, 1)).astype(BF16)
            send1[q, 3 + 2 * h] = jnp.where(low, pltpu.roll(vx, 64, 1), vy).astype(BF16)
        return carry

    lax.fori_loop(0, NG, by_group, 0, unroll=2)

    pltpu.make_async_copy(send1.at[g], recv1.at[g], rsem1).start()
    for k in GRP_STEPS:
        d = gs[k]
        pltpu.make_async_remote_copy(
            send1.at[d], recv1.at[g], ssem1, rsem1, device_id=(w, d), device_id_type=MESH
        ).start()
    pltpu.make_async_copy(recv1, recv1, rsem1).wait()

    def choose(d, carry):
        t0 = tiles[g * 32 + d]
        t1 = tiles[g * 32 + 16 + d]
        t = jnp.where(lax.shift_right_logical(t0, 6) == w, t0, t1)
        upper = jnp.bitwise_and(lax.shift_right_logical(t, 5), 1) * 4
        col = jnp.bitwise_and(t, 3)
        odd = jnp.bitwise_and(t, 1)
        pair = lax.shift_right_logical(col, 1)
        right = (lane * 0 + odd) == 1
        for q in range(4):
            send2[d, q] = recv1[upper + q, 2 + col]
        for q in range(2):
            a = recv1[upper + 2 * q, pair].astype(F32)
            b = recv1[upper + 2 * q + 1, pair].astype(F32)
            lo = jnp.where(right, pltpu.roll(a, 64, 1), a)
            hi = jnp.where(right, b, pltpu.roll(b, 64, 1))
            send2[d, 4 + q] = jnp.where(low, lo, hi).astype(BF16)
        return carry

    lax.fori_loop(0, NW, choose, 0)

    pltpu.make_async_copy(send2.at[w], recv2.at[w], rsem2).start()
    for k in WIDE_STEPS:
        d = ws[k]
        pltpu.make_async_remote_copy(
            send2.at[d], recv2.at[w], ssem2, rsem2, device_id=(d, g), device_id_type=MESH
        ).start()
    pltpu.make_async_copy(recv2, recv2, rsem2).wait()

    for s in range(2):
        t = tiles[g * 32 + s * 16 + w]
        band = jnp.bitwise_and(lax.shift_right_logical(t, 6), NW - 1)
        for q in range(6):
            foot[s, q] = recv2[band, q]

    sent(send, D - 1, ssem)
    sent(send1, NG - 1, ssem1)
    sent(send2, NW - 1, ssem2)


def patch_tables():
    pos = np.arange(SIDE)
    edge = np.minimum(pos, SIDE - 1 - pos)
    dist = np.minimum(edge[:, None], edge[None, :])
    weight = 0.3 + 0.7 * np.exp(-8.0 * dist / SIDE)
    x = np.arange(SIDE)
    pick = np.zeros((2, L, SIDE))
    for h in range(2):
        pick[h, 64 * h + x // 2, x] = 1.0
    rows = np.zeros((SIDE, TS))
    rows[x, x // 2] = 1.0
    halves = np.zeros((2, SIDE, 32))
    for i in range(SIDE):
        r = i // 2
        blk, within = r // 16, r % 16
        halves[blk % 2, i, (blk // 2) * 16 + within] = 1.0
    z = Z_BOTTOM + (np.arange(LV) + 0.5) * ((Z_TOP - Z_BOTTOM) / LV)
    prof = np.exp(DECAY_RATE * (z - Z_TOP))
    return (
        jnp.asarray(prof, F32),
        jnp.asarray(weight, F32),
        jnp.asarray(pick, F32).astype(BF16),
        jnp.asarray(rows, F32).astype(BF16),
        jnp.asarray(halves, F32).astype(BF16),
    )


RB = 16
PAD = 8
CHUNK = 16
TOGETHER = 8
BAND = 32


def rank_of(tiles, q, want):
    at = jnp.int32(0)
    for step in (16, 8, 4, 2, 1):
        at = at + jnp.where(tiles[q * 32 + at + step - 1] < want, step, 0)
    return at


def fall_kernel(
    tiles, prof, phys, foot, state, weight, pick, rows, halves, down_rows, down_cols,
    tw_c, tw_s, spread,
    state_out, landed, sea_out,
    source, st, hh, cf, bl, cm, got, tb, send, recv,
    in_sem, out_sem, csem, gsem, ssem, rsem,
):
    def fetch(s, i):
        part = pl.ds(i * CHUNK, CHUNK)
        return pltpu.make_async_copy(state.at[s, part], st.at[s, part], in_sem.at[s, i])

    def put(s, r):
        part = pl.ds(r * BAND, BAND)
        return pltpu.make_async_copy(
            st.at[s, :, part], state_out.at[s, :, part], out_sem.at[s, r]
        )

    for s in range(2):
        for i in range(LV // CHUNK):
            fetch(s, i).start()

    w, g, ws, gs = around()
    me = w * NG + g
    barrier = greet_all(ws, gs)

    scale = LV / (Z_TOP - Z_BOTTOM)
    lane = lax.broadcasted_iota(jnp.int32, (SIDE, SIDE), 1)
    sub = lax.broadcasted_iota(jnp.int32, (SIDE, SIDE), 0)

    def up(m, sel, spread_rows):
        wide = jnp.dot(m, sel, preferred_element_type=F32).astype(BF16)
        return jnp.dot(spread_rows, wide, preferred_element_type=F32)

    def faces(a, axis, index):
        after = jnp.where(index == SIDE - 1, a, pltpu.roll(a, SIDE - 1, axis))
        before = jnp.where(index == 0, a, pltpu.roll(a, 1, axis))
        return (0.5 * COURANT) * (a + after), (0.5 * COURANT) * (before + a)

    edge = jnp.zeros((LV, PAD, SIDE), F32)
    for s in range(2):
        vel = foot[s, 0:4].reshape(64, L)
        hgt = foot[s, 4:6].reshape(32, L)
        height = up(hgt, pick[0], halves[0]) + up(hgt, pick[1], halves[1])
        ax = up(vel, pick[0], rows[...])
        ay = up(vel, pick[1], rows[...])
        hh[s] = height * scale - Z_BOTTOM * scale
        center = jnp.zeros((SIDE, SIDE), F32)
        for n, (a, axis, index) in enumerate(((ax, 1, lane), (ay, 0, sub))):
            upper, lower = faces(a, axis, index)
            center += jnp.maximum(upper, 0.0) - jnp.minimum(lower, 0.0)
            from_up = jnp.minimum(upper, 0.0)
            from_low = -jnp.maximum(lower, 0.0)
            last, first = index == SIDE - 1, index == 0
            center += jnp.where(last, from_up, 0.0) + jnp.where(first, from_low, 0.0)
            cf[s, 1 + 2 * n] = jnp.where(last, 0.0, from_up)
            cf[s, 2 + 2 * n] = jnp.where(first, 0.0, from_low)
        cf[s, 0] = center
        bl[s, :, 0:PAD, :] = edge
        bl[s, :, PAD + SIDE:, :] = edge

    for q in range(NG):
        want = (2 * w + g // 4) * 32 + 4 * q
        at = rank_of(tiles, q, want)
        for c in range(4):
            found = tiles[q * 32 + at]
            source[0, 4 * q + c] = jnp.bitwise_and(at, NW - 1) * NG + q
            source[1, 4 * q + c] = lax.shift_right_logical(at, 4)
            source[2, 4 * q + c] = jnp.where(found == want + c, 1, 0)
            at = jnp.minimum(at + jnp.where(found <= want + c, 1, 0), 31)

    for s in range(2):
        for i in range(LV // CHUNK):
            fetch(s, i).wait()

            def blend(o, carry, s=s, i=i):
                for b in range(SIDE // RB):
                    rs = slice(b * RB, (b + 1) * RB)
                    h, wt = hh[s, rs, :], weight[rs, :]
                    keep = 1.0 - wt
                    for l in range(TOGETHER):
                        k = i * CHUNK + o * TOGETHER + l
                        under = jnp.clip(h - lax.convert_element_type(k, F32), 0.0, 1.0)
                        bl[s, k, PAD + b * RB:PAD + (b + 1) * RB, :] = (
                            wt * under + keep * st[s, k, rs, :].astype(F32)
                        )
                return carry

            lax.fori_loop(0, CHUNK // TOGETHER, blend, 0)

    high = lax.Precision.HIGHEST
    for r in range(SIDE // BAND):
        block = jnp.zeros((R, L), F32)
        for s in range(2):

            def move(o, accs, s=s, r=r):
                accs = list(accs)
                for n in range(BAND // RB):
                    first_row = r * BAND + n * RB
                    rs = slice(first_row, first_row + RB)
                    at = PAD + first_row
                    c0, c1, c2, c3, c4 = (cf[s, m, rs, :] for m in range(5))
                    for l in range(TOGETHER):
                        k = o * TOGETHER + l
                        mid = bl[s, k, at:at + RB, :]
                        nxt = bl[s, k, at + 1:at + 1 + RB, :]
                        prv = bl[s, k, at - 1:at - 1 + RB, :]
                        flow = c0 * mid + c1 * pltpu.roll(mid, SIDE - 1, 1)
                        flow = flow + c2 * pltpu.roll(mid, 1, 1) + c3 * nxt + c4 * prv
                        new = jnp.clip(mid - prof[k] * flow, 0.0, 1.0)
                        st[s, k, rs, :] = new.astype(BF16)
                        accs[n] = accs[n] + new
                return tuple(accs)

            none = jnp.zeros((RB, SIDE), F32)
            accs = lax.fori_loop(0, LV // TOGETHER, move, (none,) * (BAND // RB))
            put(s, r).start()
            column = jnp.concatenate(accs, axis=0) * (1.0 / scale) + Z_BOTTOM
            part = jnp.dot(down_rows[...], column, preferred_element_type=F32, precision=high)
            block += jnp.dot(part, down_cols[s], preferred_element_type=F32, precision=high)
        cm[r] = (0.25 * block).astype(BF16)

        if r == 0:
            pl.semaphore_wait(barrier, D - 1)
        for to in (r, r + 4):
            for kw in WIDE_STEPS + [0]:

                def post(to=to, kw=kw, r=r):
                    pltpu.make_async_remote_copy(
                        cm.at[r], got.at[me], csem, gsem,
                        device_id=(ws[kw], to), device_id_type=MESH,
                    ).start()

                if kw:
                    post()
                else:
                    pl.when(g != to)(post)

                    @pl.when(g == to)
                    def _(r=r):
                        pltpu.make_async_copy(cm.at[r], got.at[me], gsem).start()

    pltpu.make_async_copy(got, got, gsem).wait()

    lane = lane_iota(R)
    low = lane < 64
    x = []
    for k2 in range(16):
        sides = []
        for h in range(2):
            cc = 2 * k2 + h
            tile = got[source[0, cc]].astype(F32)
            same = (lane * 0 + source[1, cc]) == h
            sides.append(jnp.where(same, tile, pltpu.roll(tile, 64, 1)))
        there = jnp.where(low, source[2, 2 * k2], source[2, 2 * k2 + 1]) == 1
        ht = phys[k2 * R:(k2 + 1) * R, :]
        vx = phys[256 + k2 * R:256 + (k2 + 1) * R, :]
        vy = phys[512 + k2 * R:512 + (k2 + 1) * R, :]
        sea = jnp.where(there, jnp.where(low, sides[0], sides[1]), ht)
        sea_out[:, k2 * L:(k2 + 1) * L] = sea
        x.append((-(sea + 0.5 * (vx * vx + vy * vy)), jnp.zeros((R, L), F32)))
    y = sixteenth(x, -1)
    for k1 in range(16):
        c, s = tw_c[k1:k1 + 1, :], tw_s[k1:k1 + 1, :]
        a, b = y[k1]
        re = (a * c - b * s).astype(BF16)
        im = (a * s + b * c).astype(BF16)
        q, e = k1 // 4, k1 % 4
        up_rows = slice(e * R, (e + 1) * R)
        dn_rows = slice(64 + e * R, 64 + (e + 1) * R)
        tb[q, up_rows, 0:L] = re
        tb[q, up_rows, L:2 * L] = -im
        tb[q, dn_rows, 0:L] = im
        tb[q, dn_rows, L:2 * L] = re

    for q in range(2):
        rhs = tb[2 * q:2 * q + 2].reshape(2 * L, 2 * L)
        z = nt_dot(spread[...], rhs)
        send[:, 2 * q, :] = z[:, :L]
        send[:, 2 * q + 1, :] = z[:, L:]

    spread_all(send, recv, ssem, rsem, ws, gs)
    for q in range(4):
        landed[q] = recv[:, q, :].astype(BF16)

    sent(got, D - 1, csem)
    sent(send, D - 1, ssem)
    for s in range(2):
        for r in range(SIDE // BAND):
            put(s, r).wait()


def settle_kernel(
    landed, sea, state, gather, bt_c, bt_s, finish,
    surface, state_out, tendency,
    out32, held, in_sem, out_sem,
):
    def copy(i, source, target, sem):
        s, part = i // 4, pl.ds((i % 4) * CHUNK, CHUNK)
        return pltpu.make_async_copy(source.at[s, part], target.at[s, part], sem.at[i])

    for i in range(8):
        copy(i, state, held, in_sem).start()
    surface[...] = sea[...]

    for i in range(8):
        copy(i, state, held, in_sem).wait()
        copy(i, held, state_out, out_sem).start()

    flip = jnp.where(lane_iota(D) < 64, -1.0, 1.0).astype(F32)
    for q in range(2):
        xx = jnp.concatenate([landed[2 * q], landed[2 * q + 1]], axis=1)
        t = blocks_in(xx, gather[...], bt_c[...], bt_s[...], flip)
        done = nt_dot(finish[...], t) * (1.0 / N)
        for h in range(2):
            for c in range(2):
                for e in range(4):
                    r0 = (c * 4 + e) * R
                    out32[pl.ds(c * 256 + 8 * q + 4 * h + e, R, stride=R), :] = done[
                        r0:r0 + R, h * L:(h + 1) * L
                    ]
    for c in range(2):
        for k2 in range(16):
            at = c * 256 + k2 * R
            tendency[c, :, k2 * L:(k2 + 1) * L] = out32[at:at + R, :]

    for i in range(8):
        copy(i, held, state_out, out_sem).wait()


def vmem(n):
    return [pl.BlockSpec(memory_space=pltpu.VMEM)] * n


def shards(eta_hat, phi_hat, patch_tiles, fraction):
    smem = pl.BlockSpec(memory_space=pltpu.SMEM)
    dma = pltpu.SemaphoreType.DMA
    phys, foot = pl.pallas_call(
        rise_kernel,
        out_shape=(
            jax.ShapeDtypeStruct((48 * R, L), F32),
            jax.ShapeDtypeStruct((2, 6, R, L), BF16),
        ),
        in_specs=[smem] + vmem(9),
        out_specs=tuple(vmem(2)),
        scratch_shapes=[
            pltpu.VMEM((16, L, 2 * L), BF16),
            pltpu.VMEM((D * R, L), F32),
            pltpu.VMEM((D, R, L), BF16),
            pltpu.VMEM((D, R, L), BF16),
            pltpu.VMEM((NG, 6, R, L), BF16),
            pltpu.VMEM((NG, 6, R, L), BF16),
            pltpu.VMEM((NW, 6, R, L), BF16),
            pltpu.VMEM((NW, 6, R, L), BF16),
        ] + [dma] * 6,
        compiler_params=pltpu.CompilerParams(
            collective_id=1, has_side_effects=True, vmem_limit_bytes=VMEM_LIMIT
        ),
        name="rise",
    )(patch_tiles, eta_hat, phi_hat, *lane_tables(1), *block_tables(1, 3, False))

    prof, weight, pick, rows, halves = patch_tables()
    down_rows = jnp.swapaxes(rows[:BAND, :R], 0, 1).astype(F32)
    down_cols = jnp.swapaxes(pick, 1, 2).astype(F32)
    anywhere = pl.BlockSpec(memory_space=pl.ANY)
    new_state, landed, sea = pl.pallas_call(
        fall_kernel,
        out_shape=(
            jax.ShapeDtypeStruct((2, LV, SIDE, SIDE), BF16),
            jax.ShapeDtypeStruct((4, D, L), BF16),
            jax.ShapeDtypeStruct((R, N), F32),
        ),
        in_specs=[smem, smem] + vmem(2) + [anywhere] + vmem(9),
        out_specs=(anywhere,) + tuple(vmem(2)),
        scratch_shapes=[
            pltpu.SMEM((3, 32), jnp.int32),
            pltpu.VMEM((2, LV, SIDE, SIDE), BF16),
            pltpu.VMEM((2, SIDE, SIDE), F32),
            pltpu.VMEM((2, 5, SIDE, SIDE), F32),
            pltpu.VMEM((2, LV, SIDE + 2 * PAD, SIDE), F32),
            pltpu.VMEM((4, R, L), BF16),
            pltpu.VMEM((D, R, L), BF16),
            pltpu.VMEM((4, L, 2 * L), BF16),
            pltpu.VMEM((D, 4, L), F32),
            pltpu.VMEM((D, 4, L), F32),
            dma((2, LV // CHUNK)),
            dma((2, SIDE // BAND)),
        ] + [dma] * 4,
        compiler_params=pltpu.CompilerParams(
            collective_id=2, has_side_effects=True, vmem_limit_bytes=VMEM_LIMIT
        ),
        name="fall",
    )(
        patch_tiles, prof, phys, foot, fraction[:, 0], weight, pick, rows, halves,
        down_rows, down_cols, *lane_tables(-1),
    )

    surface, new_state, tendency = pl.pallas_call(
        settle_kernel,
        out_shape=(
            jax.ShapeDtypeStruct((R, N), F32),
            jax.ShapeDtypeStruct((2, LV, SIDE, SIDE), BF16),
            jax.ShapeDtypeStruct((2, R, N), F32),
        ),
        in_specs=vmem(2) + [anywhere] + vmem(4),
        out_specs=(vmem(1)[0], anywhere, vmem(1)[0]),
        scratch_shapes=[
            pltpu.VMEM((512, L), F32),
            pltpu.VMEM((2, LV, SIDE, SIDE), BF16),
            dma((8,)),
            dma((8,)),
        ],
        compiler_params=pltpu.CompilerParams(vmem_limit_bytes=VMEM_LIMIT),
        name="settle",
    )(landed, sea, new_state, *block_tables(-1, 4, True))
    return (surface, new_state[:, None], tendency)


def solution(mesh):
    placed = (
        P(None, ("wide", "grp"), None),
        P(None, ("wide", "grp"), None),
        P(),
        P(None, ("wide", "grp"), None, None, None),
    )
    return jax.shard_map(
        shards,
        mesh=mesh,
        in_specs=placed,
        out_specs=(
            P(("wide", "grp"), None),
            P(None, ("wide", "grp"), None, None, None),
            P(None, ("wide", "grp"), None),
        ),
        check_vma=False,
    )
```

```python
import functools
import math

import jax
import jax.numpy as jnp
import numpy as np
from jax import lax
from jax.experimental import pallas as pl
from jax.experimental.pallas import tpu as pltpu
from jax.sharding import PartitionSpec as P

F32 = jnp.float32
BF16 = jnp.bfloat16
MESH = pl.DeviceIdType.MESH

N = 2048
D = 128
NW = 16
NG = 8
L = 128
R = 16
LV = 64
SIDE = 128
TS = 64
Z_BOTTOM = -2.0
Z_TOP = 2.0
DECAY_RATE = 0.5
COURANT = 0.3
VMEM_LIMIT = 56 << 20


def unit(phase, length):
    angle = (phase % length) * (2.0 * math.pi / length)
    return np.cos(angle), np.sin(angle)


def lane_tables(sign):
    k1 = np.arange(R)[:, None]
    n2 = np.arange(L)[None, :]
    tc, ts = unit(k1 * n2, N)
    k2 = np.arange(D)[:, None]
    c, s = unit(k2 * n2, D)
    spread = np.concatenate([c, sign * s], axis=1)
    return (
        jnp.asarray(tc, F32),
        jnp.asarray(sign * ts, F32),
        jnp.asarray(spread, F32).astype(BF16),
    )


def block_tables(sign, blocks, full):
    k1 = np.arange(D)[:, None]
    src = np.arange(D)[None, :]
    c, s = unit(k1 * src, D)
    gather = np.concatenate([c, sign * s], axis=0)
    j = np.tile(np.arange(R), 8)[None, :]
    tc, ts = unit(k1 * j, N)
    k2 = np.arange(R)[:, None]
    jj = np.arange(R)[None, :]
    cc, ss = unit(k2 * jj, R)
    ss = sign * ss
    rows = []
    for part in range(2 if full else 1):
        for e in range(blocks):
            out = np.zeros((R, 2, 4, R))
            out[:, 0, e, :] = cc if part == 0 else ss
            out[:, 1, e, :] = -ss if part == 0 else cc
            rows.append(out.reshape(R, L))
    finish = np.concatenate(rows, axis=0)
    return (
        jnp.asarray(gather, F32).astype(BF16),
        jnp.asarray(tc, F32),
        jnp.asarray(sign * ts, F32),
        jnp.asarray(finish, F32).astype(BF16),
    )


def fourth(x, sign):
    (ar, ai), (br, bi), (cr, ci), (dr, di) = x
    t0r, t0i, t1r, t1i = ar + cr, ai + ci, ar - cr, ai - ci
    t2r, t2i, t3r, t3i = br + dr, bi + di, br - dr, bi - di
    if sign < 0:
        t3r, t3i = -t3r, -t3i
    return (
        (t0r + t2r, t0i + t2i),
        (t1r - t3i, t1i + t3r),
        (t0r - t2r, t0i - t2i),
        (t1r + t3i, t1i - t3r),
    )


def times(x, re, im):
    if abs(im) < 1e-12 and abs(re - 1.0) < 1e-12:
        return x
    a, b = x
    return (a * re - b * im, a * im + b * re)


def sixteenth(x, sign):
    inner = []
    for b in range(4):
        y = fourth([x[4 * a + b] for a in range(4)], sign)
        turned = []
        for c in range(4):
            angle = sign * 2.0 * math.pi * b * c / 16
            turned.append(times(y[c], math.cos(angle), math.sin(angle)))
        inner.append(turned)
    out = [None] * 16
    for c in range(4):
        z = fourth([inner[b][c] for b in range(4)], sign)
        for d in range(4):
            out[c + 4 * d] = z[d]
    return out


def nt_dot(a, b):
    return lax.dot_general(a, b, (((1,), (1,)), ((), ())), preferred_element_type=F32)


def blocks_in(x, gather, tc, ts, flip):
    both = jnp.dot(gather, x, preferred_element_type=F32)
    parts = []
    for h in range(2):
        a = both[:D, h * L:(h + 1) * L]
        b = both[D:, h * L:(h + 1) * L]
        u = a * tc - b * ts
        v = b * tc + a * ts
        parts.append((u + flip * pltpu.roll(v, 64, 1)).astype(BF16))
    return jnp.concatenate(parts, axis=0)


def lane_iota(rows):
    return lax.broadcasted_iota(jnp.int32, (rows, L), 1)


def hops(step):
    return min(step, 4 - step)


def far(kw, kg):
    return hops(kw // 4) + hops(kw % 4) + hops(kg // 2) + 0.5 * (kg % 2)


WIDE_STEPS = sorted(range(1, NW), key=lambda k: -far(k, 0))
GRP_STEPS = sorted(range(1, NG), key=lambda k: -far(0, k))
ALL_STEPS = sorted(
    [(kw, kg) for kw in range(NW) for kg in range(NG) if kw or kg], key=lambda k: -far(*k)
)


def around():
    w = lax.axis_index("wide")
    g = lax.axis_index("grp")
    y = [lax.rem(w // 4 + k, 4) for k in range(4)]
    z = [lax.rem(w % 4 + k, 4) for k in range(4)]
    x = [lax.rem(g // 2 + k, 4) for k in range(4)]
    c = [g % 2, 1 - g % 2]
    ws = [y[k // 4] * 4 + z[k % 4] for k in range(NW)]
    gs = [x[k // 2] * 2 + c[k % 2] for k in range(NG)]
    return w, g, ws, gs


def greet_all(ws, gs):
    barrier = pltpu.get_barrier_semaphore()
    for kw, kg in ALL_STEPS:
        pl.semaphore_signal(
            barrier, inc=1, device_id=(ws[kw], gs[kg]), device_id_type=MESH
        )
    return barrier


def spread_all(send, recv, ssem, rsem, ws, gs):
    me = ws[0] * NG + gs[0]
    pltpu.make_async_copy(send.at[me], recv.at[me], rsem).start()
    for kw, kg in ALL_STEPS:
        pltpu.make_async_remote_copy(
            send.at[ws[kw] * NG + gs[kg]], recv.at[me], ssem, rsem,
            device_id=(ws[kw], gs[kg]), device_id_type=MESH,
        ).start()


def spread_grp(send, recv, ssem, rsem, ws, gs):
    pltpu.make_async_copy(send.at[gs[0]], recv.at[gs[0]], rsem).start()
    for k in GRP_STEPS:
        pltpu.make_async_remote_copy(
            send.at[gs[k]], recv.at[gs[0]], ssem, rsem,
            device_id=(ws[0], gs[k]), device_id_type=MESH,
        ).start()


def spread_wide(send, recv, ssem, rsem, ws, gs):
    pltpu.make_async_copy(send.at[ws[0]], recv.at[ws[0]], rsem).start()
    for k in WIDE_STEPS:
        pltpu.make_async_remote_copy(
            send.at[ws[k]], recv.at[ws[0]], ssem, rsem,
            device_id=(ws[k], gs[0]), device_id_type=MESH,
        ).start()


def landed_all(buf, sem):
    pltpu.make_async_copy(buf, buf, sem).wait()


def sent(buf, n, sem):
    pltpu.make_async_copy(buf.at[pl.ds(0, n)], buf.at[pl.ds(0, n)], sem).wait()


def patch_tables():
    pos = np.arange(SIDE)
    edge = np.minimum(pos, SIDE - 1 - pos)
    dist = np.minimum(edge[:, None], edge[None, :])
    weight = 0.3 + 0.7 * np.exp(-8.0 * dist / SIDE)
    x = np.arange(SIDE)
    pick = np.zeros((2, L, SIDE))
    for h in range(2):
        pick[h, 64 * h + x // 2, x] = 1.0
    rows = np.zeros((SIDE, TS))
    rows[x, x // 2] = 1.0
    halves = np.zeros((2, SIDE, 32))
    for i in range(SIDE):
        r = i // 2
        blk, within = r // 16, r % 16
        halves[blk % 2, i, (blk // 2) * 16 + within] = 1.0
    z = Z_BOTTOM + (np.arange(LV) + 0.5) * ((Z_TOP - Z_BOTTOM) / LV)
    prof = np.exp(DECAY_RATE * (z - Z_TOP))
    return (
        jnp.asarray(prof, F32),
        jnp.asarray(weight, F32),
        jnp.asarray(pick, F32).astype(BF16),
        jnp.asarray(rows, F32).astype(BF16),
        jnp.asarray(halves, F32).astype(BF16),
    )


RB = 16
PAD = 8
CHUNK = 16
TOGETHER = 8
BAND = 32


def rank_of(tiles, q, want):
    at = jnp.int32(0)
    for step in (16, 8, 4, 2, 1):
        at = at + jnp.where(tiles[q * 32 + at + step - 1] < want, step, 0)
    return at


def step_kernel(
    tiles, prof, eta, phi, state, weight, pick, rows, halves, down_rows, down_cols,
    up_c, up_s, up_spread, gather, bt_c, bt_s, finish, tw_c, tw_s, spread,
    state_out, landed, sea_out,
    source, tb_a, wide32, send_a, recv_a, phys,
    send1h, recv1h, send1v, recv1v, send2h, recv2h, send2v, recv2v,
    st, hh, cf, bl, cm, got, tb, send, recv,
    in_sem, out_sem, asem, arsem, ssem1h, rsem1h, ssem1v, rsem1v,
    ssem2h, rsem2h, ssem2v, rsem2v, csem, gsem, ssem, rsem,
):
    def fetch(s, i):
        part = pl.ds(i * CHUNK, CHUNK)
        return pltpu.make_async_copy(state.at[s, part], st.at[s, part], in_sem.at[s, i])

    def put(s, r):
        part = pl.ds(r * BAND, BAND)
        return pltpu.make_async_copy(
            st.at[s, :, part], state_out.at[s, :, part], out_sem.at[s, r]
        )

    w, g, ws, gs = around()
    me = w * NG + g
    barrier = greet_all(ws, gs)
    for s in range(2):
        for i in range(LV // CHUNK):
            fetch(s, i).start()

    row = lax.broadcasted_iota(jnp.int32, (R, L), 0)
    lane = lane_iota(R)
    kx = me * R + row
    kx = jnp.where(kx >= N // 2, kx - N, kx).astype(F32) * (2.0 * math.pi / N)

    for f in range(3):
        x = []
        for n1 in range(16):
            cols = slice(n1 * L, (n1 + 1) * L)
            if f == 0:
                x.append((eta[0, :, cols].astype(F32), eta[1, :, cols].astype(F32)))
            else:
                if f == 1:
                    k = kx
                else:
                    base = n1 * L if n1 < 8 else n1 * L - N
                    k = (lane + base).astype(F32) * (2.0 * math.pi / N)
                x.append((-k * phi[1, :, cols].astype(F32), k * phi[0, :, cols].astype(F32)))
        y = sixteenth(x, 1)
        for k1 in range(16):
            c, s = up_c[k1:k1 + 1, :], up_s[k1:k1 + 1, :]
            a, b = y[k1]
            re = (a * c - b * s).astype(BF16)
            im = (a * s + b * c).astype(BF16)
            up = slice(f * R, (f + 1) * R)
            dn = slice(64 + f * R, 64 + (f + 1) * R)
            tb_a[k1, up, 0:L] = re
            tb_a[k1, up, L:2 * L] = -im
            tb_a[k1, dn, 0:L] = im
            tb_a[k1, dn, L:2 * L] = re

    zero = jnp.zeros((R, 2 * L), BF16)

    def rows_out(kk, carry):
        for h in range(2):
            tb_a[2 * kk + h, 48:64, :] = zero
            tb_a[2 * kk + h, 112:128, :] = zero
        rhs = tb_a[pl.ds(2 * kk, 2)].reshape(2 * L, 2 * L)
        z = nt_dot(up_spread[...], rhs)
        wide32[pl.ds(2 * kk, D, stride=R), :] = z[:, :L]
        wide32[pl.ds(2 * kk + 1, D, stride=R), :] = z[:, L:]
        return carry

    lax.fori_loop(0, 8, rows_out, 0, unroll=2)

    def narrow(i, carry):
        part = wide32[pl.ds(pl.multiple_of(i * 128, 128), 128), :]
        send_a[pl.ds(i * 8, 8)] = part.reshape(8, R, L).astype(BF16)
        return carry

    lax.fori_loop(0, 16, narrow, 0)

    pl.semaphore_wait(barrier, D - 1)
    spread_all(send_a, recv_a, asem, arsem, ws, gs)

    for q in range(NG):
        want = (2 * w + g // 4) * 32 + 4 * q
        at = rank_of(tiles, q, want)
        for c in range(4):
            found = tiles[q * 32 + at]
            source[0, 4 * q + c] = jnp.bitwise_and(at, NW - 1) * NG + q
            source[1, 4 * q + c] = lax.shift_right_logical(at, 4)
            source[2, 4 * q + c] = jnp.where(found == want + c, 1, 0)
            at = jnp.minimum(at + jnp.where(found <= want + c, 1, 0), 31)

    edge = jnp.zeros((LV, PAD, SIDE), F32)
    for s in range(2):
        bl[s, :, 0:PAD, :] = edge
        bl[s, :, PAD + SIDE:, :] = edge
        for i in range(LV // CHUNK):
            fetch(s, i).wait()

        def share(o, carry, s=s):
            for b in range(SIDE // RB):
                rs = slice(b * RB, (b + 1) * RB)
                keep = 1.0 - weight[rs, :]
                for l in range(TOGETHER):
                    k = o * TOGETHER + l
                    bl[s, k, PAD + b * RB:PAD + (b + 1) * RB, :] = (
                        keep * st[s, k, rs, :].astype(F32)
                    )
            return carry

        lax.fori_loop(0, LV // TOGETHER, share, 0)

    landed_all(recv_a, arsem)

    def widen(i, carry):
        part = recv_a[pl.ds(i * 8, 8)].astype(F32)
        wide32[pl.ds(pl.multiple_of(i * 128, 128), 128), :] = part.reshape(128, L)
        return carry

    lax.fori_loop(0, 16, widen, 0)

    flip = jnp.where(lane_iota(D) < 64, -1.0, 1.0).astype(F32)

    def columns(yy, carry):
        x = jnp.concatenate(
            [
                wide32[pl.ds(2 * yy, D, stride=R), :].astype(BF16),
                wide32[pl.ds(2 * yy + 1, D, stride=R), :].astype(BF16),
            ],
            axis=1,
        )
        t = blocks_in(x, gather[...], bt_c[...], bt_s[...], flip)
        out = nt_dot(finish[...], t)
        phys[pl.ds(2 * yy, 48, stride=R), :] = out[:, :L]
        phys[pl.ds(2 * yy + 1, 48, stride=R), :] = out[:, L:]
        return carry

    lax.fori_loop(0, 8, columns, 0, unroll=4)

    low = lane < 64

    def heights(q, carry):
        for h in range(2):
            at = pl.multiple_of((2 * q + h) * R, R)
            send1h[q, h] = phys[pl.ds(at, R), :].astype(BF16)
        return carry

    lax.fori_loop(0, NG, heights, 0, unroll=4)
    spread_grp(send1h, recv1h, ssem1h, rsem1h, ws, gs)

    def speeds(q, carry):
        for h in range(2):
            vx = phys[pl.ds(pl.multiple_of((16 + 2 * q + h) * R, R), R), :]
            vy = phys[pl.ds(pl.multiple_of((32 + 2 * q + h) * R, R), R), :]
            send1v[q, 2 * h] = jnp.where(low, vx, pltpu.roll(vy, 64, 1)).astype(BF16)
            send1v[q, 2 * h + 1] = jnp.where(low, pltpu.roll(vx, 64, 1), vy).astype(BF16)
        return carry

    lax.fori_loop(0, NG, speeds, 0, unroll=2)
    spread_grp(send1v, recv1v, ssem1v, rsem1v, ws, gs)

    def tile_for(d):
        t0 = tiles[g * 32 + d]
        t1 = tiles[g * 32 + 16 + d]
        t = jnp.where(lax.shift_right_logical(t0, 6) == w, t0, t1)
        return jnp.bitwise_and(lax.shift_right_logical(t, 5), 1) * 4, jnp.bitwise_and(t, 3)

    landed_all(recv1h, rsem1h)

    def choose_heights(d, carry):
        upper, col = tile_for(d)
        right = (lane * 0 + jnp.bitwise_and(col, 1)) == 1
        pair = lax.shift_right_logical(col, 1)
        for q in range(2):
            a = recv1h[upper + 2 * q, pair].astype(F32)
            b = recv1h[upper + 2 * q + 1, pair].astype(F32)
            lo = jnp.where(right, pltpu.roll(a, 64, 1), a)
            hi = jnp.where(right, b, pltpu.roll(b, 64, 1))
            send2h[d, q] = jnp.where(low, lo, hi).astype(BF16)
        return carry

    lax.fori_loop(0, NW, choose_heights, 0, unroll=4)
    spread_wide(send2h, recv2h, ssem2h, rsem2h, ws, gs)

    landed_all(recv1v, rsem1v)

    def choose_speeds(d, carry):
        upper, col = tile_for(d)
        for q in range(4):
            send2v[d, q] = recv1v[upper + q, col]
        return carry

    lax.fori_loop(0, NW, choose_speeds, 0, unroll=4)
    spread_wide(send2v, recv2v, ssem2v, rsem2v, ws, gs)

    bands = [
        jnp.bitwise_and(lax.shift_right_logical(tiles[g * 32 + s * 16 + w], 6), NW - 1)
        for s in range(2)
    ]
    scale = LV / (Z_TOP - Z_BOTTOM)

    def up(m, sel, spread_rows):
        wide = jnp.dot(m, sel, preferred_element_type=F32).astype(BF16)
        return jnp.dot(spread_rows, wide, preferred_element_type=F32)

    landed_all(recv2h, rsem2h)
    for s in range(2):
        hgt = recv2h[bands[s]].reshape(32, L)
        height = up(hgt, pick[0], halves[0]) + up(hgt, pick[1], halves[1])
        hh[s] = height * scale - Z_BOTTOM * scale

        def blend(o, carry, s=s):
            for b in range(SIDE // RB):
                rs = slice(b * RB, (b + 1) * RB)
                h, wt = hh[s, rs, :], weight[rs, :]
                for l in range(TOGETHER):
                    k = o * TOGETHER + l
                    under = jnp.clip(h - lax.convert_element_type(k, F32), 0.0, 1.0)
                    bl[s, k, PAD + b * RB:PAD + (b + 1) * RB, :] += wt * under
            return carry

        lax.fori_loop(0, LV // TOGETHER, blend, 0)

    across = lax.broadcasted_iota(jnp.int32, (SIDE, SIDE), 1)
    sub = lax.broadcasted_iota(jnp.int32, (SIDE, SIDE), 0)

    def faces(a, axis, index):
        after = jnp.where(index == SIDE - 1, a, pltpu.roll(a, SIDE - 1, axis))
        before = jnp.where(index == 0, a, pltpu.roll(a, 1, axis))
        return (0.5 * COURANT) * (a + after), (0.5 * COURANT) * (before + a)

    landed_all(recv2v, rsem2v)
    for s in range(2):
        vel = recv2v[bands[s]].reshape(64, L)
        ax = up(vel, pick[0], rows[...])
        ay = up(vel, pick[1], rows[...])
        center = jnp.zeros((SIDE, SIDE), F32)
        for n, (a, axis, index) in enumerate(((ax, 1, across), (ay, 0, sub))):
            upper, lower = faces(a, axis, index)
            center += jnp.maximum(upper, 0.0) - jnp.minimum(lower, 0.0)
            from_up = jnp.minimum(upper, 0.0)
            from_low = -jnp.maximum(lower, 0.0)
            last, first = index == SIDE - 1, index == 0
            center += jnp.where(last, from_up, 0.0) + jnp.where(first, from_low, 0.0)
            cf[s, 1 + 2 * n] = jnp.where(last, 0.0, from_up)
            cf[s, 2 + 2 * n] = jnp.where(first, 0.0, from_low)
        cf[s, 0] = center

    high = lax.Precision.HIGHEST
    for r in range(SIDE // BAND):
        block = jnp.zeros((R, L), F32)
        for s in range(2):

            def move(o, accs, s=s, r=r):
                accs = list(accs)
                for n in range(BAND // RB):
                    first_row = r * BAND + n * RB
                    rs = slice(first_row, first_row + RB)
                    at = PAD + first_row
                    c0, c1, c2, c3, c4 = (cf[s, m, rs, :] for m in range(5))
                    for l in range(TOGETHER):
                        k = o * TOGETHER + l
                        mid = bl[s, k, at:at + RB, :]
                        nxt = bl[s, k, at + 1:at + 1 + RB, :]
                        prv = bl[s, k, at - 1:at - 1 + RB, :]
                        flow = c0 * mid + c1 * pltpu.roll(mid, SIDE - 1, 1)
                        flow = flow + c2 * pltpu.roll(mid, 1, 1) + c3 * nxt + c4 * prv
                        new = jnp.clip(mid - prof[k] * flow, 0.0, 1.0)
                        st[s, k, rs, :] = new.astype(BF16)
                        accs[n] = accs[n] + new
                return tuple(accs)

            none = jnp.zeros((RB, SIDE), F32)
            accs = lax.fori_loop(0, LV // TOGETHER, move, (none,) * (BAND // RB))
            put(s, r).start()
            column = jnp.concatenate(accs, axis=0) * (1.0 / scale) + Z_BOTTOM
            part = jnp.dot(down_rows[...], column, preferred_element_type=F32, precision=high)
            block += jnp.dot(part, down_cols[s], preferred_element_type=F32, precision=high)
        cm[r] = (0.25 * block).astype(BF16)

        for to in (r, r + 4):
            for kw in WIDE_STEPS + [0]:

                def post(to=to, kw=kw, r=r):
                    pltpu.make_async_remote_copy(
                        cm.at[r], got.at[me], csem, gsem,
                        device_id=(ws[kw], to), device_id_type=MESH,
                    ).start()

                if kw:
                    post()
                else:
                    pl.when(g != to)(post)

                    @pl.when(g == to)
                    def _(r=r):
                        pltpu.make_async_copy(cm.at[r], got.at[me], gsem).start()

    landed_all(got, gsem)

    x = []
    for k2 in range(16):
        sides = []
        for h in range(2):
            cc = 2 * k2 + h
            tile = got[source[0, cc]].astype(F32)
            same = (lane * 0 + source[1, cc]) == h
            sides.append(jnp.where(same, tile, pltpu.roll(tile, 64, 1)))
        there = jnp.where(low, source[2, 2 * k2], source[2, 2 * k2 + 1]) == 1
        ht = phys[k2 * R:(k2 + 1) * R, :]
        vx = phys[256 + k2 * R:256 + (k2 + 1) * R, :]
        vy = phys[512 + k2 * R:512 + (k2 + 1) * R, :]
        sea = jnp.where(there, jnp.where(low, sides[0], sides[1]), ht)
        sea_out[:, k2 * L:(k2 + 1) * L] = sea
        x.append((-(sea + 0.5 * (vx * vx + vy * vy)), jnp.zeros((R, L), F32)))
    y = sixteenth(x, -1)
    for k1 in range(16):
        c, s = tw_c[k1:k1 + 1, :], tw_s[k1:k1 + 1, :]
        a, b = y[k1]
        re = (a * c - b * s).astype(BF16)
        im = (a * s + b * c).astype(BF16)
        q, e = k1 // 4, k1 % 4
        up_rows = slice(e * R, (e + 1) * R)
        dn_rows = slice(64 + e * R, 64 + (e + 1) * R)
        tb[q, up_rows, 0:L] = re
        tb[q, up_rows, L:2 * L] = -im
        tb[q, dn_rows, 0:L] = im
        tb[q, dn_rows, L:2 * L] = re

    for q in range(2):
        rhs = tb[2 * q:2 * q + 2].reshape(2 * L, 2 * L)
        z = nt_dot(spread[...], rhs)
        send[:, 2 * q, :] = z[:, :L]
        send[:, 2 * q + 1, :] = z[:, L:]

    spread_all(send, recv, ssem, rsem, ws, gs)
    landed_all(recv, rsem)
    for q in range(4):
        landed[q] = recv[:, q, :].astype(BF16)

    sent(send_a, D - 1, asem)
    sent(send1h, NG - 1, ssem1h)
    sent(send1v, NG - 1, ssem1v)
    sent(send2h, NW - 1, ssem2h)
    sent(send2v, NW - 1, ssem2v)
    sent(got, D - 1, csem)
    sent(send, D - 1, ssem)
    for s in range(2):
        for r in range(SIDE // BAND):
            put(s, r).wait()


def settle_kernel(
    landed, sea, state, gather, bt_c, bt_s, finish,
    surface, state_out, tendency,
    out32, held, in_sem, out_sem,
):
    def copy(i, source, target, sem):
        s, part = i // 4, pl.ds((i % 4) * CHUNK, CHUNK)
        return pltpu.make_async_copy(source.at[s, part], target.at[s, part], sem.at[i])

    for i in range(8):
        copy(i, state, held, in_sem).start()
    surface[...] = sea[...]

    flip = jnp.where(lane_iota(D) < 64, -1.0, 1.0).astype(F32)
    for q in range(2):
        xx = jnp.concatenate([landed[2 * q], landed[2 * q + 1]], axis=1)
        t = blocks_in(xx, gather[...], bt_c[...], bt_s[...], flip)
        done = nt_dot(finish[...], t) * (1.0 / N)
        for h in range(2):
            for c in range(2):
                for e in range(4):
                    r0 = (c * 4 + e) * R
                    out32[pl.ds(c * 256 + 8 * q + 4 * h + e, R, stride=R), :] = done[
                        r0:r0 + R, h * L:(h + 1) * L
                    ]
        for i in range(4 * q, 4 * q + 4):
            copy(i, state, held, in_sem).wait()
            copy(i, held, state_out, out_sem).start()
    for c in range(2):
        for k2 in range(16):
            at = c * 256 + k2 * R
            tendency[c, :, k2 * L:(k2 + 1) * L] = out32[at:at + R, :]

    for i in range(8):
        copy(i, held, state_out, out_sem).wait()


def vmem(n):
    return [pl.BlockSpec(memory_space=pltpu.VMEM)] * n


def shards(eta_hat, phi_hat, patch_tiles, fraction):
    smem = pl.BlockSpec(memory_space=pltpu.SMEM)
    dma = pltpu.SemaphoreType.DMA
    prof, weight, pick, rows, halves = patch_tables()
    down_rows = jnp.swapaxes(rows[:BAND, :R], 0, 1).astype(F32)
    down_cols = jnp.swapaxes(pick, 1, 2).astype(F32)
    anywhere = pl.BlockSpec(memory_space=pl.ANY)
    new_state, landed, sea = pl.pallas_call(
        step_kernel,
        out_shape=(
            jax.ShapeDtypeStruct((2, LV, SIDE, SIDE), BF16),
            jax.ShapeDtypeStruct((4, D, L), BF16),
            jax.ShapeDtypeStruct((R, N), F32),
        ),
        in_specs=[smem, smem] + vmem(2) + [anywhere] + vmem(16),
        out_specs=(anywhere,) + tuple(vmem(2)),
        scratch_shapes=[
            pltpu.SMEM((3, 32), jnp.int32),
            pltpu.VMEM((16, L, 2 * L), BF16),
            pltpu.VMEM((D * R, L), F32),
            pltpu.VMEM((D, R, L), BF16),
            pltpu.VMEM((D, R, L), BF16),
            pltpu.VMEM((48 * R, L), F32),
            pltpu.VMEM((NG, 2, R, L), BF16),
            pltpu.VMEM((NG, 2, R, L), BF16),
            pltpu.VMEM((NG, 4, R, L), BF16),
            pltpu.VMEM((NG, 4, R, L), BF16),
            pltpu.VMEM((NW, 2, R, L), BF16),
            pltpu.VMEM((NW, 2, R, L), BF16),
            pltpu.VMEM((NW, 4, R, L), BF16),
            pltpu.VMEM((NW, 4, R, L), BF16),
            pltpu.VMEM((2, LV, SIDE, SIDE), BF16),
            pltpu.VMEM((2, SIDE, SIDE), F32),
            pltpu.VMEM((2, 5, SIDE, SIDE), F32),
            pltpu.VMEM((2, LV, SIDE + 2 * PAD, SIDE), F32),
            pltpu.VMEM((4, R, L), BF16),
            pltpu.VMEM((D, R, L), BF16),
            pltpu.VMEM((4, L, 2 * L), BF16),
            pltpu.VMEM((D, 4, L), F32),
            pltpu.VMEM((D, 4, L), F32),
            dma((2, LV // CHUNK)),
            dma((2, SIDE // BAND)),
        ] + [dma] * 14,
        compiler_params=pltpu.CompilerParams(
            collective_id=1, has_side_effects=True, vmem_limit_bytes=VMEM_LIMIT
        ),
        name="step",
    )(
        patch_tiles, prof, eta_hat, phi_hat, fraction[:, 0], weight, pick, rows, halves,
        down_rows, down_cols, *lane_tables(1), *block_tables(1, 3, False), *lane_tables(-1),
    )

    surface, new_state, tendency = pl.pallas_call(
        settle_kernel,
        out_shape=(
            jax.ShapeDtypeStruct((R, N), F32),
            jax.ShapeDtypeStruct((2, LV, SIDE, SIDE), BF16),
            jax.ShapeDtypeStruct((2, R, N), F32),
        ),
        in_specs=vmem(2) + [anywhere] + vmem(4),
        out_specs=(vmem(1)[0], anywhere, vmem(1)[0]),
        scratch_shapes=[
            pltpu.VMEM((512, L), F32),
            pltpu.VMEM((2, LV, SIDE, SIDE), BF16),
            dma((8,)),
            dma((8,)),
        ],
        compiler_params=pltpu.CompilerParams(vmem_limit_bytes=VMEM_LIMIT),
        name="settle",
    )(landed, sea, new_state, *block_tables(-1, 4, True))
    return (surface, new_state[:, None], tendency)


def solution(mesh):
    placed = (
        P(None, ("wide", "grp"), None),
        P(None, ("wide", "grp"), None),
        P(),
        P(None, ("wide", "grp"), None, None, None),
    )
    return jax.shard_map(
        shards,
        mesh=mesh,
        in_specs=placed,
        out_specs=(
            P(("wide", "grp"), None),
            P(None, ("wide", "grp"), None, None, None),
            P(None, ("wide", "grp"), None),
        ),
        check_vma=False,
    )
```

```python
import functools
import math

import jax
import jax.numpy as jnp
import numpy as np
from jax import lax
from jax.experimental import pallas as pl
from jax.experimental.pallas import tpu as pltpu
from jax.sharding import PartitionSpec as P

F32 = jnp.float32
BF16 = jnp.bfloat16
MESH = pl.DeviceIdType.MESH

N = 2048
D = 128
NW = 16
NG = 8
L = 128
R = 16
LV = 64
SIDE = 128
TS = 64
Z_BOTTOM = -2.0
Z_TOP = 2.0
DECAY_RATE = 0.5
COURANT = 0.3
VMEM_LIMIT = 56 << 20


def unit(phase, length):
    angle = (phase % length) * (2.0 * math.pi / length)
    return np.cos(angle), np.sin(angle)


def lane_tables(sign):
    k1 = np.arange(R)[:, None]
    n2 = np.arange(L)[None, :]
    tc, ts = unit(k1 * n2, N)
    k2 = np.arange(D)[:, None]
    c, s = unit(k2 * n2, D)
    spread = np.concatenate([c, sign * s], axis=1)
    return (
        jnp.asarray(tc, F32),
        jnp.asarray(sign * ts, F32),
        jnp.asarray(spread, F32).astype(BF16),
    )


def block_tables(sign, blocks, full):
    k1 = np.arange(D)[:, None]
    src = np.arange(D)[None, :]
    c, s = unit(k1 * src, D)
    gather = np.concatenate([c, sign * s], axis=0)
    j = np.tile(np.arange(R), 8)[None, :]
    tc, ts = unit(k1 * j, N)
    k2 = np.arange(R)[:, None]
    jj = np.arange(R)[None, :]
    cc, ss = unit(k2 * jj, R)
    ss = sign * ss
    rows = []
    for part in range(2 if full else 1):
        for e in range(blocks):
            out = np.zeros((R, 2, 4, R))
            out[:, 0, e, :] = cc if part == 0 else ss
            out[:, 1, e, :] = -ss if part == 0 else cc
            rows.append(out.reshape(R, L))
    finish = np.concatenate(rows, axis=0)
    return (
        jnp.asarray(gather, F32).astype(BF16),
        jnp.asarray(tc, F32),
        jnp.asarray(sign * ts, F32),
        jnp.asarray(finish, F32).astype(BF16),
    )


def fourth(x, sign):
    (ar, ai), (br, bi), (cr, ci), (dr, di) = x
    t0r, t0i, t1r, t1i = ar + cr, ai + ci, ar - cr, ai - ci
    t2r, t2i, t3r, t3i = br + dr, bi + di, br - dr, bi - di
    if sign < 0:
        t3r, t3i = -t3r, -t3i
    return (
        (t0r + t2r, t0i + t2i),
        (t1r - t3i, t1i + t3r),
        (t0r - t2r, t0i - t2i),
        (t1r + t3i, t1i - t3r),
    )


def times(x, re, im):
    if abs(im) < 1e-12 and abs(re - 1.0) < 1e-12:
        return x
    a, b = x
    return (a * re - b * im, a * im + b * re)


def sixteenth(x, sign):
    inner = []
    for b in range(4):
        y = fourth([x[4 * a + b] for a in range(4)], sign)
        turned = []
        for c in range(4):
            angle = sign * 2.0 * math.pi * b * c / 16
            turned.append(times(y[c], math.cos(angle), math.sin(angle)))
        inner.append(turned)
    out = [None] * 16
    for c in range(4):
        z = fourth([inner[b][c] for b in range(4)], sign)
        for d in range(4):
            out[c + 4 * d] = z[d]
    return out


def nt_dot(a, b):
    return lax.dot_general(a, b, (((1,), (1,)), ((), ())), preferred_element_type=F32)


def blocks_in(x, gather, tc, ts, flip):
    both = jnp.dot(gather, x, preferred_element_type=F32)
    parts = []
    for h in range(2):
        a = both[:D, h * L:(h + 1) * L]
        b = both[D:, h * L:(h + 1) * L]
        u = a * tc - b * ts
        v = b * tc + a * ts
        parts.append((u + flip * pltpu.roll(v, 64, 1)).astype(BF16))
    return jnp.concatenate(parts, axis=0)


def lane_iota(rows):
    return lax.broadcasted_iota(jnp.int32, (rows, L), 1)


def hops(step):
    return min(step, 4 - step)


def far(kw, kg):
    return hops(kw // 4) + hops(kw % 4) + hops(kg // 2) + 0.5 * (kg % 2)


WIDE_STEPS = sorted(range(1, NW), key=lambda k: -far(k, 0))
GRP_STEPS = sorted(range(1, NG), key=lambda k: -far(0, k))
ALL_STEPS = sorted(
    [(kw, kg) for kw in range(NW) for kg in range(NG) if kw or kg], key=lambda k: -far(*k)
)


def around():
    w = lax.axis_index("wide")
    g = lax.axis_index("grp")
    y = [lax.rem(w // 4 + k, 4) for k in range(4)]
    z = [lax.rem(w % 4 + k, 4) for k in range(4)]
    x = [lax.rem(g // 2 + k, 4) for k in range(4)]
    c = [g % 2, 1 - g % 2]
    ws = [y[k // 4] * 4 + z[k % 4] for k in range(NW)]
    gs = [x[k // 2] * 2 + c[k % 2] for k in range(NG)]
    return w, g, ws, gs


def greet_all(ws, gs):
    barrier = pltpu.get_barrier_semaphore()
    for kw, kg in ALL_STEPS:
        pl.semaphore_signal(
            barrier, inc=1, device_id=(ws[kw], gs[kg]), device_id_type=MESH
        )
    return barrier


def spread_all(send, recv, ssem, rsem, ws, gs):
    me = ws[0] * NG + gs[0]
    pltpu.make_async_copy(send.at[me], recv.at[me], rsem).start()
    for kw, kg in ALL_STEPS:
        pltpu.make_async_remote_copy(
            send.at[ws[kw] * NG + gs[kg]], recv.at[me], ssem, rsem,
            device_id=(ws[kw], gs[kg]), device_id_type=MESH,
        ).start()


def spread_grp(send, recv, ssem, rsem, ws, gs):
    pltpu.make_async_copy(send.at[gs[0]], recv.at[gs[0]], rsem).start()
    for k in GRP_STEPS:
        pltpu.make_async_remote_copy(
            send.at[gs[k]], recv.at[gs[0]], ssem, rsem,
            device_id=(ws[0], gs[k]), device_id_type=MESH,
        ).start()


def spread_wide(send, recv, ssem, rsem, ws, gs):
    pltpu.make_async_copy(send.at[ws[0]], recv.at[ws[0]], rsem).start()
    for k in WIDE_STEPS:
        pltpu.make_async_remote_copy(
            send.at[ws[k]], recv.at[ws[0]], ssem, rsem,
            device_id=(ws[k], gs[0]), device_id_type=MESH,
        ).start()


def landed_all(buf, sem):
    pltpu.make_async_copy(buf, buf, sem).wait()


def sent(buf, n, sem):
    pltpu.make_async_copy(buf.at[pl.ds(0, n)], buf.at[pl.ds(0, n)], sem).wait()


def patch_tables():
    pos = np.arange(SIDE)
    edge = np.minimum(pos, SIDE - 1 - pos)
    dist = np.minimum(edge[:, None], edge[None, :])
    weight = 0.3 + 0.7 * np.exp(-8.0 * dist / SIDE)
    x = np.arange(SIDE)
    pick = np.zeros((2, L, SIDE))
    for h in range(2):
        pick[h, 64 * h + x // 2, x] = 1.0
    rows = np.zeros((SIDE, TS))
    rows[x, x // 2] = 1.0
    halves = np.zeros((2, SIDE, 32))
    for i in range(SIDE):
        r = i // 2
        blk, within = r // 16, r % 16
        halves[blk % 2, i, (blk // 2) * 16 + within] = 1.0
    z = Z_BOTTOM + (np.arange(LV) + 0.5) * ((Z_TOP - Z_BOTTOM) / LV)
    prof = np.exp(DECAY_RATE * (z - Z_TOP))
    return (
        jnp.asarray(prof, F32),
        jnp.asarray(weight, F32),
        jnp.asarray(pick, F32).astype(BF16),
        jnp.asarray(rows, F32).astype(BF16),
        jnp.asarray(halves, F32).astype(BF16),
    )


RB = 16
PAD = 8
CHUNK = 16
TOGETHER = 8
LONG = 32
BAND = 32


def rank_of(tiles, q, want):
    at = jnp.int32(0)
    for step in (16, 8, 4, 2, 1):
        at = at + jnp.where(tiles[q * 32 + at + step - 1] < want, step, 0)
    return at


EARLY = 5


def step_kernel(tiles, prof, state, *refs):
    operands, refs = refs[:18], refs[18:]
    state_out, landed_out, sea_out = refs[:3]
    held, refs = refs[3:21], refs[21:]
    load_sem, done_sem = refs[-2:]
    step_body(
        tiles, prof, state, state_out, landed_out, sea_out, operands, held, load_sem, done_sem,
        *held, *refs[:-2]
    )


def step_body(
    tiles, prof, state, state_out, landed_out, sea_out, operands, held, load_sem, done_sem,
    eta, phi, up_c, up_s, up_spread,
    weight, pick, rows, halves, down_rows, down_cols,
    gather, bt_c, bt_s, finish, tw_c, tw_s, spread,
    landed, sea_held, source, tb_a, wide32, send_a, recv_a, phys,
    send1h, recv1h, send1v, recv1v, send2h, recv2h, send2v, recv2v,
    st, hh, cf, bl, cm, got, tb, send, recv,
    in_sem, out_sem, asem, arsem, ssem1h, rsem1h, ssem1v, rsem1v,
    ssem2h, rsem2h, ssem2v, rsem2v, csem, gsem, ssem, rsem,
):
    def fetch(s, i):
        part = pl.ds(i * CHUNK, CHUNK)
        return pltpu.make_async_copy(state.at[s, part], st.at[s, part], in_sem.at[s, i])

    def put(s, r):
        part = pl.ds(r * BAND, BAND)
        return pltpu.make_async_copy(
            st.at[s, :, part], state_out.at[s, :, part], out_sem.at[s, r]
        )

    def load(n):
        return pltpu.make_async_copy(operands[n], held[n], load_sem.at[n])

    for n in range(EARLY):
        load(n).start()
    w, g, ws, gs = around()
    me = w * NG + g
    barrier = greet_all(ws, gs)
    for n in range(EARLY, len(operands)):
        load(n).start()
    for s in range(2):
        for i in range(LV // CHUNK):
            fetch(s, i).start()
    for n in range(EARLY):
        load(n).wait()

    row = lax.broadcasted_iota(jnp.int32, (R, L), 0)
    lane = lane_iota(R)
    kx = me * R + row
    kx = jnp.where(kx >= N // 2, kx - N, kx).astype(F32) * (2.0 * math.pi / N)

    for f in range(3):
        x = []
        for n1 in range(16):
            cols = slice(n1 * L, (n1 + 1) * L)
            if f == 0:
                x.append((eta[0, :, cols].astype(F32), eta[1, :, cols].astype(F32)))
            else:
                if f == 1:
                    k = kx
                else:
                    base = n1 * L if n1 < 8 else n1 * L - N
                    k = (lane + base).astype(F32) * (2.0 * math.pi / N)
                x.append((-k * phi[1, :, cols].astype(F32), k * phi[0, :, cols].astype(F32)))
        y = sixteenth(x, 1)
        for k1 in range(16):
            c, s = up_c[k1:k1 + 1, :], up_s[k1:k1 + 1, :]
            a, b = y[k1]
            re = (a * c - b * s).astype(BF16)
            im = (a * s + b * c).astype(BF16)
            up = slice(f * R, (f + 1) * R)
            dn = slice(64 + f * R, 64 + (f + 1) * R)
            tb_a[k1, up, 0:L] = re
            tb_a[k1, up, L:2 * L] = -im
            tb_a[k1, dn, 0:L] = im
            tb_a[k1, dn, L:2 * L] = re

    zero = jnp.zeros((R, 2 * L), BF16)

    def rows_out(kk, carry):
        for h in range(2):
            tb_a[2 * kk + h, 48:64, :] = zero
            tb_a[2 * kk + h, 112:128, :] = zero
        rhs = tb_a[pl.ds(2 * kk, 2)].reshape(2 * L, 2 * L)
        z = nt_dot(up_spread[...], rhs)
        wide32[pl.ds(2 * kk, D, stride=R), :] = z[:, :L]
        wide32[pl.ds(2 * kk + 1, D, stride=R), :] = z[:, L:]
        return carry

    lax.fori_loop(0, 8, rows_out, 0, unroll=2)

    def narrow(i, carry):
        part = wide32[pl.ds(pl.multiple_of(i * 128, 128), 128), :]
        send_a[pl.ds(i * 8, 8)] = part.reshape(8, R, L).astype(BF16)
        return carry

    lax.fori_loop(0, 16, narrow, 0)

    pl.semaphore_wait(barrier, D - 1)
    spread_all(send_a, recv_a, asem, arsem, ws, gs)

    for q in range(NG):
        want = (2 * w + g // 4) * 32 + 4 * q
        at = rank_of(tiles, q, want)
        for c in range(4):
            found = tiles[q * 32 + at]
            source[0, 4 * q + c] = jnp.bitwise_and(at, NW - 1) * NG + q
            source[1, 4 * q + c] = lax.shift_right_logical(at, 4)
            source[2, 4 * q + c] = jnp.where(found == want + c, 1, 0)
            at = jnp.minimum(at + jnp.where(found <= want + c, 1, 0), 31)

    for n in range(EARLY, len(operands)):
        load(n).wait()
    edge = jnp.zeros((LV, PAD, SIDE), F32)
    for s in range(2):
        bl[s, :, 0:PAD, :] = edge
        bl[s, :, PAD + SIDE:, :] = edge
        for i in range(LV // CHUNK):
            fetch(s, i).wait()

        def share(o, carry, s=s):
            for b in range(SIDE // RB):
                rs = slice(b * RB, (b + 1) * RB)
                keep = 1.0 - weight[rs, :]
                for l in range(TOGETHER):
                    k = o * TOGETHER + l
                    bl[s, k, PAD + b * RB:PAD + (b + 1) * RB, :] = (
                        keep * st[s, k, rs, :].astype(F32)
                    )
            return carry

        lax.fori_loop(0, LV // TOGETHER, share, 0)

    landed_all(recv_a, arsem)

    def widen(i, carry):
        part = recv_a[pl.ds(i * 8, 8)].astype(F32)
        wide32[pl.ds(pl.multiple_of(i * 128, 128), 128), :] = part.reshape(128, L)
        return carry

    lax.fori_loop(0, 16, widen, 0)

    flip = jnp.where(lane_iota(D) < 64, -1.0, 1.0).astype(F32)

    def columns(yy, carry):
        x = jnp.concatenate(
            [
                wide32[pl.ds(2 * yy, D, stride=R), :].astype(BF16),
                wide32[pl.ds(2 * yy + 1, D, stride=R), :].astype(BF16),
            ],
            axis=1,
        )
        t = blocks_in(x, gather[...], bt_c[...], bt_s[...], flip)
        out = nt_dot(finish[...], t)
        phys[pl.ds(2 * yy, 48, stride=R), :] = out[:, :L]
        phys[pl.ds(2 * yy + 1, 48, stride=R), :] = out[:, L:]
        return carry

    lax.fori_loop(0, 8, columns, 0, unroll=4)

    low = lane < 64

    def heights(q, carry):
        for h in range(2):
            at = pl.multiple_of((2 * q + h) * R, R)
            send1h[q, h] = phys[pl.ds(at, R), :].astype(BF16)
        return carry

    lax.fori_loop(0, NG, heights, 0, unroll=4)
    spread_grp(send1h, recv1h, ssem1h, rsem1h, ws, gs)

    def speeds(q, carry):
        for h in range(2):
            vx = phys[pl.ds(pl.multiple_of((16 + 2 * q + h) * R, R), R), :]
            vy = phys[pl.ds(pl.multiple_of((32 + 2 * q + h) * R, R), R), :]
            send1v[q, 2 * h] = jnp.where(low, vx, pltpu.roll(vy, 64, 1)).astype(BF16)
            send1v[q, 2 * h + 1] = jnp.where(low, pltpu.roll(vx, 64, 1), vy).astype(BF16)
        return carry

    lax.fori_loop(0, NG, speeds, 0, unroll=2)
    spread_grp(send1v, recv1v, ssem1v, rsem1v, ws, gs)

    def tile_for(d):
        t0 = tiles[g * 32 + d]
        t1 = tiles[g * 32 + 16 + d]
        t = jnp.where(lax.shift_right_logical(t0, 6) == w, t0, t1)
        return jnp.bitwise_and(lax.shift_right_logical(t, 5), 1) * 4, jnp.bitwise_and(t, 3)

    landed_all(recv1h, rsem1h)

    def choose_heights(d, carry):
        upper, col = tile_for(d)
        right = (lane * 0 + jnp.bitwise_and(col, 1)) == 1
        pair = lax.shift_right_logical(col, 1)
        for q in range(2):
            a = recv1h[upper + 2 * q, pair].astype(F32)
            b = recv1h[upper + 2 * q + 1, pair].astype(F32)
            lo = jnp.where(right, pltpu.roll(a, 64, 1), a)
            hi = jnp.where(right, b, pltpu.roll(b, 64, 1))
            send2h[d, q] = jnp.where(low, lo, hi).astype(BF16)
        return carry

    lax.fori_loop(0, NW, choose_heights, 0, unroll=4)
    spread_wide(send2h, recv2h, ssem2h, rsem2h, ws, gs)

    landed_all(recv1v, rsem1v)

    def choose_speeds(d, carry):
        upper, col = tile_for(d)
        for q in range(4):
            send2v[d, q] = recv1v[upper + q, col]
        return carry

    lax.fori_loop(0, NW, choose_speeds, 0, unroll=4)
    spread_wide(send2v, recv2v, ssem2v, rsem2v, ws, gs)

    bands = [
        jnp.bitwise_and(lax.shift_right_logical(tiles[g * 32 + s * 16 + w], 6), NW - 1)
        for s in range(2)
    ]
    scale = LV / (Z_TOP - Z_BOTTOM)

    def up(m, sel, spread_rows):
        wide = jnp.dot(m, sel, preferred_element_type=F32).astype(BF16)
        return jnp.dot(spread_rows, wide, preferred_element_type=F32)

    landed_all(recv2h, rsem2h)
    for s in range(2):
        hgt = recv2h[bands[s]].reshape(32, L)
        height = up(hgt, pick[0], halves[0]) + up(hgt, pick[1], halves[1])
        hh[s] = height * scale - Z_BOTTOM * scale

        def blend(o, carry, s=s):
            for b in range(SIDE // RB):
                rs = slice(b * RB, (b + 1) * RB)
                h, wt = hh[s, rs, :], weight[rs, :]
                for l in range(TOGETHER):
                    k = o * TOGETHER + l
                    under = jnp.clip(h - lax.convert_element_type(k, F32), 0.0, 1.0)
                    bl[s, k, PAD + b * RB:PAD + (b + 1) * RB, :] += wt * under
            return carry

        lax.fori_loop(0, LV // TOGETHER, blend, 0)

    across = lax.broadcasted_iota(jnp.int32, (SIDE, SIDE), 1)
    sub = lax.broadcasted_iota(jnp.int32, (SIDE, SIDE), 0)

    def faces(a, axis, index):
        after = jnp.where(index == SIDE - 1, a, pltpu.roll(a, SIDE - 1, axis))
        before = jnp.where(index == 0, a, pltpu.roll(a, 1, axis))
        return (0.5 * COURANT) * (a + after), (0.5 * COURANT) * (before + a)

    landed_all(recv2v, rsem2v)
    for s in range(2):
        vel = recv2v[bands[s]].reshape(64, L)
        ax = up(vel, pick[0], rows[...])
        ay = up(vel, pick[1], rows[...])
        center = jnp.zeros((SIDE, SIDE), F32)
        for n, (a, axis, index) in enumerate(((ax, 1, across), (ay, 0, sub))):
            upper, lower = faces(a, axis, index)
            center += jnp.maximum(upper, 0.0) - jnp.minimum(lower, 0.0)
            from_up = jnp.minimum(upper, 0.0)
            from_low = -jnp.maximum(lower, 0.0)
            last, first = index == SIDE - 1, index == 0
            center += jnp.where(last, from_up, 0.0) + jnp.where(first, from_low, 0.0)
            cf[s, 1 + 2 * n] = jnp.where(last, 0.0, from_up)
            cf[s, 2 + 2 * n] = jnp.where(first, 0.0, from_low)
        cf[s, 0] = center

    high = lax.Precision.HIGHEST
    for r in range(SIDE // BAND):

        def slot(s, block, r=r):

            def move(o, accs):
                accs = list(accs)
                for n in range(BAND // RB):
                    first_row = r * BAND + n * RB
                    rs = slice(first_row, first_row + RB)
                    at = PAD + first_row
                    c0, c1, c2, c3, c4 = (cf[s, m, rs, :] for m in range(5))
                    for l in range(LONG):
                        k = o * LONG + l
                        mid = bl[s, k, at:at + RB, :]
                        nxt = bl[s, k, at + 1:at + 1 + RB, :]
                        prv = bl[s, k, at - 1:at - 1 + RB, :]
                        flow = c0 * mid + c1 * pltpu.roll(mid, SIDE - 1, 1)
                        flow = flow + c2 * pltpu.roll(mid, 1, 1) + c3 * nxt + c4 * prv
                        new = jnp.clip(mid - prof[k] * flow, 0.0, 1.0)
                        st[s, k, rs, :] = new.astype(BF16)
                        accs[n] = accs[n] + new
                return tuple(accs)

            none = jnp.zeros((RB, SIDE), F32)
            accs = lax.fori_loop(0, LV // LONG, move, (none,) * (BAND // RB))
            column = jnp.concatenate(accs, axis=0) * (1.0 / scale) + Z_BOTTOM
            part = jnp.dot(down_rows[...], column, preferred_element_type=F32, precision=high)
            return block + jnp.dot(
                part, down_cols[s], preferred_element_type=F32, precision=high
            )

        block = lax.fori_loop(0, 2, slot, jnp.zeros((R, L), F32))
        cm[r] = (0.25 * block).astype(BF16)
        for s in range(2):
            put(s, r).start()

        for to in (r, r + 4):
            for kw in WIDE_STEPS + [0]:

                def post(to=to, kw=kw, r=r):
                    pltpu.make_async_remote_copy(
                        cm.at[r], got.at[me], csem, gsem,
                        device_id=(ws[kw], to), device_id_type=MESH,
                    ).start()

                if kw:
                    post()
                else:
                    pl.when(g != to)(post)

                    @pl.when(g == to)
                    def _(r=r):
                        pltpu.make_async_copy(cm.at[r], got.at[me], gsem).start()

    landed_all(got, gsem)

    x = []
    for k2 in range(16):
        sides = []
        for h in range(2):
            cc = 2 * k2 + h
            tile = got[source[0, cc]].astype(F32)
            same = (lane * 0 + source[1, cc]) == h
            sides.append(jnp.where(same, tile, pltpu.roll(tile, 64, 1)))
        there = jnp.where(low, source[2, 2 * k2], source[2, 2 * k2 + 1]) == 1
        ht = phys[k2 * R:(k2 + 1) * R, :]
        vx = phys[256 + k2 * R:256 + (k2 + 1) * R, :]
        vy = phys[512 + k2 * R:512 + (k2 + 1) * R, :]
        sea = jnp.where(there, jnp.where(low, sides[0], sides[1]), ht)
        sea_held[:, k2 * L:(k2 + 1) * L] = sea
        x.append((-(sea + 0.5 * (vx * vx + vy * vy)), jnp.zeros((R, L), F32)))
    y = sixteenth(x, -1)
    for k1 in range(16):
        c, s = tw_c[k1:k1 + 1, :], tw_s[k1:k1 + 1, :]
        a, b = y[k1]
        re = (a * c - b * s).astype(BF16)
        im = (a * s + b * c).astype(BF16)
        q, e = k1 // 4, k1 % 4
        up_rows = slice(e * R, (e + 1) * R)
        dn_rows = slice(64 + e * R, 64 + (e + 1) * R)
        tb[q, up_rows, 0:L] = re
        tb[q, up_rows, L:2 * L] = -im
        tb[q, dn_rows, 0:L] = im
        tb[q, dn_rows, L:2 * L] = re

    for q in range(2):
        rhs = tb[2 * q:2 * q + 2].reshape(2 * L, 2 * L)
        z = nt_dot(spread[...], rhs)
        send[:, 2 * q, :] = z[:, :L]
        send[:, 2 * q + 1, :] = z[:, L:]

    spread_all(send, recv, ssem, rsem, ws, gs)
    sea_done = pltpu.make_async_copy(sea_held, sea_out, done_sem.at[0])
    sea_done.start()
    landed_all(recv, rsem)
    for q in range(4):
        landed[q] = recv[:, q, :].astype(BF16)
    all_done = pltpu.make_async_copy(landed, landed_out, done_sem.at[1])
    all_done.start()

    sent(send_a, D - 1, asem)
    sent(send1h, NG - 1, ssem1h)
    sent(send1v, NG - 1, ssem1v)
    sent(send2h, NW - 1, ssem2h)
    sent(send2v, NW - 1, ssem2v)
    sent(got, D - 1, csem)
    sent(send, D - 1, ssem)
    for s in range(2):
        for r in range(SIDE // BAND):
            put(s, r).wait()
    sea_done.wait()
    all_done.wait()


def settle_kernel(*refs):
    operands, (state,) = refs[:6], refs[6:7]
    surface, state_out, tendency = refs[7:10]
    held = refs[10:16]
    landed, gather, bt_c, bt_s, finish, sea = held
    out32, spectrum, kept, load_sem, done_sem, in_sem, out_sem = refs[16:]

    def copy(i, source, target, sem):
        s, part = i // 4, pl.ds((i % 4) * CHUNK, CHUNK)
        return pltpu.make_async_copy(source.at[s, part], target.at[s, part], sem.at[i])

    loads = [
        pltpu.make_async_copy(operands[n], held[n], load_sem.at[n]) for n in range(6)
    ]
    for n in range(6):
        loads[n].start()
    for i in range(8):
        copy(i, state, kept, in_sem).start()
    for n in range(6):
        loads[n].wait()
    sea_done = pltpu.make_async_copy(sea, surface, done_sem.at[0])
    sea_done.start()

    flip = jnp.where(lane_iota(D) < 64, -1.0, 1.0).astype(F32)
    for q in range(2):
        xx = jnp.concatenate([landed[2 * q], landed[2 * q + 1]], axis=1)
        t = blocks_in(xx, gather[...], bt_c[...], bt_s[...], flip)
        done = nt_dot(finish[...], t) * (1.0 / N)
        for h in range(2):
            for c in range(2):
                for e in range(4):
                    r0 = (c * 4 + e) * R
                    out32[pl.ds(c * 256 + 8 * q + 4 * h + e, R, stride=R), :] = done[
                        r0:r0 + R, h * L:(h + 1) * L
                    ]
        for i in range(4 * q, 4 * q + 4):
            copy(i, state, kept, in_sem).wait()
            copy(i, kept, state_out, out_sem).start()
    for c in range(2):
        for k2 in range(16):
            at = c * 256 + k2 * R
            spectrum[c, :, k2 * L:(k2 + 1) * L] = out32[at:at + R, :]
    all_done = pltpu.make_async_copy(spectrum, tendency, done_sem.at[1])
    all_done.start()

    for i in range(8):
        copy(i, kept, state_out, out_sem).wait()
    sea_done.wait()
    all_done.wait()


def shards(eta_hat, phi_hat, patch_tiles, fraction):
    smem = pl.BlockSpec(memory_space=pltpu.SMEM)
    dma = pltpu.SemaphoreType.DMA
    prof, weight, pick, rows, halves = patch_tables()
    down_rows = jnp.swapaxes(rows[:BAND, :R], 0, 1).astype(F32)
    down_cols = jnp.swapaxes(pick, 1, 2).astype(F32)
    anywhere = pl.BlockSpec(memory_space=pl.ANY)
    operands = (
        eta_hat, phi_hat, *lane_tables(1), weight, pick, rows, halves,
        down_rows, down_cols, *block_tables(1, 3, False), *lane_tables(-1),
    )
    new_state, landed, sea = pl.pallas_call(
        step_kernel,
        out_shape=(
            jax.ShapeDtypeStruct((2, LV, SIDE, SIDE), BF16),
            jax.ShapeDtypeStruct((4, D, L), BF16),
            jax.ShapeDtypeStruct((R, N), F32),
        ),
        in_specs=[smem, smem] + [anywhere] * (1 + len(operands)),
        out_specs=(anywhere,) * 3,
        scratch_shapes=[pltpu.VMEM(x.shape, x.dtype) for x in operands] + [
            pltpu.VMEM((4, D, L), BF16),
            pltpu.VMEM((R, N), F32),
            pltpu.SMEM((3, 32), jnp.int32),
            pltpu.VMEM((16, L, 2 * L), BF16),
            pltpu.VMEM((D * R, L), F32),
            pltpu.VMEM((D, R, L), BF16),
            pltpu.VMEM((D, R, L), BF16),
            pltpu.VMEM((48 * R, L), F32),
            pltpu.VMEM((NG, 2, R, L), BF16),
            pltpu.VMEM((NG, 2, R, L), BF16),
            pltpu.VMEM((NG, 4, R, L), BF16),
            pltpu.VMEM((NG, 4, R, L), BF16),
            pltpu.VMEM((NW, 2, R, L), BF16),
            pltpu.VMEM((NW, 2, R, L), BF16),
            pltpu.VMEM((NW, 4, R, L), BF16),
            pltpu.VMEM((NW, 4, R, L), BF16),
            pltpu.VMEM((2, LV, SIDE, SIDE), BF16),
            pltpu.VMEM((2, SIDE, SIDE), F32),
            pltpu.VMEM((2, 5, SIDE, SIDE), F32),
            pltpu.VMEM((2, LV, SIDE + 2 * PAD, SIDE), F32),
            pltpu.VMEM((4, R, L), BF16),
            pltpu.VMEM((D, R, L), BF16),
            pltpu.VMEM((4, L, 2 * L), BF16),
            pltpu.VMEM((D, 4, L), F32),
            pltpu.VMEM((D, 4, L), F32),
            dma((2, LV // CHUNK)),
            dma((2, SIDE // BAND)),
        ] + [dma] * 14 + [dma((len(operands),)), dma((2,))],
        compiler_params=pltpu.CompilerParams(
            collective_id=1, has_side_effects=True, vmem_limit_bytes=VMEM_LIMIT
        ),
        name="step",
    )(patch_tiles, prof, fraction[:, 0], *operands)

    last = (landed, *block_tables(-1, 4, True), sea)
    surface, new_state, tendency = pl.pallas_call(
        settle_kernel,
        out_shape=(
            jax.ShapeDtypeStruct((R, N), F32),
            jax.ShapeDtypeStruct((2, LV, SIDE, SIDE), BF16),
            jax.ShapeDtypeStruct((2, R, N), F32),
        ),
        in_specs=[anywhere] * 7,
        out_specs=(anywhere,) * 3,
        scratch_shapes=[pltpu.VMEM(x.shape, x.dtype) for x in last] + [
            pltpu.VMEM((512, L), F32),
            pltpu.VMEM((2, R, N), F32),
            pltpu.VMEM((2, LV, SIDE, SIDE), BF16),
            dma((6,)),
            dma((2,)),
            dma((8,)),
            dma((8,)),
        ],
        compiler_params=pltpu.CompilerParams(vmem_limit_bytes=VMEM_LIMIT),
        name="settle",
    )(*last, new_state)
    return (surface, new_state[:, None], tendency)


def solution(mesh):
    placed = (
        P(None, ("wide", "grp"), None),
        P(None, ("wide", "grp"), None),
        P(),
        P(None, ("wide", "grp"), None, None, None),
    )
    return jax.shard_map(
        shards,
        mesh=mesh,
        in_specs=placed,
        out_specs=(
            P(("wide", "grp"), None),
            P(None, ("wide", "grp"), None, None, None),
            P(None, ("wide", "grp"), None),
        ),
        check_vma=False,
    )
```

```python
import functools
import math

import jax
import jax.numpy as jnp
import numpy as np
from jax import lax
from jax.experimental import pallas as pl
from jax.experimental.pallas import tpu as pltpu
from jax.sharding import PartitionSpec as P

F32 = jnp.float32
BF16 = jnp.bfloat16
MESH = pl.DeviceIdType.MESH

N = 2048
D = 128
NW = 16
NG = 8
L = 128
R = 16
LV = 64
SIDE = 128
TS = 64
Z_BOTTOM = -2.0
Z_TOP = 2.0
DECAY_RATE = 0.5
COURANT = 0.3
VMEM_LIMIT = 56 << 20


def unit(phase, length):
    angle = (phase % length) * (2.0 * math.pi / length)
    return np.cos(angle), np.sin(angle)


def lane_tables(sign):
    k1 = np.arange(R)[:, None]
    n2 = np.arange(L)[None, :]
    tc, ts = unit(k1 * n2, N)
    k2 = np.arange(D)[:, None]
    c, s = unit(k2 * n2, D)
    spread = np.concatenate([c, sign * s], axis=1)
    return (
        jnp.asarray(tc, F32),
        jnp.asarray(sign * ts, F32),
        jnp.asarray(spread, F32).astype(BF16),
    )


def block_tables(sign, blocks, full):
    k1 = np.arange(D)[:, None]
    src = np.arange(D)[None, :]
    c, s = unit(k1 * src, D)
    gather = np.concatenate([c, sign * s], axis=0)
    j = np.tile(np.arange(R), 8)[None, :]
    tc, ts = unit(k1 * j, N)
    k2 = np.arange(R)[:, None]
    jj = np.arange(R)[None, :]
    cc, ss = unit(k2 * jj, R)
    ss = sign * ss
    rows = []
    for part in range(2 if full else 1):
        for e in range(blocks):
            out = np.zeros((R, 2, 4, R))
            out[:, 0, e, :] = cc if part == 0 else ss
            out[:, 1, e, :] = -ss if part == 0 else cc
            rows.append(out.reshape(R, L))
    finish = np.concatenate(rows, axis=0)
    return (
        jnp.asarray(gather, F32).astype(BF16),
        jnp.asarray(tc, F32),
        jnp.asarray(sign * ts, F32),
        jnp.asarray(finish, F32).astype(BF16),
    )


def fourth(x, sign):
    (ar, ai), (br, bi), (cr, ci), (dr, di) = x
    t0r, t0i, t1r, t1i = ar + cr, ai + ci, ar - cr, ai - ci
    t2r, t2i, t3r, t3i = br + dr, bi + di, br - dr, bi - di
    if sign < 0:
        t3r, t3i = -t3r, -t3i
    return (
        (t0r + t2r, t0i + t2i),
        (t1r - t3i, t1i + t3r),
        (t0r - t2r, t0i - t2i),
        (t1r + t3i, t1i - t3r),
    )


def times(x, re, im):
    if abs(im) < 1e-12 and abs(re - 1.0) < 1e-12:
        return x
    a, b = x
    return (a * re - b * im, a * im + b * re)


def sixteenth(x, sign):
    inner = []
    for b in range(4):
        y = fourth([x[4 * a + b] for a in range(4)], sign)
        turned = []
        for c in range(4):
            angle = sign * 2.0 * math.pi * b * c / 16
            turned.append(times(y[c], math.cos(angle), math.sin(angle)))
        inner.append(turned)
    out = [None] * 16
    for c in range(4):
        z = fourth([inner[b][c] for b in range(4)], sign)
        for d in range(4):
            out[c + 4 * d] = z[d]
    return out


def nt_dot(a, b):
    return lax.dot_general(a, b, (((1,), (1,)), ((), ())), preferred_element_type=F32)


def blocks_in(x, gather, tc, ts, flip):
    both = jnp.dot(gather, x, preferred_element_type=F32)
    parts = []
    for h in range(2):
        a = both[:D, h * L:(h + 1) * L]
        b = both[D:, h * L:(h + 1) * L]
        u = a * tc - b * ts
        v = b * tc + a * ts
        parts.append((u + flip * pltpu.roll(v, 64, 1)).astype(BF16))
    return jnp.concatenate(parts, axis=0)


def lane_iota(rows):
    return lax.broadcasted_iota(jnp.int32, (rows, L), 1)


def hops(step):
    return min(step, 4 - step)


def far(kw, kg):
    return hops(kw // 4) + hops(kw % 4) + hops(kg // 2) + 0.5 * (kg % 2)


WIDE_STEPS = sorted(range(1, NW), key=lambda k: -far(k, 0))
GRP_STEPS = sorted(range(1, NG), key=lambda k: -far(0, k))
ALL_STEPS = sorted(
    [(kw, kg) for kw in range(NW) for kg in range(NG) if kw or kg], key=lambda k: -far(*k)
)


def around():
    w = lax.axis_index("wide")
    g = lax.axis_index("grp")
    y = [lax.rem(w // 4 + k, 4) for k in range(4)]
    z = [lax.rem(w % 4 + k, 4) for k in range(4)]
    x = [lax.rem(g // 2 + k, 4) for k in range(4)]
    c = [g % 2, 1 - g % 2]
    ws = [y[k // 4] * 4 + z[k % 4] for k in range(NW)]
    gs = [x[k // 2] * 2 + c[k % 2] for k in range(NG)]
    return w, g, ws, gs


def greet_all(ws, gs):
    barrier = pltpu.get_barrier_semaphore()
    for kw, kg in ALL_STEPS:
        pl.semaphore_signal(
            barrier, inc=1, device_id=(ws[kw], gs[kg]), device_id_type=MESH
        )
    return barrier


def spread_all(send, recv, ssem, rsem, ws, gs):
    me = ws[0] * NG + gs[0]
    pltpu.make_async_copy(send.at[me], recv.at[me], rsem).start()
    for kw, kg in ALL_STEPS:
        pltpu.make_async_remote_copy(
            send.at[ws[kw] * NG + gs[kg]], recv.at[me], ssem, rsem,
            device_id=(ws[kw], gs[kg]), device_id_type=MESH,
        ).start()


def spread_grp(send, recv, ssem, rsem, ws, gs):
    pltpu.make_async_copy(send.at[gs[0]], recv.at[gs[0]], rsem).start()
    for k in GRP_STEPS:
        pltpu.make_async_remote_copy(
            send.at[gs[k]], recv.at[gs[0]], ssem, rsem,
            device_id=(ws[0], gs[k]), device_id_type=MESH,
        ).start()


def spread_wide(send, recv, ssem, rsem, ws, gs):
    pltpu.make_async_copy(send.at[ws[0]], recv.at[ws[0]], rsem).start()
    for k in WIDE_STEPS:
        pltpu.make_async_remote_copy(
            send.at[ws[k]], recv.at[ws[0]], ssem, rsem,
            device_id=(ws[k], gs[0]), device_id_type=MESH,
        ).start()


def landed_all(buf, sem):
    pltpu.make_async_copy(buf, buf, sem).wait()


def sent(buf, n, sem):
    pltpu.make_async_copy(buf.at[pl.ds(0, n)], buf.at[pl.ds(0, n)], sem).wait()


def patch_tables():
    pos = np.arange(SIDE)
    edge = np.minimum(pos, SIDE - 1 - pos)
    dist = np.minimum(edge[:, None], edge[None, :])
    weight = 0.3 + 0.7 * np.exp(-8.0 * dist / SIDE)
    x = np.arange(SIDE)
    pick = np.zeros((2, L, SIDE))
    for h in range(2):
        pick[h, 64 * h + x // 2, x] = 1.0
    rows = np.zeros((SIDE, TS))
    rows[x, x // 2] = 1.0
    halves = np.zeros((2, SIDE, 32))
    for i in range(SIDE):
        r = i // 2
        blk, within = r // 16, r % 16
        halves[blk % 2, i, (blk // 2) * 16 + within] = 1.0
    z = Z_BOTTOM + (np.arange(LV) + 0.5) * ((Z_TOP - Z_BOTTOM) / LV)
    prof = np.exp(DECAY_RATE * (z - Z_TOP))
    return (
        jnp.asarray(prof, F32),
        jnp.asarray(weight, F32),
        jnp.asarray(pick, F32).astype(BF16),
        jnp.asarray(rows, F32).astype(BF16),
        jnp.asarray(halves, F32).astype(BF16),
    )


RB = 16
PAD = 8
CHUNK = 16
TOGETHER = 8
LONG = 64
BAND = 32


def rank_of(tiles, q, want):
    at = jnp.int32(0)
    for step in (16, 8, 4, 2, 1):
        at = at + jnp.where(tiles[q * 32 + at + step - 1] < want, step, 0)
    return at


EARLY = 5


def step_kernel(tiles, prof, state, *refs):
    operands, refs = refs[:18], refs[18:]
    state_out, landed_out, sea_out = refs[:3]
    held, refs = refs[3:21], refs[21:]
    load_sem, done_sem = refs[-2:]
    step_body(
        tiles, prof, state, state_out, landed_out, sea_out, operands, held, load_sem, done_sem,
        *held, *refs[:-2]
    )


def step_body(
    tiles, prof, state, state_out, landed_out, sea_out, operands, held, load_sem, done_sem,
    eta, phi, up_c, up_s, up_spread,
    weight, pick, rows, halves, down_rows, down_cols,
    gather, bt_c, bt_s, finish, tw_c, tw_s, spread,
    landed, sea_held, source, tb_a, wide32, send_a, recv_a, phys,
    send1h, recv1h, send1v, recv1v, send2h, recv2h, send2v, recv2v,
    st, hh, cf, bl, cm, got, tb, send, recv,
    in_sem, out_sem, asem, arsem, ssem1h, rsem1h, ssem1v, rsem1v,
    ssem2h, rsem2h, ssem2v, rsem2v, csem, gsem, ssem, rsem,
):
    def fetch(s, i):
        part = pl.ds(i * CHUNK, CHUNK)
        return pltpu.make_async_copy(state.at[s, part], st.at[s, part], in_sem.at[s, i])

    def put(s, r):
        part = pl.ds(r * BAND, BAND)
        return pltpu.make_async_copy(
            st.at[s, :, part], state_out.at[s, :, part], out_sem.at[s, r]
        )

    def load(n):
        return pltpu.make_async_copy(operands[n], held[n], load_sem.at[n])

    for n in range(EARLY):
        load(n).start()
    w, g, ws, gs = around()
    me = w * NG + g
    barrier = greet_all(ws, gs)
    for n in range(EARLY, len(operands)):
        load(n).start()
    for s in range(2):
        for i in range(LV // CHUNK):
            fetch(s, i).start()
    for n in range(EARLY):
        load(n).wait()

    row = lax.broadcasted_iota(jnp.int32, (R, L), 0)
    lane = lane_iota(R)
    kx = me * R + row
    kx = jnp.where(kx >= N // 2, kx - N, kx).astype(F32) * (2.0 * math.pi / N)

    for f in range(3):
        x = []
        for n1 in range(16):
            cols = slice(n1 * L, (n1 + 1) * L)
            if f == 0:
                x.append((eta[0, :, cols].astype(F32), eta[1, :, cols].astype(F32)))
            else:
                if f == 1:
                    k = kx
                else:
                    base = n1 * L if n1 < 8 else n1 * L - N
                    k = (lane + base).astype(F32) * (2.0 * math.pi / N)
                x.append((-k * phi[1, :, cols].astype(F32), k * phi[0, :, cols].astype(F32)))
        y = sixteenth(x, 1)
        for k1 in range(16):
            c, s = up_c[k1:k1 + 1, :], up_s[k1:k1 + 1, :]
            a, b = y[k1]
            re = (a * c - b * s).astype(BF16)
            im = (a * s + b * c).astype(BF16)
            up = slice(f * R, (f + 1) * R)
            dn = slice(64 + f * R, 64 + (f + 1) * R)
            tb_a[k1, up, 0:L] = re
            tb_a[k1, up, L:2 * L] = -im
            tb_a[k1, dn, 0:L] = im
            tb_a[k1, dn, L:2 * L] = re

    zero = jnp.zeros((R, 2 * L), BF16)

    def rows_out(kk, carry):
        for h in range(2):
            tb_a[2 * kk + h, 48:64, :] = zero
            tb_a[2 * kk + h, 112:128, :] = zero
        rhs = tb_a[pl.ds(2 * kk, 2)].reshape(2 * L, 2 * L)
        z = nt_dot(up_spread[...], rhs)
        wide32[pl.ds(2 * kk, D, stride=R), :] = z[:, :L]
        wide32[pl.ds(2 * kk + 1, D, stride=R), :] = z[:, L:]
        return carry

    lax.fori_loop(0, 8, rows_out, 0, unroll=2)

    def narrow(i, carry):
        part = wide32[pl.ds(pl.multiple_of(i * 128, 128), 128), :]
        send_a[pl.ds(i * 8, 8)] = part.reshape(8, R, L).astype(BF16)
        return carry

    lax.fori_loop(0, 16, narrow, 0)

    pl.semaphore_wait(barrier, D - 1)
    spread_all(send_a, recv_a, asem, arsem, ws, gs)

    for q in range(NG):
        want = (2 * w + g // 4) * 32 + 4 * q
        at = rank_of(tiles, q, want)
        for c in range(4):
            found = tiles[q * 32 + at]
            source[0, 4 * q + c] = jnp.bitwise_and(at, NW - 1) * NG + q
            source[1, 4 * q + c] = lax.shift_right_logical(at, 4)
            source[2, 4 * q + c] = jnp.where(found == want + c, 1, 0)
            at = jnp.minimum(at + jnp.where(found <= want + c, 1, 0), 31)

    for n in range(EARLY, len(operands)):
        load(n).wait()
    edge = jnp.zeros((LV, PAD, SIDE), F32)
    for s in range(2):
        bl[s, :, 0:PAD, :] = edge
        bl[s, :, PAD + SIDE:, :] = edge
        for i in range(LV // CHUNK):
            fetch(s, i).wait()

        def share(o, carry, s=s):
            for b in range(SIDE // RB):
                rs = slice(b * RB, (b + 1) * RB)
                keep = 1.0 - weight[rs, :]
                for l in range(TOGETHER):
                    k = o * TOGETHER + l
                    bl[s, k, PAD + b * RB:PAD + (b + 1) * RB, :] = (
                        keep * st[s, k, rs, :].astype(F32)
                    )
            return carry

        lax.fori_loop(0, LV // TOGETHER, share, 0)

    landed_all(recv_a, arsem)

    def widen(i, carry):
        part = recv_a[pl.ds(i * 8, 8)].astype(F32)
        wide32[pl.ds(pl.multiple_of(i * 128, 128), 128), :] = part.reshape(128, L)
        return carry

    lax.fori_loop(0, 16, widen, 0)

    flip = jnp.where(lane_iota(D) < 64, -1.0, 1.0).astype(F32)

    def columns(yy, carry):
        x = jnp.concatenate(
            [
                wide32[pl.ds(2 * yy, D, stride=R), :].astype(BF16),
                wide32[pl.ds(2 * yy + 1, D, stride=R), :].astype(BF16),
            ],
            axis=1,
        )
        t = blocks_in(x, gather[...], bt_c[...], bt_s[...], flip)
        out = nt_dot(finish[...], t)
        phys[pl.ds(2 * yy, 48, stride=R), :] = out[:, :L]
        phys[pl.ds(2 * yy + 1, 48, stride=R), :] = out[:, L:]
        return carry

    lax.fori_loop(0, 8, columns, 0, unroll=4)

    low = lane < 64

    def heights(q, carry):
        for h in range(2):
            at = pl.multiple_of((2 * q + h) * R, R)
            send1h[q, h] = phys[pl.ds(at, R), :].astype(BF16)
        return carry

    lax.fori_loop(0, NG, heights, 0, unroll=4)
    spread_grp(send1h, recv1h, ssem1h, rsem1h, ws, gs)

    def speeds(q, carry):
        for h in range(2):
            vx = phys[pl.ds(pl.multiple_of((16 + 2 * q + h) * R, R), R), :]
            vy = phys[pl.ds(pl.multiple_of((32 + 2 * q + h) * R, R), R), :]
            send1v[q, 2 * h] = jnp.where(low, vx, pltpu.roll(vy, 64, 1)).astype(BF16)
            send1v[q, 2 * h + 1] = jnp.where(low, pltpu.roll(vx, 64, 1), vy).astype(BF16)
        return carry

    lax.fori_loop(0, NG, speeds, 0, unroll=2)
    spread_grp(send1v, recv1v, ssem1v, rsem1v, ws, gs)

    def tile_for(d):
        t0 = tiles[g * 32 + d]
        t1 = tiles[g * 32 + 16 + d]
        t = jnp.where(lax.shift_right_logical(t0, 6) == w, t0, t1)
        return jnp.bitwise_and(lax.shift_right_logical(t, 5), 1) * 4, jnp.bitwise_and(t, 3)

    landed_all(recv1h, rsem1h)

    def choose_heights(d, carry):
        upper, col = tile_for(d)
        right = (lane * 0 + jnp.bitwise_and(col, 1)) == 1
        pair = lax.shift_right_logical(col, 1)
        for q in range(2):
            a = recv1h[upper + 2 * q, pair].astype(F32)
            b = recv1h[upper + 2 * q + 1, pair].astype(F32)
            lo = jnp.where(right, pltpu.roll(a, 64, 1), a)
            hi = jnp.where(right, b, pltpu.roll(b, 64, 1))
            send2h[d, q] = jnp.where(low, lo, hi).astype(BF16)
        return carry

    lax.fori_loop(0, NW, choose_heights, 0, unroll=8)
    spread_wide(send2h, recv2h, ssem2h, rsem2h, ws, gs)

    landed_all(recv1v, rsem1v)

    def choose_speeds(d, carry):
        upper, col = tile_for(d)
        for q in range(4):
            send2v[d, q] = recv1v[upper + q, col]
        return carry

    lax.fori_loop(0, NW, choose_speeds, 0, unroll=16)
    spread_wide(send2v, recv2v, ssem2v, rsem2v, ws, gs)

    bands = [
        jnp.bitwise_and(lax.shift_right_logical(tiles[g * 32 + s * 16 + w], 6), NW - 1)
        for s in range(2)
    ]
    scale = LV / (Z_TOP - Z_BOTTOM)

    def up(m, sel, spread_rows):
        wide = jnp.dot(m, sel, preferred_element_type=F32).astype(BF16)
        return jnp.dot(spread_rows, wide, preferred_element_type=F32)

    landed_all(recv2h, rsem2h)
    for s in range(2):
        hgt = recv2h[bands[s]].reshape(32, L)
        height = up(hgt, pick[0], halves[0]) + up(hgt, pick[1], halves[1])
        hh[s] = height * scale - Z_BOTTOM * scale

        def blend(o, carry, s=s):
            for b in range(SIDE // RB):
                rs = slice(b * RB, (b + 1) * RB)
                h, wt = hh[s, rs, :], weight[rs, :]
                for l in range(TOGETHER):
                    k = o * TOGETHER + l
                    under = jnp.clip(h - lax.convert_element_type(k, F32), 0.0, 1.0)
                    bl[s, k, PAD + b * RB:PAD + (b + 1) * RB, :] += wt * under
            return carry

        lax.fori_loop(0, LV // TOGETHER, blend, 0)

    across = lax.broadcasted_iota(jnp.int32, (SIDE, SIDE), 1)
    sub = lax.broadcasted_iota(jnp.int32, (SIDE, SIDE), 0)

    def faces(a, axis, index):
        after = jnp.where(index == SIDE - 1, a, pltpu.roll(a, SIDE - 1, axis))
        before = jnp.where(index == 0, a, pltpu.roll(a, 1, axis))
        return (0.5 * COURANT) * (a + after), (0.5 * COURANT) * (before + a)

    landed_all(recv2v, rsem2v)
    for s in range(2):
        vel = recv2v[bands[s]].reshape(64, L)
        ax = up(vel, pick[0], rows[...])
        ay = up(vel, pick[1], rows[...])
        center = jnp.zeros((SIDE, SIDE), F32)
        for n, (a, axis, index) in enumerate(((ax, 1, across), (ay, 0, sub))):
            upper, lower = faces(a, axis, index)
            center += jnp.maximum(upper, 0.0) - jnp.minimum(lower, 0.0)
            from_up = jnp.minimum(upper, 0.0)
            from_low = -jnp.maximum(lower, 0.0)
            last, first = index == SIDE - 1, index == 0
            center += jnp.where(last, from_up, 0.0) + jnp.where(first, from_low, 0.0)
            cf[s, 1 + 2 * n] = jnp.where(last, 0.0, from_up)
            cf[s, 2 + 2 * n] = jnp.where(first, 0.0, from_low)
        cf[s, 0] = center

    high = lax.Precision.HIGHEST
    for r in range(SIDE // BAND):

        def slot(s, block, r=r):

            def move(o, accs):
                accs = list(accs)
                for n in range(BAND // RB):
                    first_row = r * BAND + n * RB
                    rs = slice(first_row, first_row + RB)
                    at = PAD + first_row
                    c0, c1, c2, c3, c4 = (cf[s, m, rs, :] for m in range(5))
                    for l in range(LONG):
                        k = o * LONG + l
                        mid = bl[s, k, at:at + RB, :]
                        nxt = bl[s, k, at + 1:at + 1 + RB, :]
                        prv = bl[s, k, at - 1:at - 1 + RB, :]
                        flow = c0 * mid + c1 * pltpu.roll(mid, SIDE - 1, 1)
                        flow = flow + c2 * pltpu.roll(mid, 1, 1) + c3 * nxt + c4 * prv
                        new = jnp.clip(mid - prof[k] * flow, 0.0, 1.0)
                        st[s, k, rs, :] = new.astype(BF16)
                        accs[n] = accs[n] + new
                return tuple(accs)

            none = jnp.zeros((RB, SIDE), F32)
            accs = lax.fori_loop(0, LV // LONG, move, (none,) * (BAND // RB))
            column = jnp.concatenate(accs, axis=0) * (1.0 / scale) + Z_BOTTOM
            part = jnp.dot(down_rows[...], column, preferred_element_type=F32, precision=high)
            return block + jnp.dot(
                part, down_cols[s], preferred_element_type=F32, precision=high
            )

        block = lax.fori_loop(0, 2, slot, jnp.zeros((R, L), F32))
        cm[r] = (0.25 * block).astype(BF16)
        for s in range(2):
            put(s, r).start()

        for to in (r, r + 4):
            for kw in WIDE_STEPS + [0]:

                def post(to=to, kw=kw, r=r):
                    pltpu.make_async_remote_copy(
                        cm.at[r], got.at[me], csem, gsem,
                        device_id=(ws[kw], to), device_id_type=MESH,
                    ).start()

                if kw:
                    post()
                else:
                    pl.when(g != to)(post)

                    @pl.when(g == to)
                    def _(r=r):
                        pltpu.make_async_copy(cm.at[r], got.at[me], gsem).start()

    landed_all(got, gsem)

    x = []
    for k2 in range(16):
        sides = []
        for h in range(2):
            cc = 2 * k2 + h
            tile = got[source[0, cc]].astype(F32)
            same = (lane * 0 + source[1, cc]) == h
            sides.append(jnp.where(same, tile, pltpu.roll(tile, 64, 1)))
        there = jnp.where(low, source[2, 2 * k2], source[2, 2 * k2 + 1]) == 1
        ht = phys[k2 * R:(k2 + 1) * R, :]
        vx = phys[256 + k2 * R:256 + (k2 + 1) * R, :]
        vy = phys[512 + k2 * R:512 + (k2 + 1) * R, :]
        sea = jnp.where(there, jnp.where(low, sides[0], sides[1]), ht)
        sea_held[:, k2 * L:(k2 + 1) * L] = sea
        x.append((-(sea + 0.5 * (vx * vx + vy * vy)), jnp.zeros((R, L), F32)))
    y = sixteenth(x, -1)
    for k1 in range(16):
        c, s = tw_c[k1:k1 + 1, :], tw_s[k1:k1 + 1, :]
        a, b = y[k1]
        re = (a * c - b * s).astype(BF16)
        im = (a * s + b * c).astype(BF16)
        q, e = k1 // 4, k1 % 4
        up_rows = slice(e * R, (e + 1) * R)
        dn_rows = slice(64 + e * R, 64 + (e + 1) * R)
        tb[q, up_rows, 0:L] = re
        tb[q, up_rows, L:2 * L] = -im
        tb[q, dn_rows, 0:L] = im
        tb[q, dn_rows, L:2 * L] = re

    for q in range(2):
        rhs = tb[2 * q:2 * q + 2].reshape(2 * L, 2 * L)
        z = nt_dot(spread[...], rhs)
        send[:, 2 * q, :] = z[:, :L]
        send[:, 2 * q + 1, :] = z[:, L:]

    spread_all(send, recv, ssem, rsem, ws, gs)
    sea_done = pltpu.make_async_copy(sea_held, sea_out, done_sem.at[0])
    sea_done.start()
    landed_all(recv, rsem)
    for q in range(4):
        landed[q] = recv[:, q, :].astype(BF16)
    all_done = pltpu.make_async_copy(landed, landed_out, done_sem.at[1])
    all_done.start()

    sent(send_a, D - 1, asem)
    sent(send1h, NG - 1, ssem1h)
    sent(send1v, NG - 1, ssem1v)
    sent(send2h, NW - 1, ssem2h)
    sent(send2v, NW - 1, ssem2v)
    sent(got, D - 1, csem)
    sent(send, D - 1, ssem)
    for s in range(2):
        for r in range(SIDE // BAND):
            put(s, r).wait()
    sea_done.wait()
    all_done.wait()


def settle_kernel(*refs):
    operands, (state,) = refs[:6], refs[6:7]
    surface, state_out, tendency = refs[7:10]
    held = refs[10:16]
    landed, gather, bt_c, bt_s, finish, sea = held
    out32, spectrum, kept, load_sem, done_sem, in_sem, out_sem = refs[16:]

    def copy(i, source, target, sem):
        s, part = i // 4, pl.ds((i % 4) * CHUNK, CHUNK)
        return pltpu.make_async_copy(source.at[s, part], target.at[s, part], sem.at[i])

    loads = [
        pltpu.make_async_copy(operands[n], held[n], load_sem.at[n]) for n in range(6)
    ]
    for n in range(6):
        loads[n].start()
    for i in range(8):
        copy(i, state, kept, in_sem).start()
    for n in range(6):
        loads[n].wait()
    sea_done = pltpu.make_async_copy(sea, surface, done_sem.at[0])
    sea_done.start()

    def hand_on(i):
        copy(i, state, kept, in_sem).wait()
        copy(i, kept, state_out, out_sem).start()

    for i in range(4):
        hand_on(i)

    flip = jnp.where(lane_iota(D) < 64, -1.0, 1.0).astype(F32)
    turned = [
        blocks_in(
            jnp.concatenate([landed[2 * q], landed[2 * q + 1]], axis=1),
            gather[...], bt_c[...], bt_s[...], flip,
        )
        for q in range(2)
    ]
    done = nt_dot(finish[...], jnp.concatenate(turned, axis=0)) * (1.0 / N)
    for h in range(4):
        for c in range(2):
            for e in range(4):
                r0 = (c * 4 + e) * R
                out32[pl.ds(c * 256 + 4 * h + e, R, stride=R), :] = done[
                    r0:r0 + R, h * L:(h + 1) * L
                ]
    for i in range(4, 8):
        hand_on(i)
    for c in range(2):
        for k2 in range(16):
            at = c * 256 + k2 * R
            spectrum[c, :, k2 * L:(k2 + 1) * L] = out32[at:at + R, :]
    all_done = pltpu.make_async_copy(spectrum, tendency, done_sem.at[1])
    all_done.start()

    for i in range(8):
        copy(i, kept, state_out, out_sem).wait()
    sea_done.wait()
    all_done.wait()


def shards(eta_hat, phi_hat, patch_tiles, fraction):
    smem = pl.BlockSpec(memory_space=pltpu.SMEM)
    dma = pltpu.SemaphoreType.DMA
    prof, weight, pick, rows, halves = patch_tables()
    down_rows = jnp.swapaxes(rows[:BAND, :R], 0, 1).astype(F32)
    down_cols = jnp.swapaxes(pick, 1, 2).astype(F32)
    anywhere = pl.BlockSpec(memory_space=pl.ANY)
    operands = (
        eta_hat, phi_hat, *lane_tables(1), weight, pick, rows, halves,
        down_rows, down_cols, *block_tables(1, 3, False), *lane_tables(-1),
    )
    new_state, landed, sea = pl.pallas_call(
        step_kernel,
        out_shape=(
            jax.ShapeDtypeStruct((2, LV, SIDE, SIDE), BF16),
            jax.ShapeDtypeStruct((4, D, L), BF16),
            jax.ShapeDtypeStruct((R, N), F32),
        ),
        in_specs=[smem, smem] + [anywhere] * (1 + len(operands)),
        out_specs=(anywhere,) * 3,
        scratch_shapes=[pltpu.VMEM(x.shape, x.dtype) for x in operands] + [
            pltpu.VMEM((4, D, L), BF16),
            pltpu.VMEM((R, N), F32),
            pltpu.SMEM((3, 32), jnp.int32),
            pltpu.VMEM((16, L, 2 * L), BF16),
            pltpu.VMEM((D * R, L), F32),
            pltpu.VMEM((D, R, L), BF16),
            pltpu.VMEM((D, R, L), BF16),
            pltpu.VMEM((48 * R, L), F32),
            pltpu.VMEM((NG, 2, R, L), BF16),
            pltpu.VMEM((NG, 2, R, L), BF16),
            pltpu.VMEM((NG, 4, R, L), BF16),
            pltpu.VMEM((NG, 4, R, L), BF16),
            pltpu.VMEM((NW, 2, R, L), BF16),
            pltpu.VMEM((NW, 2, R, L), BF16),
            pltpu.VMEM((NW, 4, R, L), BF16),
            pltpu.VMEM((NW, 4, R, L), BF16),
            pltpu.VMEM((2, LV, SIDE, SIDE), BF16),
            pltpu.VMEM((2, SIDE, SIDE), F32),
            pltpu.VMEM((2, 5, SIDE, SIDE), F32),
            pltpu.VMEM((2, LV, SIDE + 2 * PAD, SIDE), F32),
            pltpu.VMEM((4, R, L), BF16),
            pltpu.VMEM((D, R, L), BF16),
            pltpu.VMEM((4, L, 2 * L), BF16),
            pltpu.VMEM((D, 4, L), F32),
            pltpu.VMEM((D, 4, L), F32),
            dma((2, LV // CHUNK)),
            dma((2, SIDE // BAND)),
        ] + [dma] * 14 + [dma((len(operands),)), dma((2,))],
        compiler_params=pltpu.CompilerParams(
            collective_id=1, has_side_effects=True, vmem_limit_bytes=VMEM_LIMIT
        ),
        name="step",
    )(patch_tiles, prof, fraction[:, 0], *operands)

    last = (landed, *block_tables(-1, 4, True), sea)
    surface, new_state, tendency = pl.pallas_call(
        settle_kernel,
        out_shape=(
            jax.ShapeDtypeStruct((R, N), F32),
            jax.ShapeDtypeStruct((2, LV, SIDE, SIDE), BF16),
            jax.ShapeDtypeStruct((2, R, N), F32),
        ),
        in_specs=[anywhere] * 7,
        out_specs=(anywhere,) * 3,
        scratch_shapes=[pltpu.VMEM(x.shape, x.dtype) for x in last] + [
            pltpu.VMEM((512, L), F32),
            pltpu.VMEM((2, R, N), F32),
            pltpu.VMEM((2, LV, SIDE, SIDE), BF16),
            dma((6,)),
            dma((2,)),
            dma((8,)),
            dma((8,)),
        ],
        compiler_params=pltpu.CompilerParams(vmem_limit_bytes=VMEM_LIMIT),
        name="settle",
    )(*last, new_state)
    return (surface, new_state[:, None], tendency)


def solution(mesh):
    placed = (
        P(None, ("wide", "grp"), None),
        P(None, ("wide", "grp"), None),
        P(),
        P(None, ("wide", "grp"), None, None, None),
    )
    return jax.shard_map(
        shards,
        mesh=mesh,
        in_specs=placed,
        out_specs=(
            P(("wide", "grp"), None),
            P(None, ("wide", "grp"), None, None, None),
            P(None, ("wide", "grp"), None),
        ),
        check_vma=False,
    )
```

```python
import functools
import math

import jax
import jax.numpy as jnp
import numpy as np
from jax import lax
from jax.experimental import pallas as pl
from jax.experimental.pallas import tpu as pltpu
from jax.sharding import PartitionSpec as P

F32 = jnp.float32
BF16 = jnp.bfloat16
MESH = pl.DeviceIdType.MESH

N = 2048
D = 128
NW = 16
NG = 8
L = 128
R = 16
LV = 64
SIDE = 128
TS = 64
Z_BOTTOM = -2.0
Z_TOP = 2.0
DECAY_RATE = 0.5
COURANT = 0.3
VMEM_LIMIT = 56 << 20


def unit(phase, length):
    angle = (phase % length) * (2.0 * math.pi / length)
    return np.cos(angle), np.sin(angle)


def lane_tables(sign):
    k1 = np.arange(R)[:, None]
    n2 = np.arange(L)[None, :]
    tc, ts = unit(k1 * n2, N)
    k2 = np.arange(D)[:, None]
    c, s = unit(k2 * n2, D)
    spread = np.concatenate([c, sign * s], axis=1)
    return (
        jnp.asarray(tc, F32),
        jnp.asarray(sign * ts, F32),
        jnp.asarray(spread, F32).astype(BF16),
    )


def block_tables(sign, blocks, full):
    k1 = np.arange(D)[:, None]
    src = np.arange(D)[None, :]
    c, s = unit(k1 * src, D)
    gather = np.concatenate([c, sign * s], axis=0)
    j = np.tile(np.arange(R), 8)[None, :]
    tc, ts = unit(k1 * j, N)
    k2 = np.arange(R)[:, None]
    jj = np.arange(R)[None, :]
    cc, ss = unit(k2 * jj, R)
    ss = sign * ss
    rows = []
    for part in range(2 if full else 1):
        for e in range(blocks):
            out = np.zeros((R, 2, 4, R))
            out[:, 0, e, :] = cc if part == 0 else ss
            out[:, 1, e, :] = -ss if part == 0 else cc
            rows.append(out.reshape(R, L))
    finish = np.concatenate(rows, axis=0)
    return (
        jnp.asarray(gather, F32).astype(BF16),
        jnp.asarray(tc, F32),
        jnp.asarray(sign * ts, F32),
        jnp.asarray(finish, F32).astype(BF16),
    )


def fourth(x, sign):
    (ar, ai), (br, bi), (cr, ci), (dr, di) = x
    t0r, t0i, t1r, t1i = ar + cr, ai + ci, ar - cr, ai - ci
    t2r, t2i, t3r, t3i = br + dr, bi + di, br - dr, bi - di
    if sign < 0:
        t3r, t3i = -t3r, -t3i
    return (
        (t0r + t2r, t0i + t2i),
        (t1r - t3i, t1i + t3r),
        (t0r - t2r, t0i - t2i),
        (t1r + t3i, t1i - t3r),
    )


def times(x, re, im):
    if abs(im) < 1e-12 and abs(re - 1.0) < 1e-12:
        return x
    a, b = x
    return (a * re - b * im, a * im + b * re)


def sixteenth(x, sign):
    inner = []
    for b in range(4):
        y = fourth([x[4 * a + b] for a in range(4)], sign)
        turned = []
        for c in range(4):
            angle = sign * 2.0 * math.pi * b * c / 16
            turned.append(times(y[c], math.cos(angle), math.sin(angle)))
        inner.append(turned)
    out = [None] * 16
    for c in range(4):
        z = fourth([inner[b][c] for b in range(4)], sign)
        for d in range(4):
            out[c + 4 * d] = z[d]
    return out


def nt_dot(a, b):
    return lax.dot_general(a, b, (((1,), (1,)), ((), ())), preferred_element_type=F32)


def blocks_in(x, gather, tc, ts, flip):
    both = jnp.dot(gather, x, preferred_element_type=F32)
    parts = []
    for h in range(2):
        a = both[:D, h * L:(h + 1) * L]
        b = both[D:, h * L:(h + 1) * L]
        u = a * tc - b * ts
        v = b * tc + a * ts
        parts.append((u + flip * pltpu.roll(v, 64, 1)).astype(BF16))
    return jnp.concatenate(parts, axis=0)


def lane_iota(rows):
    return lax.broadcasted_iota(jnp.int32, (rows, L), 1)


def hops(step):
    return min(step, 4 - step)


def far(kw, kg):
    return hops(kw // 4) + hops(kw % 4) + hops(kg // 2) + 0.5 * (kg % 2)


WIDE_STEPS = sorted(range(1, NW), key=lambda k: -far(k, 0))
GRP_STEPS = sorted(range(1, NG), key=lambda k: -far(0, k))
ALL_STEPS = sorted(
    [(kw, kg) for kw in range(NW) for kg in range(NG) if kw or kg], key=lambda k: -far(*k)
)


def around():
    w = lax.axis_index("wide")
    g = lax.axis_index("grp")
    y = [lax.rem(w // 4 + k, 4) for k in range(4)]
    z = [lax.rem(w % 4 + k, 4) for k in range(4)]
    x = [lax.rem(g // 2 + k, 4) for k in range(4)]
    c = [g % 2, 1 - g % 2]
    ws = [y[k // 4] * 4 + z[k % 4] for k in range(NW)]
    gs = [x[k // 2] * 2 + c[k % 2] for k in range(NG)]
    return w, g, ws, gs


def greet_all(ws, gs):
    barrier = pltpu.get_barrier_semaphore()
    for kw, kg in ALL_STEPS:
        pl.semaphore_signal(
            barrier, inc=1, device_id=(ws[kw], gs[kg]), device_id_type=MESH
        )
    return barrier


def spread_all(send, recv, ssem, rsem, ws, gs):
    me = ws[0] * NG + gs[0]
    pltpu.make_async_copy(send.at[me], recv.at[me], rsem).start()
    for kw, kg in ALL_STEPS:
        pltpu.make_async_remote_copy(
            send.at[ws[kw] * NG + gs[kg]], recv.at[me], ssem, rsem,
            device_id=(ws[kw], gs[kg]), device_id_type=MESH,
        ).start()


def spread_grp(send, recv, ssem, rsem, ws, gs):
    pltpu.make_async_copy(send.at[gs[0]], recv.at[gs[0]], rsem).start()
    for k in GRP_STEPS:
        pltpu.make_async_remote_copy(
            send.at[gs[k]], recv.at[gs[0]], ssem, rsem,
            device_id=(ws[0], gs[k]), device_id_type=MESH,
        ).start()


def spread_wide(send, recv, ssem, rsem, ws, gs):
    pltpu.make_async_copy(send.at[ws[0]], recv.at[ws[0]], rsem).start()
    for k in WIDE_STEPS:
        pltpu.make_async_remote_copy(
            send.at[ws[k]], recv.at[ws[0]], ssem, rsem,
            device_id=(ws[k], gs[0]), device_id_type=MESH,
        ).start()


def landed_all(buf, sem):
    pltpu.make_async_copy(buf, buf, sem).wait()


def sent(buf, n, sem):
    pltpu.make_async_copy(buf.at[pl.ds(0, n)], buf.at[pl.ds(0, n)], sem).wait()


def patch_tables():
    pos = np.arange(SIDE)
    edge = np.minimum(pos, SIDE - 1 - pos)
    dist = np.minimum(edge[:, None], edge[None, :])
    weight = 0.3 + 0.7 * np.exp(-8.0 * dist / SIDE)
    x = np.arange(SIDE)
    pick = np.zeros((2, L, SIDE))
    for h in range(2):
        pick[h, 64 * h + x // 2, x] = 1.0
    rows = np.zeros((SIDE, TS))
    rows[x, x // 2] = 1.0
    halves = np.zeros((2, SIDE, 32))
    for i in range(SIDE):
        r = i // 2
        blk, within = r // 16, r % 16
        halves[blk % 2, i, (blk // 2) * 16 + within] = 1.0
    z = Z_BOTTOM + (np.arange(LV) + 0.5) * ((Z_TOP - Z_BOTTOM) / LV)
    prof = np.exp(DECAY_RATE * (z - Z_TOP))
    return (
        jnp.asarray(prof, F32),
        jnp.asarray(weight, F32),
        jnp.asarray(pick, F32).astype(BF16),
        jnp.asarray(rows, F32).astype(BF16),
        jnp.asarray(halves, F32).astype(BF16),
    )


RB = 16
PAD = 8
CHUNK = 16
TOGETHER = 8
LONG = 32
BAND = 32


def rank_of(tiles, q, want):
    at = jnp.int32(0)
    for step in (16, 8, 4, 2, 1):
        at = at + jnp.where(tiles[q * 32 + at + step - 1] < want, step, 0)
    return at


EARLY = 5


def step_kernel(tiles, prof, state, *refs):
    operands, refs = refs[:18], refs[18:]
    state_out, landed_out, sea_out = refs[:3]
    held, refs = refs[3:21], refs[21:]
    load_sem, done_sem = refs[-2:]
    step_body(
        tiles, prof, state, state_out, landed_out, sea_out, operands, held, load_sem, done_sem,
        *held, *refs[:-2]
    )


def step_body(
    tiles, prof, state, state_out, landed_out, sea_out, operands, held, load_sem, done_sem,
    eta, phi, up_c, up_s, up_spread,
    weight, pick, rows, halves, down_rows, down_cols,
    gather, bt_c, bt_s, finish, tw_c, tw_s, spread,
    landed, sea_held, source, tb_a, wide32, send_a, recv_a, phys,
    send1h, recv1h, send1v, recv1v, send2h, recv2h, send2v, recv2v,
    st, hh, cf, bl, cm, got, tb, send, recv,
    in_sem, out_sem, asem, arsem, ssem1h, rsem1h, ssem1v, rsem1v,
    ssem2h, rsem2h, ssem2v, rsem2v, csem, gsem, ssem, rsem,
):
    def fetch(s, i):
        part = pl.ds(i * CHUNK, CHUNK)
        return pltpu.make_async_copy(state.at[s, part], st.at[s, part], in_sem.at[s, i])

    def put(s, r):
        part = pl.ds(r * BAND, BAND)
        return pltpu.make_async_copy(
            st.at[s, :, part], state_out.at[s, :, part], out_sem.at[s, r]
        )

    def load(n):
        return pltpu.make_async_copy(operands[n], held[n], load_sem.at[n])

    for n in range(EARLY):
        load(n).start()
    w, g, ws, gs = around()
    me = w * NG + g
    barrier = greet_all(ws, gs)
    for n in range(EARLY, len(operands)):
        load(n).start()
    for s in range(2):
        for i in range(LV // CHUNK):
            fetch(s, i).start()
    for n in range(EARLY):
        load(n).wait()

    row = lax.broadcasted_iota(jnp.int32, (R, L), 0)
    lane = lane_iota(R)
    kx = me * R + row
    kx = jnp.where(kx >= N // 2, kx - N, kx).astype(F32) * (2.0 * math.pi / N)

    for f in range(3):
        x = []
        for n1 in range(16):
            cols = slice(n1 * L, (n1 + 1) * L)
            if f == 0:
                x.append((eta[0, :, cols].astype(F32), eta[1, :, cols].astype(F32)))
            else:
                if f == 1:
                    k = kx
                else:
                    base = n1 * L if n1 < 8 else n1 * L - N
                    k = (lane + base).astype(F32) * (2.0 * math.pi / N)
                x.append((-k * phi[1, :, cols].astype(F32), k * phi[0, :, cols].astype(F32)))
        y = sixteenth(x, 1)
        for k1 in range(16):
            c, s = up_c[k1:k1 + 1, :], up_s[k1:k1 + 1, :]
            a, b = y[k1]
            re = (a * c - b * s).astype(BF16)
            im = (a * s + b * c).astype(BF16)
            up = slice(f * R, (f + 1) * R)
            dn = slice(64 + f * R, 64 + (f + 1) * R)
            tb_a[k1, up, 0:L] = re
            tb_a[k1, up, L:2 * L] = -im
            tb_a[k1, dn, 0:L] = im
            tb_a[k1, dn, L:2 * L] = re

    zero = jnp.zeros((R, 2 * L), BF16)

    def rows_out(kk, carry):
        for h in range(2):
            tb_a[2 * kk + h, 48:64, :] = zero
            tb_a[2 * kk + h, 112:128, :] = zero
        rhs = tb_a[pl.ds(2 * kk, 2)].reshape(2 * L, 2 * L)
        z = nt_dot(up_spread[...], rhs)
        wide32[pl.ds(2 * kk, D, stride=R), :] = z[:, :L]
        wide32[pl.ds(2 * kk + 1, D, stride=R), :] = z[:, L:]
        return carry

    lax.fori_loop(0, 8, rows_out, 0, unroll=2)

    def narrow(i, carry):
        part = wide32[pl.ds(pl.multiple_of(i * 128, 128), 128), :]
        send_a[pl.ds(i * 8, 8)] = part.reshape(8, R, L).astype(BF16)
        return carry

    lax.fori_loop(0, 16, narrow, 0)

    pl.semaphore_wait(barrier, D - 1)
    spread_all(send_a, recv_a, asem, arsem, ws, gs)

    for q in range(NG):
        want = (2 * w + g // 4) * 32 + 4 * q
        at = rank_of(tiles, q, want)
        for c in range(4):
            found = tiles[q * 32 + at]
            source[0, 4 * q + c] = jnp.bitwise_and(at, NW - 1) * NG + q
            source[1, 4 * q + c] = lax.shift_right_logical(at, 4)
            source[2, 4 * q + c] = jnp.where(found == want + c, 1, 0)
            at = jnp.minimum(at + jnp.where(found <= want + c, 1, 0), 31)

    for n in range(EARLY, len(operands)):
        load(n).wait()
    edge = jnp.zeros((LV, PAD, SIDE), F32)
    for s in range(2):
        bl[s, :, 0:PAD, :] = edge
        bl[s, :, PAD + SIDE:, :] = edge
        for i in range(LV // CHUNK):
            fetch(s, i).wait()

        def share(o, carry, s=s):
            for b in range(SIDE // RB):
                rs = slice(b * RB, (b + 1) * RB)
                keep = 1.0 - weight[rs, :]
                for l in range(TOGETHER):
                    k = o * TOGETHER + l
                    bl[s, k, PAD + b * RB:PAD + (b + 1) * RB, :] = (
                        keep * st[s, k, rs, :].astype(F32)
                    )
            return carry

        lax.fori_loop(0, LV // TOGETHER, share, 0)

    landed_all(recv_a, arsem)

    def widen(i, carry):
        part = recv_a[pl.ds(i * 8, 8)].astype(F32)
        wide32[pl.ds(pl.multiple_of(i * 128, 128), 128), :] = part.reshape(128, L)
        return carry

    lax.fori_loop(0, 16, widen, 0)

    flip = jnp.where(lane_iota(D) < 64, -1.0, 1.0).astype(F32)

    def columns(yy, carry):
        x = jnp.concatenate(
            [
                wide32[pl.ds(2 * yy, D, stride=R), :].astype(BF16),
                wide32[pl.ds(2 * yy + 1, D, stride=R), :].astype(BF16),
            ],
            axis=1,
        )
        t = blocks_in(x, gather[...], bt_c[...], bt_s[...], flip)
        out = nt_dot(finish[...], t)
        phys[pl.ds(2 * yy, 48, stride=R), :] = out[:, :L]
        phys[pl.ds(2 * yy + 1, 48, stride=R), :] = out[:, L:]
        return carry

    lax.fori_loop(0, 8, columns, 0, unroll=4)

    low = lane < 64

    def heights(q, carry):
        for h in range(2):
            at = pl.multiple_of((2 * q + h) * R, R)
            send1h[q, h] = phys[pl.ds(at, R), :].astype(BF16)
        return carry

    lax.fori_loop(0, NG, heights, 0, unroll=4)
    spread_grp(send1h, recv1h, ssem1h, rsem1h, ws, gs)

    def speeds(q, carry):
        for h in range(2):
            vx = phys[pl.ds(pl.multiple_of((16 + 2 * q + h) * R, R), R), :]
            vy = phys[pl.ds(pl.multiple_of((32 + 2 * q + h) * R, R), R), :]
            send1v[q, 2 * h] = jnp.where(low, vx, pltpu.roll(vy, 64, 1)).astype(BF16)
            send1v[q, 2 * h + 1] = jnp.where(low, pltpu.roll(vx, 64, 1), vy).astype(BF16)
        return carry

    lax.fori_loop(0, NG, speeds, 0, unroll=2)
    spread_grp(send1v, recv1v, ssem1v, rsem1v, ws, gs)

    def tile_for(d):
        t0 = tiles[g * 32 + d]
        t1 = tiles[g * 32 + 16 + d]
        t = jnp.where(lax.shift_right_logical(t0, 6) == w, t0, t1)
        return jnp.bitwise_and(lax.shift_right_logical(t, 5), 1) * 4, jnp.bitwise_and(t, 3)

    landed_all(recv1h, rsem1h)

    def choose_heights(d, carry):
        upper, col = tile_for(d)
        right = (lane * 0 + jnp.bitwise_and(col, 1)) == 1
        pair = lax.shift_right_logical(col, 1)
        for q in range(2):
            a = recv1h[upper + 2 * q, pair].astype(F32)
            b = recv1h[upper + 2 * q + 1, pair].astype(F32)
            lo = jnp.where(right, pltpu.roll(a, 64, 1), a)
            hi = jnp.where(right, b, pltpu.roll(b, 64, 1))
            send2h[d, q] = jnp.where(low, lo, hi).astype(BF16)
        return carry

    lax.fori_loop(0, NW, choose_heights, 0, unroll=8)
    spread_wide(send2h, recv2h, ssem2h, rsem2h, ws, gs)

    landed_all(recv1v, rsem1v)

    def choose_speeds(d, carry):
        upper, col = tile_for(d)
        for q in range(4):
            send2v[d, q] = recv1v[upper + q, col]
        return carry

    lax.fori_loop(0, NW, choose_speeds, 0, unroll=16)
    spread_wide(send2v, recv2v, ssem2v, rsem2v, ws, gs)

    bands = [
        jnp.bitwise_and(lax.shift_right_logical(tiles[g * 32 + s * 16 + w], 6), NW - 1)
        for s in range(2)
    ]
    scale = LV / (Z_TOP - Z_BOTTOM)

    def up(m, sel, spread_rows):
        wide = jnp.dot(m, sel, preferred_element_type=F32).astype(BF16)
        return jnp.dot(spread_rows, wide, preferred_element_type=F32)

    landed_all(recv2h, rsem2h)
    for s in range(2):
        hgt = recv2h[bands[s]].reshape(32, L)
        height = up(hgt, pick[0], halves[0]) + up(hgt, pick[1], halves[1])
        hh[s] = height * scale - Z_BOTTOM * scale

        def blend(o, carry, s=s):
            for b in range(SIDE // RB):
                rs = slice(b * RB, (b + 1) * RB)
                h, wt = hh[s, rs, :], weight[rs, :]
                for l in range(TOGETHER):
                    k = o * TOGETHER + l
                    under = jnp.clip(h - lax.convert_element_type(k, F32), 0.0, 1.0)
                    bl[s, k, PAD + b * RB:PAD + (b + 1) * RB, :] += wt * under
            return carry

        lax.fori_loop(0, LV // TOGETHER, blend, 0)

    across = lax.broadcasted_iota(jnp.int32, (SIDE, SIDE), 1)
    sub = lax.broadcasted_iota(jnp.int32, (SIDE, SIDE), 0)

    def faces(a, axis, index):
        after = jnp.where(index == SIDE - 1, a, pltpu.roll(a, SIDE - 1, axis))
        before = jnp.where(index == 0, a, pltpu.roll(a, 1, axis))
        return (0.5 * COURANT) * (a + after), (0.5 * COURANT) * (before + a)

    landed_all(recv2v, rsem2v)
    for s in range(2):
        vel = recv2v[bands[s]].reshape(64, L)
        ax = up(vel, pick[0], rows[...])
        ay = up(vel, pick[1], rows[...])
        center = jnp.zeros((SIDE, SIDE), F32)
        for n, (a, axis, index) in enumerate(((ax, 1, across), (ay, 0, sub))):
            upper, lower = faces(a, axis, index)
            center += jnp.maximum(upper, 0.0) - jnp.minimum(lower, 0.0)
            from_up = jnp.minimum(upper, 0.0)
            from_low = -jnp.maximum(lower, 0.0)
            last, first = index == SIDE - 1, index == 0
            center += jnp.where(last, from_up, 0.0) + jnp.where(first, from_low, 0.0)
            cf[s, 1 + 2 * n] = jnp.where(last, 0.0, from_up)
            cf[s, 2 + 2 * n] = jnp.where(first, 0.0, from_low)
        cf[s, 0] = center

    high = lax.Precision.HIGHEST
    for r in range(SIDE // BAND):

        def move(o, accs, r=r):
            accs = list(accs)
            for s in range(2):
                for n in range(BAND // RB):
                    first_row = r * BAND + n * RB
                    rs = slice(first_row, first_row + RB)
                    at = PAD + first_row
                    c0, c1, c2, c3, c4 = (cf[s, m, rs, :] for m in range(5))
                    acc = accs[2 * s + n]
                    for l in range(LONG):
                        k = o * LONG + l
                        mid = bl[s, k, at:at + RB, :]
                        nxt = bl[s, k, at + 1:at + 1 + RB, :]
                        prv = bl[s, k, at - 1:at - 1 + RB, :]
                        flow = c0 * mid + c1 * pltpu.roll(mid, SIDE - 1, 1)
                        flow = flow + c2 * pltpu.roll(mid, 1, 1) + c3 * nxt + c4 * prv
                        new = jnp.clip(mid - prof[k] * flow, 0.0, 1.0)
                        st[s, k, rs, :] = new.astype(BF16)
                        acc = acc + new
                    accs[2 * s + n] = acc
            return tuple(accs)

        none = jnp.zeros((RB, SIDE), F32)
        accs = lax.fori_loop(0, LV // LONG, move, (none,) * 4)
        slots = [
            jnp.concatenate(accs[2 * s:2 * s + 2], axis=0) * (1.0 / scale) + Z_BOTTOM
            for s in range(2)
        ]
        part = jnp.dot(
            down_rows[...], jnp.concatenate(slots, axis=1),
            preferred_element_type=F32, precision=high,
        )
        block = jnp.dot(
            part, down_cols[...].reshape(2 * SIDE, L), preferred_element_type=F32, precision=high
        )
        cm[r] = (0.25 * block).astype(BF16)
        for s in range(2):
            put(s, r).start()

        for to in (r, r + 4):
            for kw in WIDE_STEPS + [0]:

                def post(to=to, kw=kw, r=r):
                    pltpu.make_async_remote_copy(
                        cm.at[r], got.at[me], csem, gsem,
                        device_id=(ws[kw], to), device_id_type=MESH,
                    ).start()

                if kw:
                    post()
                else:
                    pl.when(g != to)(post)

                    @pl.when(g == to)
                    def _(r=r):
                        pltpu.make_async_copy(cm.at[r], got.at[me], gsem).start()

    landed_all(got, gsem)

    x = []
    for k2 in range(16):
        sides = []
        for h in range(2):
            cc = 2 * k2 + h
            tile = got[source[0, cc]].astype(F32)
            same = (lane * 0 + source[1, cc]) == h
            sides.append(jnp.where(same, tile, pltpu.roll(tile, 64, 1)))
        there = jnp.where(low, source[2, 2 * k2], source[2, 2 * k2 + 1]) == 1
        ht = phys[k2 * R:(k2 + 1) * R, :]
        vx = phys[256 + k2 * R:256 + (k2 + 1) * R, :]
        vy = phys[512 + k2 * R:512 + (k2 + 1) * R, :]
        sea = jnp.where(there, jnp.where(low, sides[0], sides[1]), ht)
        sea_held[:, k2 * L:(k2 + 1) * L] = sea
        x.append((-(sea + 0.5 * (vx * vx + vy * vy)), jnp.zeros((R, L), F32)))
    y = sixteenth(x, -1)
    for k1 in range(16):
        c, s = tw_c[k1:k1 + 1, :], tw_s[k1:k1 + 1, :]
        a, b = y[k1]
        re = (a * c - b * s).astype(BF16)
        im = (a * s + b * c).astype(BF16)
        q, e = k1 // 4, k1 % 4
        up_rows = slice(e * R, (e + 1) * R)
        dn_rows = slice(64 + e * R, 64 + (e + 1) * R)
        tb[q, up_rows, 0:L] = re
        tb[q, up_rows, L:2 * L] = -im
        tb[q, dn_rows, 0:L] = im
        tb[q, dn_rows, L:2 * L] = re

    for q in range(2):
        rhs = tb[2 * q:2 * q + 2].reshape(2 * L, 2 * L)
        z = nt_dot(spread[...], rhs)
        send[:, 2 * q, :] = z[:, :L]
        send[:, 2 * q + 1, :] = z[:, L:]

    spread_all(send, recv, ssem, rsem, ws, gs)
    sea_done = pltpu.make_async_copy(sea_held, sea_out, done_sem.at[0])
    sea_done.start()
    landed_all(recv, rsem)
    for q in range(4):
        landed[q] = recv[:, q, :].astype(BF16)
    all_done = pltpu.make_async_copy(landed, landed_out, done_sem.at[1])
    all_done.start()

    sent(send_a, D - 1, asem)
    sent(send1h, NG - 1, ssem1h)
    sent(send1v, NG - 1, ssem1v)
    sent(send2h, NW - 1, ssem2h)
    sent(send2v, NW - 1, ssem2v)
    sent(got, D - 1, csem)
    sent(send, D - 1, ssem)
    for s in range(2):
        for r in range(SIDE // BAND):
            put(s, r).wait()
    sea_done.wait()
    all_done.wait()


def settle_kernel(*refs):
    operands, (state,) = refs[:6], refs[6:7]
    surface, state_out, tendency = refs[7:10]
    held = refs[10:16]
    landed, gather, bt_c, bt_s, finish, sea = held
    out32, spectrum, kept, load_sem, done_sem, in_sem, out_sem = refs[16:]

    def copy(i, source, target, sem):
        s, part = i // 4, pl.ds((i % 4) * CHUNK, CHUNK)
        return pltpu.make_async_copy(source.at[s, part], target.at[s, part], sem.at[i])

    loads = [
        pltpu.make_async_copy(operands[n], held[n], load_sem.at[n]) for n in range(6)
    ]
    for n in range(6):
        loads[n].start()
    for i in range(8):
        copy(i, state, kept, in_sem).start()
    for n in range(6):
        loads[n].wait()
    sea_done = pltpu.make_async_copy(sea, surface, done_sem.at[0])
    sea_done.start()

    def hand_on(i):
        copy(i, state, kept, in_sem).wait()
        copy(i, kept, state_out, out_sem).start()

    for i in range(4):
        hand_on(i)

    flip = jnp.where(lane_iota(D) < 64, -1.0, 1.0).astype(F32)
    turned = [
        blocks_in(
            jnp.concatenate([landed[2 * q], landed[2 * q + 1]], axis=1),
            gather[...], bt_c[...], bt_s[...], flip,
        )
        for q in range(2)
    ]
    done = nt_dot(finish[...], jnp.concatenate(turned, axis=0)) * (1.0 / N)
    for h in range(4):
        for c in range(2):
            for e in range(4):
                r0 = (c * 4 + e) * R
                out32[pl.ds(c * 256 + 4 * h + e, R, stride=R), :] = done[
                    r0:r0 + R, h * L:(h + 1) * L
                ]
    for i in range(4, 8):
        hand_on(i)
    for c in range(2):
        for k2 in range(16):
            at = c * 256 + k2 * R
            spectrum[c, :, k2 * L:(k2 + 1) * L] = out32[at:at + R, :]
    all_done = pltpu.make_async_copy(spectrum, tendency, done_sem.at[1])
    all_done.start()

    for i in range(8):
        copy(i, kept, state_out, out_sem).wait()
    sea_done.wait()
    all_done.wait()


def shards(eta_hat, phi_hat, patch_tiles, fraction):
    smem = pl.BlockSpec(memory_space=pltpu.SMEM)
    dma = pltpu.SemaphoreType.DMA
    prof, weight, pick, rows, halves = patch_tables()
    down_rows = jnp.swapaxes(rows[:BAND, :R], 0, 1).astype(F32)
    down_cols = jnp.swapaxes(pick, 1, 2).astype(F32)
    anywhere = pl.BlockSpec(memory_space=pl.ANY)
    operands = (
        eta_hat, phi_hat, *lane_tables(1), weight, pick, rows, halves,
        down_rows, down_cols, *block_tables(1, 3, False), *lane_tables(-1),
    )
    new_state, landed, sea = pl.pallas_call(
        step_kernel,
        out_shape=(
            jax.ShapeDtypeStruct((2, LV, SIDE, SIDE), BF16),
            jax.ShapeDtypeStruct((4, D, L), BF16),
            jax.ShapeDtypeStruct((R, N), F32),
        ),
        in_specs=[smem, smem] + [anywhere] * (1 + len(operands)),
        out_specs=(anywhere,) * 3,
        scratch_shapes=[pltpu.VMEM(x.shape, x.dtype) for x in operands] + [
            pltpu.VMEM((4, D, L), BF16),
            pltpu.VMEM((R, N), F32),
            pltpu.SMEM((3, 32), jnp.int32),
            pltpu.VMEM((16, L, 2 * L), BF16),
            pltpu.VMEM((D * R, L), F32),
            pltpu.VMEM((D, R, L), BF16),
            pltpu.VMEM((D, R, L), BF16),
            pltpu.VMEM((48 * R, L), F32),
            pltpu.VMEM((NG, 2, R, L), BF16),
            pltpu.VMEM((NG, 2, R, L), BF16),
            pltpu.VMEM((NG, 4, R, L), BF16),
            pltpu.VMEM((NG, 4, R, L), BF16),
            pltpu.VMEM((NW, 2, R, L), BF16),
            pltpu.VMEM((NW, 2, R, L), BF16),
            pltpu.VMEM((NW, 4, R, L), BF16),
            pltpu.VMEM((NW, 4, R, L), BF16),
            pltpu.VMEM((2, LV, SIDE, SIDE), BF16),
            pltpu.VMEM((2, SIDE, SIDE), F32),
            pltpu.VMEM((2, 5, SIDE, SIDE), F32),
            pltpu.VMEM((2, LV, SIDE + 2 * PAD, SIDE), F32),
            pltpu.VMEM((4, R, L), BF16),
            pltpu.VMEM((D, R, L), BF16),
            pltpu.VMEM((4, L, 2 * L), BF16),
            pltpu.VMEM((D, 4, L), F32),
            pltpu.VMEM((D, 4, L), F32),
            dma((2, LV // CHUNK)),
            dma((2, SIDE // BAND)),
        ] + [dma] * 14 + [dma((len(operands),)), dma((2,))],
        compiler_params=pltpu.CompilerParams(
            collective_id=1, has_side_effects=True, vmem_limit_bytes=VMEM_LIMIT
        ),
        name="step",
    )(patch_tiles, prof, fraction[:, 0], *operands)

    last = (landed, *block_tables(-1, 4, True), sea)
    surface, new_state, tendency = pl.pallas_call(
        settle_kernel,
        out_shape=(
            jax.ShapeDtypeStruct((R, N), F32),
            jax.ShapeDtypeStruct((2, LV, SIDE, SIDE), BF16),
            jax.ShapeDtypeStruct((2, R, N), F32),
        ),
        in_specs=[anywhere] * 7,
        out_specs=(anywhere,) * 3,
        scratch_shapes=[pltpu.VMEM(x.shape, x.dtype) for x in last] + [
            pltpu.VMEM((512, L), F32),
            pltpu.VMEM((2, R, N), F32),
            pltpu.VMEM((2, LV, SIDE, SIDE), BF16),
            dma((6,)),
            dma((2,)),
            dma((8,)),
            dma((8,)),
        ],
        compiler_params=pltpu.CompilerParams(vmem_limit_bytes=VMEM_LIMIT),
        name="settle",
    )(*last, new_state)
    return (surface, new_state[:, None], tendency)


def solution(mesh):
    placed = (
        P(None, ("wide", "grp"), None),
        P(None, ("wide", "grp"), None),
        P(),
        P(None, ("wide", "grp"), None, None, None),
    )
    return jax.shard_map(
        shards,
        mesh=mesh,
        in_specs=placed,
        out_specs=(
            P(("wide", "grp"), None),
            P(None, ("wide", "grp"), None, None, None),
            P(None, ("wide", "grp"), None),
        ),
        check_vma=False,
    )
```
